128 devices in a mesh: tile: 32 (over x, y_hi, z), mode: 4 (over y_lo, core).
Axes of the slice: x: 4, y: 4 (y_hi: 2, y_lo: 2; y = y_hi * 2 + y_lo), z: 4, core: 2. Of those that a mesh axis runs over, the one named last changes fastest.
Arguments:
- object_real: float32 [32, 2, 384, 384], P('tile', None, 'mode'), may hold values from 0.6 to 1.2
- object_imag: float32 [32, 2, 384, 384], P('tile', None, 'mode'), may hold values from -0.4 to 0.4
- probe: float32 [2, 8, 256, 256], P(None, 'mode'), may hold values from -1.5 to 1.5
- measured: float32 [32, 2, 256, 256], P('tile'), may hold values from 0.2 to 1.6
- positions: int32 [32, 2, 2], P('tile'), may hold values from 0 to 128
Outputs:
- object_grad_real: float32 [32, 2, 384, 384], P('tile', None, 'mode')
- object_grad_imag: float32 [32, 2, 384, 384], P('tile', None, 'mode')
- probe_grad: float32 [2, 8, 256, 256], P(None, 'mode')
The draws below stay inside these ranges and needn't reach their ends.
All inputs are finite; a program needn't handle non-finite values.
Results may differ from the reference program's by a relative error of at most 0.0003.
Values sent between devices are 32-bit elements; how exact they have to be, the bound alone decides.
A program may use at most 128 MiB of HBM per device.

```python
import math
import jax
import jax.numpy as jnp
from jax import lax

PX = 256
TILE_PX = 384
MARGIN = 64
MODES = 8
SLICES = 2
FRAMES = 2
TILES = 32


def place_ends(drawn, key, low, high):
    longest = drawn.shape.index(max(drawn.shape))
    spots = []
    for shift in (0, 1):
        where = [jax.random.randint(jax.random.fold_in(key, axis), (), 0, length) for axis, length in enumerate(drawn.shape)]
        where[longest] = (where[longest] + shift) % drawn.shape[longest]
        spots.append(tuple(where))
    return drawn.at[spots[0]].set(low).at[spots[1]].set(high)


def steps_of(key, dims, split, low, high):
    def one(axis_at, blocks):
        draws = jax.random.uniform(jax.random.fold_in(jax.random.fold_in(key, 6), axis_at), (blocks,), jnp.float32, low / len(split), high / len(split))
        return jnp.repeat(jnp.exp(draws), dims[axis_at] // blocks).reshape((-1,) + (1,) * (len(dims) - axis_at - 1))

    level = one(*split[0])
    for cut in split[1:]:
        level = level * one(*cut)
    return level


def gaussian(key, dims, scale, most, cuts=(), held_as=jnp.bfloat16):
    result = jax.random.normal(key, dims, jnp.float32) * scale
    if len(cuts) > 0:
        result = steps_of(key, dims, cuts, -0.22, 0.18) * result
    return jnp.clip(result, min=-most, max=most).astype(held_as)


def setup_inputs(seed: int = 0) -> dict:
    key_of = jax.random.split(jax.random.key(seed), 6)
    object_real = jnp.clip(0.6 + 0.6 * jax.random.uniform(key_of[0], (TILES, SLICES, TILE_PX, TILE_PX), jnp.float32) ** steps_of(key_of[0], (TILES, SLICES, TILE_PX, TILE_PX), ((0, 32), (2, 4)), -0.2, 0.2), 0.6, 1.2)
    object_imag = jnp.clip(jax.random.uniform(key_of[1], (TILES, SLICES, TILE_PX, TILE_PX), jnp.float32, -0.4, 0.4) * steps_of(key_of[1], (TILES, SLICES, TILE_PX, TILE_PX), ((0, 32), (2, 4)), -0.4, 0.0), -0.4, 0.4)
    probe = gaussian(key_of[2], (2, MODES, PX, PX), 0.25, 1.5, ((1, 4),), jnp.float32)
    measured = jnp.clip(0.2 + 1.4 * jax.random.uniform(key_of[3], (TILES, FRAMES, PX, PX), jnp.float32) ** steps_of(key_of[3], (TILES, FRAMES, PX, PX), ((0, 32),), -0.2, 0.2), 0.2, 1.6)
    positions = place_ends(jax.random.randint(key_of[4], (TILES, FRAMES, 2), 0, TILE_PX - PX + 1), jax.random.fold_in(key_of[4], 1), 0, TILE_PX - PX).astype(jnp.int32)
    return {"object_real": object_real, "object_imag": object_imag, "probe": probe, "measured": measured, "positions": positions}


amplitude_floor = 0.1
fresnel_number = 40.0

def tables(width):
    index = jnp.arange(width, dtype=jnp.int32)
    product = index[:, None] * index[None, :] % width
    angle = product.astype(jnp.float32) * (-2.0 * math.pi / width)
    scaling = 1.0 / math.sqrt(width)
    freq = ((index + width // 2) % width - width // 2).astype(jnp.float32) / width
    phase = -math.pi * fresnel_number * (freq[:, None] ** 2 + freq[None, :] ** 2)
    return (jnp.cos(angle) * scaling, jnp.sin(angle) * scaling, jnp.cos(phase), jnp.sin(phase))

def transform(real_part, imag_part, cos_table, sin_table):
    highest = lax.Precision.HIGHEST
    left_re = jnp.einsum('jk,mkl->mjl', cos_table, real_part, precision=highest) - jnp.einsum('jk,mkl->mjl', sin_table, imag_part, precision=highest)
    left_im = jnp.einsum('jk,mkl->mjl', cos_table, imag_part, precision=highest) + jnp.einsum('jk,mkl->mjl', sin_table, real_part, precision=highest)
    out_re = jnp.einsum('mjk,kl->mjl', left_re, cos_table, precision=highest) - jnp.einsum('mjk,kl->mjl', left_im, sin_table, precision=highest)
    out_im = jnp.einsum('mjk,kl->mjl', left_re, sin_table, precision=highest) + jnp.einsum('mjk,kl->mjl', left_im, cos_table, precision=highest)
    return (out_re, out_im)

def forward(crop_re, crop_im, probe_re, probe_im, cos_table, sin_table, kernel_re, kernel_im):
    wave_re, wave_im = (probe_re, probe_im)
    slices = crop_re.shape[0]
    for layer in range(slices):
        trans_re, trans_im = (crop_re[layer], crop_im[layer])
        wave_re, wave_im = (wave_re * trans_re - wave_im * trans_im, wave_re * trans_im + wave_im * trans_re)
        if layer + 1 < slices:
            spec_re, spec_im = transform(wave_re, wave_im, cos_table, sin_table)
            spec_re, spec_im = (spec_re * kernel_re - spec_im * kernel_im, spec_re * kernel_im + spec_im * kernel_re)
            wave_re, wave_im = transform(spec_re, spec_im, cos_table, -sin_table)
    return transform(wave_re, wave_im, cos_table, sin_table)

def tile_loss(tile_re, tile_im, probe, offsets, amplitudes):
    cos_table, sin_table, kernel_re, kernel_im = tables(PX)
    total = jnp.zeros((), jnp.float32)
    zero_index = jnp.zeros((), jnp.int32)
    for frame in range(FRAMES):
        start = (zero_index, offsets[frame, 0].astype(jnp.int32), offsets[frame, 1].astype(jnp.int32))
        crop_re = lax.dynamic_slice(tile_re, start, (SLICES, PX, PX))
        crop_im = lax.dynamic_slice(tile_im, start, (SLICES, PX, PX))
        far_re, far_im = forward(crop_re, crop_im, probe[0], probe[1], cos_table, sin_table, kernel_re, kernel_im)
        intensity = lax.optimization_barrier(jnp.sum(far_re * far_re + far_im * far_im, axis=0))
        amplitude = jnp.sqrt(intensity + amplitude_floor)
        total = total + jnp.sum((amplitude - amplitudes[frame]) ** 2)
    return total

def combine(grads):
    left_part = jnp.concatenate([jnp.zeros_like(grads[:1, ..., -MARGIN:]), grads[:-1, ..., -MARGIN:]], axis=0)
    right_part = jnp.concatenate([grads[1:, ..., :MARGIN], jnp.zeros_like(grads[:1, ..., :MARGIN])], axis=0)
    return grads.at[..., :MARGIN].add(left_part).at[..., -MARGIN:].add(right_part)

def reference(object_real, object_imag, probe, measured, positions):
    grad_fn = jax.grad(tile_loss, argnums=(0, 1, 2))

    def visit(carried, items):
        tile_re, tile_im, offsets, amplitudes = items
        grad_re, grad_im, grad_probe = grad_fn(tile_re, tile_im, probe, offsets, amplitudes)
        return (carried + grad_probe, (grad_re, grad_im))
    probe_grad, (grad_real, grad_imag) = lax.scan(visit, jnp.zeros_like(probe), (object_real, object_imag, positions, measured))
    return (combine(grad_real), combine(grad_imag), probe_grad)
```

```python
import functools
import math

import jax
import jax.numpy as jnp
import ml_dtypes
import numpy as np
from jax import lax
from jax.experimental import pallas as pl
from jax.experimental.pallas import tpu as pltpu
from jax.sharding import PartitionSpec as P

PX = 256
HALF = PX // 2
TILE = 384
MARGIN = 64
ROWS = 96
EDGE = TILE - PX
FLOOR = 0.1
FRESNEL = 40.0
MESH = pl.DeviceIdType.MESH
F32 = jnp.float32
BF16 = jnp.bfloat16

A_LEFT, A_RIGHT, F_LEFT, F_RIGHT, B_LEFT, B_RIGHT = range(6)


def real_form(c):
    return np.block([[c.real, -c.imag], [c.imag, c.real]])


@functools.cache
def constants():
    index = np.arange(PX)
    fourier = np.exp(-2j * np.pi * (np.outer(index, index) % PX) / PX) / math.sqrt(PX)
    freq = ((index + HALF) % PX - HALF) / PX
    chirp = np.exp(-1j * np.pi * FRESNEL * freq**2)
    through = fourier.conj() @ (chirp[:, None] * fourier)
    near, far = through[:HALF, :HALF], through[:HALF, HALF:]
    pairs = [None] * 6
    moved = [(near + far) / 2, (near - far) / 2]
    split = [fourier[0::2, :HALF], fourier[1::2, :HALF]]
    pairs[A_LEFT] = [real_form(c) for c in moved]
    pairs[A_RIGHT] = [real_form(c).T for c in moved]
    pairs[F_LEFT] = [real_form(c) for c in split]
    pairs[F_RIGHT] = [real_form(c).T for c in split]
    pairs[B_LEFT] = [real_form(c.T) for c in split]
    pairs[B_RIGHT] = [real_form(c.T).T for c in split]
    table = np.array(pairs).reshape(12, PX, PX)
    high = table.astype(ml_dtypes.bfloat16)
    low = (table - high.astype(np.float64)).astype(ml_dtypes.bfloat16)
    order = np.zeros((PX, PX))
    order[np.arange(HALF), np.arange(0, PX, 2)] = 1
    order[np.arange(HALF) + HALF, np.arange(1, PX, 2)] = 1
    orders = np.array([order, order.T]).astype(ml_dtypes.bfloat16)
    return np.stack([high, low], axis=1), orders


def two_parts(x):
    high = x.astype(BF16)
    return high, (x - high.astype(F32)).astype(BF16)


def product(a, b):
    return jnp.dot(a, b, preferred_element_type=F32)


def apply_left(table, kind, sign, z):
    high, low = two_parts(z)
    c_high, c_low = table[2 * kind + sign, 0], table[2 * kind + sign, 1]
    return product(
        jnp.concatenate([c_high, c_low, c_high], axis=1),
        jnp.concatenate([high, high, low], axis=0),
    )


def apply_right(table, kind, sign, z):
    high, low = two_parts(z)
    c_high, c_low = table[2 * kind + sign, 0], table[2 * kind + sign, 1]
    return product(
        jnp.concatenate([high, high, low], axis=1),
        jnp.concatenate([c_high, c_low, c_high], axis=0),
    )


def rows_first(x):
    return x[:HALF], x[HALF:]


def lanes_first(x):
    return x[:, :HALF], x[:, HALF:]


def one_side(table, kind, re, im, left):
    halves, axis, apply = (rows_first, 0, apply_left) if left else (lanes_first, 1, apply_right)
    (r0, r1), (i0, i1) = halves(re), halves(im)
    if kind[0] != B_LEFT:
        r0, r1, i0, i1 = r0 + r1, r0 - r1, i0 + i1, i0 - i1
    which = kind[0] if left else kind[1]
    plus = apply(table, which, 0, jnp.concatenate([r0, i0], axis=axis))
    minus = apply(table, which, 1, jnp.concatenate([r1, i1], axis=axis))
    (pr, pi), (mr, mi) = halves(plus), halves(minus)
    if kind[0] != F_LEFT:
        pr, mr, pi, mi = pr + mr, pr - mr, pi + mi, pi - mi
    return jnp.concatenate([pr, mr], axis=axis), jnp.concatenate([pi, mi], axis=axis)


def both_sides(table, kind, re, im):
    re, im = one_side(table, kind, re, im, True)
    return one_side(table, kind, re, im, False)


THROUGH = (A_LEFT, A_RIGHT)
FORTH = (F_LEFT, F_RIGHT)
BACK = (B_LEFT, B_RIGHT)


def times(ar, ai, br, bi):
    return ar * br - ai * bi, ar * bi + ai * br


def kernel(
    tiles,
    obj_re,
    obj_im,
    probe_in,
    measured_in,
    positions,
    table_in,
    orders_in,
    out_re,
    out_im,
    out_probe,
    tile0,
    tile1,
    crops,
    probe,
    measured,
    table,
    orders,
    wave1,
    far,
    ipart,
    isib,
    isum,
    icross,
    factor,
    crop_grad,
    rs_send,
    rs_got,
    rs_cross,
    rs_cross_got,
    own,
    edge_send,
    edge_got,
    local_sem,
    tile_local,
    g_send,
    g_recv,
    i_send,
    i_recv,
    r_send,
    r_recv,
    e_send,
    e_recv,
):
    t = lax.axis_index("tile")
    m = lax.axis_index("mode")
    core = lax.rem(m, 2)
    high = m // 2
    sibling = high * 2 + (1 - core)
    across = (1 - high) * 2 + core
    diagonal = (1 - high) * 2 + (1 - core)
    left = lax.rem(t + tiles - 1, tiles)
    right = lax.rem(t + 1, tiles)
    to_sibling, to_across = (t, sibling), (t, across)
    to_left, to_right = (left, m), (right, m)

    barrier = pltpu.get_barrier_semaphore()
    for device in (to_sibling, to_across, to_left, to_right):
        pl.semaphore_signal(barrier, inc=1, device_id=device, device_id_type=MESH)

    loads = [
        pltpu.make_async_copy(probe_in, probe, local_sem.at[0]),
        pltpu.make_async_copy(measured_in.at[0], measured, local_sem.at[1]),
        pltpu.make_async_copy(table_in, table, local_sem.at[2]),
        pltpu.make_async_copy(orders_in, orders, local_sem.at[3]),
    ]
    for load in loads:
        load.start()

    whole = (tile0, tile1)
    objects = (obj_re, obj_im)

    def my_rows(who):
        return pl.ds(pl.multiple_of(who * ROWS, ROWS), ROWS)

    def remote(src, dst, send, recv, device):
        return pltpu.make_async_remote_copy(
            src_ref=src, dst_ref=dst, send_sem=send, recv_sem=recv, device_id=device, device_id_type=MESH
        )

    own_copies, sends, crosses, relays = {}, {}, {}, {}
    for s in range(2):
        for p in range(2):
            src = objects[p].at[0, s]
            dst = whole[s].at[p, my_rows(m)]
            own_copies[s, p] = pltpu.make_async_copy(src, dst, tile_local.at[s, p])
            crosses[s, p] = remote(src, dst, g_send.at[0, s, p], g_recv.at[0, s, p], to_across)
            sends[s, p] = remote(src, dst, g_send.at[1, s, p], g_recv.at[1, s, p], to_sibling)
            got = whole[s].at[p, my_rows(across)]
            relays[s, p] = remote(got, got, g_send.at[2, s, p], g_recv.at[2, s, p], to_sibling)

    pl.semaphore_wait(barrier, 4)
    for s in range(2):
        for p in range(2):
            crosses[s, p].start()
    for s in range(2):
        for p in range(2):
            own_copies[s, p].start()
            sends[s, p].start()

    crop_grad[...] = jnp.zeros_like(crop_grad)
    out_probe[...] = jnp.zeros_like(out_probe)
    for load in loads:
        load.wait()
    for f in range(2):
        m_high, m_low = two_parts(measured[f])
        mixed = product(orders[0], m_high) + product(orders[0], m_low)
        m_high, m_low = two_parts(mixed)
        measured[f] = product(m_high, orders[1]) + product(m_low, orders[1])

    def tile_ready(s):
        for p in range(2):
            crosses[s, p].wait_recv()
            relays[s, p].start()
        for p in range(2):
            own_copies[s, p].wait()
            sends[s, p].wait_recv()
        for p in range(2):
            relays[s, p].wait_recv()

    row = [positions[0, f, 0] for f in range(2)]
    col = [positions[0, f, 1] for f in range(2)]

    def lines_at(lines, start, count):
        length = lines.shape[0]
        return pltpu.roll(lines, lax.rem(length - start, length), 0)[:count]

    def take_crops(s):
        for f in range(2):
            back = lax.rem(TILE - col[f], TILE)
            for p in range(2):
                lines = lines_at(whole[s][p], row[f], PX)
                crops[f, s, p] = pltpu.roll(lines, back, 1)[:, :PX]

    tile_ready(0)
    take_crops(0)

    def pass_through(step, carry):
        f, mode = step // 2, lax.rem(step, 2)
        re, im = times(probe[0, mode], probe[1, mode], crops[f, 0, 0], crops[f, 0, 1])
        re, im = both_sides(table, THROUGH, re, im)
        wave1[f, mode, 0] = re
        wave1[f, mode, 1] = im
        return carry

    lax.fori_loop(0, 4, pass_through, 0)
    tile_ready(1)
    take_crops(1)

    def far_fields(f):
        ipart[f] = jnp.zeros_like(ipart[f])

        def step(mode, carry):
            re, im = times(wave1[f, mode, 0], wave1[f, mode, 1], crops[f, 1, 0], crops[f, 1, 1])
            re, im = both_sides(table, FORTH, re, im)
            far[f, mode, 0] = re
            far[f, mode, 1] = im
            ipart[f] += re * re + im * im
            return carry

        lax.fori_loop(0, 2, step, 0)

    def half_rows(who):
        return pl.ds(pl.multiple_of(who * HALF, HALF), HALF)

    to_pair = [
        remote(ipart.at[f, half_rows(1 - core)], isib.at[f], i_send.at[0, f], i_recv.at[0, f], to_sibling) for f in range(2)
    ]
    to_other = [remote(isum.at[f], icross.at[f], i_send.at[1, f], i_recv.at[1, f], to_across) for f in range(2)]
    to_share = [
        remote(
            factor.at[f, half_rows(core)],
            factor.at[f, half_rows(core)],
            i_send.at[2, f],
            i_recv.at[2, f],
            to_sibling,
        )
        for f in range(2)
    ]

    def pair_sum(f):
        to_pair[f].wait_recv()
        isum[f] = ipart[f, half_rows(core), :] + isib[f]
        to_other[f].start()

    def factors(f):
        to_other[f].wait_recv()
        total = isum[f] + icross[f]
        factor[f, half_rows(core), :] = 2.0 - 2.0 * measured[f, half_rows(core), :] / jnp.sqrt(total + FLOOR)
        to_share[f].start()

    far_fields(0)
    to_pair[0].start()
    far_fields(1)
    to_pair[1].start()
    pair_sum(0)
    pair_sum(1)
    factors(0)

    def back_to_slice_1(f):
        def step(mode, carry):
            weight = factor[f]
            re, im = weight * far[f, mode, 0], -(weight * far[f, mode, 1])
            re, im = both_sides(table, BACK, re, im)
            gr, gi = times(wave1[f, mode, 0], wave1[f, mode, 1], re, im)
            crop_grad[f, 1, 0, EDGE : EDGE + PX, :PX] += gr
            crop_grad[f, 1, 1, EDGE : EDGE + PX, :PX] -= gi
            re, im = times(crops[f, 1, 0], crops[f, 1, 1], re, im)
            far[f, mode, 0] = re
            far[f, mode, 1] = im
            return carry

        lax.fori_loop(0, 2, step, 0)

    def back_to_probe(f):
        def step(mode, carry):
            re, im = both_sides(table, THROUGH, far[f, mode, 0], far[f, mode, 1])
            gr, gi = times(probe[0, mode], probe[1, mode], re, im)
            crop_grad[f, 0, 0, EDGE : EDGE + PX, :PX] += gr
            crop_grad[f, 0, 1, EDGE : EDGE + PX, :PX] -= gi
            gr, gi = times(crops[f, 0, 0], crops[f, 0, 1], re, im)
            out_probe[0, mode] += gr
            out_probe[1, mode] -= gi
            return carry

        lax.fori_loop(0, 2, step, 0)

    def piece(s, p, who):
        total = None
        for f in range(2):
            lines = lines_at(crop_grad[f, s, p], EDGE - row[f] + who * ROWS, ROWS)
            lines = pltpu.roll(lines, col[f], 1)
            total = lines if total is None else total + lines
        return total

    rs_pair, rs_over, rs_edge = {}, {}, {}
    for s in range(2):
        for k in range(2):
            rs_pair[s, k] = remote(rs_send.at[s, k], rs_got.at[s, k], r_send.at[k, s], r_recv.at[k, s], to_sibling)
        rs_over[s] = remote(rs_cross.at[s], rs_cross_got.at[s], r_send.at[2, s], r_recv.at[2, s], to_across)
        rs_edge[s, 0] = remote(edge_send.at[s, 0], edge_got.at[s, 0], e_send.at[0, s], e_recv.at[0, s], to_right)
        rs_edge[s, 1] = remote(edge_send.at[s, 1], edge_got.at[s, 1], e_send.at[1, s], e_recv.at[1, s], to_left)

    def reduce_start(s):
        for k, who in enumerate((diagonal, sibling)):
            for p in range(2):
                rs_send[s, k, p] = piece(s, p, who)
            rs_pair[s, k].start()
        for p in range(2):
            rs_cross[s, p] = piece(s, p, across)
        rs_pair[s, 0].wait_recv()
        for p in range(2):
            rs_cross[s, p] += rs_got[s, 0, p]
        rs_over[s].start()
        for p in range(2):
            own[s, p] = piece(s, p, m)
        rs_pair[s, 1].wait_recv()
        for p in range(2):
            own[s, p] += rs_got[s, 1, p]

    lane = lax.broadcasted_iota(jnp.int32, (ROWS, 128), 1)
    lower = lane < MARGIN

    def reduce_middle(s):
        rs_over[s].wait_recv()
        for p in range(2):
            own[s, p] += rs_cross_got[s, p]
        last = (own[s, 0, :, TILE - 128 :], own[s, 1, :, TILE - 128 :])
        first = (own[s, 0, :, :128], own[s, 1, :, :128])
        edge_send[s, 0] = jnp.where(lower, pltpu.roll(last[0], MARGIN, 1), last[1])
        edge_send[s, 1] = jnp.where(lower, first[0], pltpu.roll(first[1], MARGIN, 1))
        rs_edge[s, 0].start()
        rs_edge[s, 1].start()

    def reduce_end(s):
        rs_edge[s, 0].wait_recv()
        rs_edge[s, 1].wait_recv()
        before, after = edge_got[s, 0], edge_got[s, 1]
        at_first = jnp.logical_and(lower, t > 0)
        at_last = jnp.logical_and(jnp.logical_not(lower), t < tiles - 1)
        outs = (out_re, out_im)
        befores = (before, pltpu.roll(before, MARGIN, 1))
        afters = (pltpu.roll(after, MARGIN, 1), after)
        for p in range(2):
            out = outs[p]
            out[0, s, :, :128] = own[s, p, :, :128] + jnp.where(at_first, befores[p], 0.0)
            out[0, s, :, 128 : TILE - 128] = own[s, p, :, 128 : TILE - 128]
            out[0, s, :, TILE - 128 :] = own[s, p, :, TILE - 128 :] + jnp.where(at_last, afters[p], 0.0)

    to_share[0].wait_recv()
    back_to_slice_1(0)
    back_to_probe(0)
    factors(1)
    to_share[1].wait_recv()
    back_to_slice_1(1)
    reduce_start(1)
    back_to_probe(1)
    reduce_start(0)
    reduce_middle(1)
    reduce_middle(0)
    reduce_end(1)
    reduce_end(0)

    for group in (sends, crosses, relays, rs_pair, rs_over, rs_edge):
        for copy in group.values():
            copy.wait_send()
    for group in (to_pair, to_other, to_share):
        for copy in group:
            copy.wait_send()


def gradients(obj_re, obj_im, probe, measured, positions, table, orders):
    tiles = lax.axis_size("tile")
    shape = jax.ShapeDtypeStruct
    anywhere = pl.BlockSpec(memory_space=pl.ANY)
    vmem = pl.BlockSpec(memory_space=pltpu.VMEM)
    return pl.pallas_call(
        functools.partial(kernel, tiles),
        out_shape=(shape(obj_re.shape, F32), shape(obj_im.shape, F32), shape(probe.shape, F32)),
        in_specs=[anywhere, anywhere, anywhere, anywhere, pl.BlockSpec(memory_space=pltpu.SMEM), anywhere, anywhere],
        out_specs=(vmem, vmem, vmem),
        scratch_shapes=[
            pltpu.VMEM((2, TILE, TILE), F32),
            pltpu.VMEM((2, TILE, TILE), F32),
            pltpu.VMEM((2, 2, 2, PX, PX), F32),
            pltpu.VMEM((2, 2, PX, PX), F32),
            pltpu.VMEM((2, PX, PX), F32),
            pltpu.VMEM(table.shape, BF16),
            pltpu.VMEM(orders.shape, BF16),
            pltpu.VMEM((2, 2, 2, PX, PX), F32),
            pltpu.VMEM((2, 2, 2, PX, PX), F32),
            pltpu.VMEM((2, PX, PX), F32),
            pltpu.VMEM((2, HALF, PX), F32),
            pltpu.VMEM((2, HALF, PX), F32),
            pltpu.VMEM((2, HALF, PX), F32),
            pltpu.VMEM((2, PX, PX), F32),
            pltpu.VMEM((2, 2, 2, PX + 2 * EDGE, TILE), F32),
            pltpu.VMEM((2, 2, 2, ROWS, TILE), F32),
            pltpu.VMEM((2, 2, 2, ROWS, TILE), F32),
            pltpu.VMEM((2, 2, ROWS, TILE), F32),
            pltpu.VMEM((2, 2, ROWS, TILE), F32),
            pltpu.VMEM((2, 2, ROWS, TILE), F32),
            pltpu.VMEM((2, 2, ROWS, 128), F32),
            pltpu.VMEM((2, 2, ROWS, 128), F32),
            pltpu.SemaphoreType.DMA((4,)),
            pltpu.SemaphoreType.DMA((2, 2)),
            pltpu.SemaphoreType.DMA((3, 2, 2)),
            pltpu.SemaphoreType.DMA((3, 2, 2)),
            pltpu.SemaphoreType.DMA((3, 2)),
            pltpu.SemaphoreType.DMA((3, 2)),
            pltpu.SemaphoreType.DMA((3, 2)),
            pltpu.SemaphoreType.DMA((3, 2)),
            pltpu.SemaphoreType.DMA((2, 2)),
            pltpu.SemaphoreType.DMA((2, 2)),
        ],
        compiler_params=pltpu.CompilerParams(
            collective_id=0, has_side_effects=True, vmem_limit_bytes=56 * 1024 * 1024
        ),
        cost_estimate=pl.CostEstimate(flops=7 * 10**9, bytes_accessed=10**7, transcendentals=10**6),
    )(obj_re, obj_im, probe, measured, positions, table, orders)


def total_of(shard, axis):
    count = lax.axis_size(axis)
    lines = shard.reshape(count, -1, shard.shape[-1])
    tiles = lax.all_to_all(lines, axis, 0, 0, tiled=True)
    own = jnp.sum(tiles, axis=0)
    copies = jnp.broadcast_to(own, (count, *own.shape))
    return lax.all_to_all(copies, axis, 0, 0, tiled=True).reshape(shard.shape)


def body(object_real, object_imag, probe, measured, positions):
    table, orders = constants()
    grad_re, grad_im, probe_part = gradients(
        object_real, object_imag, probe, measured, positions, jnp.asarray(table), jnp.asarray(orders)
    )
    return grad_re, grad_im, total_of(probe_part, "tile")


def solution(mesh):
    return jax.shard_map(
        body,
        mesh=mesh,
        in_specs=(
            P("tile", None, "mode", None),
            P("tile", None, "mode", None),
            P(None, "mode", None, None),
            P("tile", None, None, None),
            P("tile", None, None),
        ),
        out_specs=(
            P("tile", None, "mode", None),
            P("tile", None, "mode", None),
            P(None, "mode", None, None),
        ),
        check_vma=False,
    )
```

```python
import functools
import math

import jax
import jax.numpy as jnp
import ml_dtypes
import numpy as np
from jax import lax
from jax.experimental import pallas as pl
from jax.experimental.pallas import tpu as pltpu
from jax.sharding import PartitionSpec as P

PX = 256
HALF = PX // 2
TILE = 384
MARGIN = 64
ROWS = 96
EDGE = TILE - PX
FLOOR = 0.1
FRESNEL = 40.0
MESH = pl.DeviceIdType.MESH
F32 = jnp.float32
BF16 = jnp.bfloat16

A_LEFT, A_RIGHT, F_LEFT, F_RIGHT, B_LEFT, B_RIGHT = range(6)


def real_form(c):
    return np.block([[c.real, -c.imag], [c.imag, c.real]])


@functools.cache
def constants():
    index = np.arange(PX)
    fourier = np.exp(-2j * np.pi * (np.outer(index, index) % PX) / PX) / math.sqrt(PX)
    freq = ((index + HALF) % PX - HALF) / PX
    chirp = np.exp(-1j * np.pi * FRESNEL * freq**2)
    through = fourier.conj() @ (chirp[:, None] * fourier)
    near, far = through[:HALF, :HALF], through[:HALF, HALF:]
    pairs = [None] * 6
    moved = [(near + far) / 2, (near - far) / 2]
    split = [fourier[0::2, :HALF], fourier[1::2, :HALF]]
    pairs[A_LEFT] = [real_form(c) for c in moved]
    pairs[A_RIGHT] = [real_form(c).T for c in moved]
    pairs[F_LEFT] = [real_form(c) for c in split]
    pairs[F_RIGHT] = [real_form(c).T for c in split]
    pairs[B_LEFT] = [real_form(c.T) for c in split]
    pairs[B_RIGHT] = [real_form(c.T).T for c in split]
    table = np.array(pairs).reshape(12, PX, PX)
    high = table.astype(ml_dtypes.bfloat16)
    low = (table - high.astype(np.float64)).astype(ml_dtypes.bfloat16)
    order = np.zeros((PX, PX))
    order[np.arange(HALF), np.arange(0, PX, 2)] = 1
    order[np.arange(HALF) + HALF, np.arange(1, PX, 2)] = 1
    orders = np.array([order, order.T]).astype(ml_dtypes.bfloat16)
    return np.stack([high, low], axis=1), orders


def two_parts(x):
    high = x.astype(BF16)
    return high, (x - high.astype(F32)).astype(BF16)


def product(a, b):
    return jnp.dot(a, b, preferred_element_type=F32)


def apply_left(table, kind, sign, z):
    high, low = two_parts(z)
    c_high, c_low = table[2 * kind + sign, 0], table[2 * kind + sign, 1]
    return product(
        jnp.concatenate([c_high, c_low, c_high], axis=1),
        jnp.concatenate([high, high, low], axis=0),
    )


def apply_right(table, kind, sign, z):
    high, low = two_parts(z)
    c_high, c_low = table[2 * kind + sign, 0], table[2 * kind + sign, 1]
    return product(
        jnp.concatenate([high, high, low], axis=1),
        jnp.concatenate([c_high, c_low, c_high], axis=0),
    )


def rows_first(x):
    return x[:HALF], x[HALF:]


def lanes_first(x):
    return x[:, :HALF], x[:, HALF:]


def one_side(table, kind, re, im, left):
    halves, axis, apply = (rows_first, 0, apply_left) if left else (lanes_first, 1, apply_right)
    (r0, r1), (i0, i1) = halves(re), halves(im)
    if kind[0] != B_LEFT:
        r0, r1, i0, i1 = r0 + r1, r0 - r1, i0 + i1, i0 - i1
    which = kind[0] if left else kind[1]
    plus = apply(table, which, 0, jnp.concatenate([r0, i0], axis=axis))
    minus = apply(table, which, 1, jnp.concatenate([r1, i1], axis=axis))
    (pr, pi), (mr, mi) = halves(plus), halves(minus)
    if kind[0] != F_LEFT:
        pr, mr, pi, mi = pr + mr, pr - mr, pi + mi, pi - mi
    return jnp.concatenate([pr, mr], axis=axis), jnp.concatenate([pi, mi], axis=axis)


def both_sides(table, kind, re, im):
    re, im = one_side(table, kind, re, im, True)
    return one_side(table, kind, re, im, False)


THROUGH = (A_LEFT, A_RIGHT)
FORTH = (F_LEFT, F_RIGHT)
BACK = (B_LEFT, B_RIGHT)


def times(ar, ai, br, bi):
    return ar * br - ai * bi, ar * bi + ai * br


def kernel(
    tiles,
    obj_re,
    obj_im,
    probe_in,
    measured_in,
    positions,
    table_in,
    orders_in,
    out_re,
    out_im,
    out_probe,
    tile0,
    tile1,
    crops,
    probe,
    measured,
    table,
    orders,
    wave1,
    far,
    ipart,
    isib,
    isum,
    icross,
    factor,
    crop_grad,
    tile_grad,
    rs_send,
    rs_got,
    rs_cross,
    rs_cross_got,
    own,
    edge_send,
    edge_got,
    local_sem,
    tile_local,
    g_send,
    g_recv,
    i_send,
    i_recv,
    r_send,
    r_recv,
    e_send,
    e_recv,
    partial,
    got_a,
    got_b,
    part_b,
    y_send_buf,
    y_got,
    p_send,
    p_recv,
):
    t = lax.axis_index("tile")
    m = lax.axis_index("mode")
    core = lax.rem(m, 2)
    high = m // 2
    sibling = high * 2 + (1 - core)
    across = (1 - high) * 2 + core
    diagonal = (1 - high) * 2 + (1 - core)
    left = lax.rem(t + tiles - 1, tiles)
    right = lax.rem(t + 1, tiles)
    to_sibling, to_across = (t, sibling), (t, across)
    to_left, to_right = (left, m), (right, m)

    ring = 4
    tz, ty, tx = lax.rem(t, ring), lax.rem(t // ring, 2), t // (2 * ring)
    z_peers = [(t - tz + lax.rem(tz + d, ring), m) for d in range(1, ring)]
    x_peers = [(lax.rem(t + 2 * ring * d, tiles), m) for d in range(1, ring)]
    y_peer = (t + ring * (1 - 2 * ty), m)

    barrier = pltpu.get_barrier_semaphore()
    for device in (to_sibling, to_across, to_left, to_right, y_peer, *z_peers, *x_peers):
        pl.semaphore_signal(barrier, inc=1, device_id=device, device_id_type=MESH)

    loads = [
        pltpu.make_async_copy(probe_in, probe, local_sem.at[0]),
        pltpu.make_async_copy(measured_in.at[0], measured, local_sem.at[1]),
        pltpu.make_async_copy(table_in, table, local_sem.at[2]),
        pltpu.make_async_copy(orders_in, orders, local_sem.at[3]),
    ]
    for load in loads:
        load.start()

    whole = (tile0, tile1)
    objects = (obj_re, obj_im)

    def my_rows(who):
        return pl.ds(pl.multiple_of(who * ROWS, ROWS), ROWS)

    def remote(src, dst, send, recv, device):
        return pltpu.make_async_remote_copy(
            src_ref=src, dst_ref=dst, send_sem=send, recv_sem=recv, device_id=device, device_id_type=MESH
        )

    own_copies, sends, crosses, relays = {}, {}, {}, {}
    for s in range(2):
        for p in range(2):
            src = objects[p].at[0, s]
            dst = whole[s].at[p, my_rows(m)]
            own_copies[s, p] = pltpu.make_async_copy(src, dst, tile_local.at[s, p])
            crosses[s, p] = remote(src, dst, g_send.at[0, s, p], g_recv.at[0, s, p], to_across)
            sends[s, p] = remote(src, dst, g_send.at[1, s, p], g_recv.at[1, s, p], to_sibling)
            got = whole[s].at[p, my_rows(across)]
            relays[s, p] = remote(got, got, g_send.at[2, s, p], g_recv.at[2, s, p], to_sibling)

    pl.semaphore_wait(barrier, 11)
    for s in range(2):
        for p in range(2):
            crosses[s, p].start()
    for s in range(2):
        for p in range(2):
            own_copies[s, p].start()
            sends[s, p].start()

    crop_grad[...] = jnp.zeros_like(crop_grad)
    partial[...] = jnp.zeros_like(partial)
    for load in loads:
        load.wait()
    for f in range(2):
        m_high, m_low = two_parts(measured[f])
        mixed = product(orders[0], m_high) + product(orders[0], m_low)
        m_high, m_low = two_parts(mixed)
        measured[f] = product(m_high, orders[1]) + product(m_low, orders[1])

    def tile_ready(s):
        for p in range(2):
            crosses[s, p].wait_recv()
            relays[s, p].start()
        for p in range(2):
            own_copies[s, p].wait()
            sends[s, p].wait_recv()
        for p in range(2):
            relays[s, p].wait_recv()

    row = [positions[0, f, 0] for f in range(2)]
    col = [positions[0, f, 1] for f in range(2)]

    def take_crops(s):
        for f in range(2):
            up, back = lax.rem(TILE - row[f], TILE), lax.rem(TILE - col[f], TILE)
            for p in range(2):
                lines = pltpu.roll(whole[s][p], up, 0)[:PX]
                crops[f, s, p] = pltpu.roll(lines, back, 1)[:, :PX]

    tile_ready(0)
    take_crops(0)

    def pass_through(step, carry):
        f, mode = step // 2, lax.rem(step, 2)
        re, im = times(probe[0, mode], probe[1, mode], crops[f, 0, 0], crops[f, 0, 1])
        re, im = both_sides(table, THROUGH, re, im)
        wave1[f, mode, 0] = re
        wave1[f, mode, 1] = im
        return carry

    lax.fori_loop(0, 4, pass_through, 0)
    tile_ready(1)
    take_crops(1)

    def far_fields(f):
        ipart[f] = jnp.zeros_like(ipart[f])

        def step(mode, carry):
            re, im = times(wave1[f, mode, 0], wave1[f, mode, 1], crops[f, 1, 0], crops[f, 1, 1])
            re, im = both_sides(table, FORTH, re, im)
            far[f, mode, 0] = re
            far[f, mode, 1] = im
            ipart[f] += re * re + im * im
            return carry

        lax.fori_loop(0, 2, step, 0)

    def half_rows(who):
        return pl.ds(pl.multiple_of(who * HALF, HALF), HALF)

    to_pair = [
        remote(ipart.at[f, half_rows(1 - core)], isib.at[f], i_send.at[0, f], i_recv.at[0, f], to_sibling) for f in range(2)
    ]
    to_other = [remote(isum.at[f], icross.at[f], i_send.at[1, f], i_recv.at[1, f], to_across) for f in range(2)]
    to_share = [
        remote(
            factor.at[f, half_rows(core)],
            factor.at[f, half_rows(core)],
            i_send.at[2, f],
            i_recv.at[2, f],
            to_sibling,
        )
        for f in range(2)
    ]

    def pair_sum(f):
        to_pair[f].wait_recv()
        isum[f] = ipart[f, half_rows(core), :] + isib[f]
        to_other[f].start()

    def factors(f):
        to_other[f].wait_recv()
        total = isum[f] + icross[f]
        factor[f, half_rows(core), :] = 2.0 - 2.0 * measured[f, half_rows(core), :] / jnp.sqrt(total + FLOOR)
        to_share[f].start()

    far_fields(0)
    to_pair[0].start()
    far_fields(1)
    to_pair[1].start()
    pair_sum(0)
    pair_sum(1)
    factors(0)

    def back_to_slice_1(f):
        def step(mode, carry):
            weight = factor[f]
            re, im = weight * far[f, mode, 0], -(weight * far[f, mode, 1])
            re, im = both_sides(table, BACK, re, im)
            gr, gi = times(wave1[f, mode, 0], wave1[f, mode, 1], re, im)
            crop_grad[f, 1, 0] += gr
            crop_grad[f, 1, 1] -= gi
            re, im = times(crops[f, 1, 0], crops[f, 1, 1], re, im)
            far[f, mode, 0] = re
            far[f, mode, 1] = im
            return carry

        lax.fori_loop(0, 2, step, 0)

    def back_to_probe(steps):
        def step(k, carry):
            f, mode = steps[0][0], steps[0][1]
            if len(steps) > 1:
                f = f + k * (steps[1][0] - f)
                mode = mode + k * (steps[1][1] - mode)
            re, im = both_sides(table, THROUGH, far[f, mode, 0], far[f, mode, 1])
            gr, gi = times(probe[0, mode], probe[1, mode], re, im)
            crop_grad[f, 0, 0] += gr
            crop_grad[f, 0, 1] -= gi
            gr, gi = times(crops[f, 0, 0], crops[f, 0, 1], re, im)
            partial[mode, 0] += gr
            partial[mode, 1] -= gi
            return carry

        lax.fori_loop(0, len(steps), step, 0)

    def place(s):
        for p in range(2):
            total = None
            for f in range(2):
                wide = jnp.concatenate([crop_grad[f, s, p], jnp.zeros((PX, EDGE), F32)], axis=1)
                wide = pltpu.roll(wide, col[f], 1)
                wide = jnp.concatenate([wide, jnp.zeros((EDGE, TILE), F32)], axis=0)
                wide = pltpu.roll(wide, row[f], 0)
                total = wide if total is None else total + wide
            tile_grad[s, p] = total

    def piece(s, p, who):
        return tile_grad[s, p, my_rows(who), :]

    rs_pair, rs_over, rs_edge = {}, {}, {}
    for s in range(2):
        for k in range(2):
            rs_pair[s, k] = remote(rs_send.at[s, k], rs_got.at[s, k], r_send.at[k, s], r_recv.at[k, s], to_sibling)
        rs_over[s] = remote(rs_cross.at[s], rs_cross_got.at[s], r_send.at[2, s], r_recv.at[2, s], to_across)
        rs_edge[s, 0] = remote(edge_send.at[s, 0], edge_got.at[s, 0], e_send.at[0, s], e_recv.at[0, s], to_right)
        rs_edge[s, 1] = remote(edge_send.at[s, 1], edge_got.at[s, 1], e_send.at[1, s], e_recv.at[1, s], to_left)

    def reduce_start(s):
        place(s)
        for k, who in enumerate((diagonal, sibling)):
            for p in range(2):
                rs_send[s, k, p] = piece(s, p, who)
            rs_pair[s, k].start()
        for p in range(2):
            rs_cross[s, p] = piece(s, p, across)
        rs_pair[s, 0].wait_recv()
        for p in range(2):
            rs_cross[s, p] += rs_got[s, 0, p]
        rs_over[s].start()
        for p in range(2):
            own[s, p] = piece(s, p, m)
        rs_pair[s, 1].wait_recv()
        for p in range(2):
            own[s, p] += rs_got[s, 1, p]

    lane = lax.broadcasted_iota(jnp.int32, (ROWS, 128), 1)
    lower = lane < MARGIN

    def reduce_middle(s):
        rs_over[s].wait_recv()
        for p in range(2):
            own[s, p] += rs_cross_got[s, p]
        last = (own[s, 0, :, TILE - 128 :], own[s, 1, :, TILE - 128 :])
        first = (own[s, 0, :, :128], own[s, 1, :, :128])
        edge_send[s, 0] = jnp.where(lower, pltpu.roll(last[0], MARGIN, 1), last[1])
        edge_send[s, 1] = jnp.where(lower, first[0], pltpu.roll(first[1], MARGIN, 1))
        rs_edge[s, 0].start()
        rs_edge[s, 1].start()

    def reduce_end(s):
        rs_edge[s, 0].wait_recv()
        rs_edge[s, 1].wait_recv()
        before, after = edge_got[s, 0], edge_got[s, 1]
        at_first = jnp.logical_and(lower, t > 0)
        at_last = jnp.logical_and(jnp.logical_not(lower), t < tiles - 1)
        outs = (out_re, out_im)
        befores = (before, pltpu.roll(before, MARGIN, 1))
        afters = (pltpu.roll(after, MARGIN, 1), after)
        for p in range(2):
            out = outs[p]
            out[0, s, :, :128] = own[s, p, :, :128] + jnp.where(at_first, befores[p], 0.0)
            out[0, s, :, 128 : TILE - 128] = own[s, p, :, 128 : TILE - 128]
            out[0, s, :, TILE - 128 :] = own[s, p, :, TILE - 128 :] + jnp.where(at_last, afters[p], 0.0)

    axes = (((tz, z_peers), (tx, x_peers)), ((tx, x_peers), (tz, z_peers)))

    def block(length, index, base=0):
        return pl.ds(pl.multiple_of(base + index * length, length), length)

    scatter_a, scatter_b, swap_y, gather_b, gather_a = {}, {}, {}, {}, {}
    for c in range(2):
        (ia, peers_a), (ib, peers_b) = axes[c]
        for d in range(1, ring):
            k = d - 1
            ja, jb = lax.rem(ia + d, ring), lax.rem(ib + d, ring)
            scatter_a[c, k] = remote(
                partial.at[c, :, block(64, ja)], got_a.at[c, k], p_send.at[c, 0, k], p_recv.at[c, 0, k], peers_a[k]
            )
            scatter_b[c, k] = remote(
                part_b.at[c, :, block(16, jb)], got_b.at[c, k], p_send.at[c, 1, k], p_recv.at[c, 1, k], peers_b[k]
            )
            mine_b = out_probe.at[:, c, block(16, ib, ia * 64)]
            gather_b[c, k] = remote(mine_b, mine_b, p_send.at[c, 2, k], p_recv.at[c, 2, k], peers_b[k])
            mine_a = out_probe.at[:, c, block(64, ia)]
            gather_a[c, k] = remote(mine_a, mine_a, p_send.at[c, 3, k], p_recv.at[c, 3, k], peers_a[k])
        swap_y[c] = remote(y_send_buf.at[c], y_got.at[c], p_send.at[c, 4, 0], p_recv.at[c, 4, 0], y_peer)

    def probe_1(c):
        for k in (1, 0, 2):
            scatter_a[c, k].start()

    def probe_2(c):
        ia = axes[c][0][0]
        for k in range(3):
            scatter_a[c, k].wait_recv()
        part_b[c] = partial[c, :, block(64, ia), :] + got_a[c, 0] + got_a[c, 1] + got_a[c, 2]
        for k in (1, 0, 2):
            scatter_b[c, k].start()

    def probe_3(c):
        ib = axes[c][1][0]
        for k in range(3):
            scatter_b[c, k].wait_recv()
        y_send_buf[c] = part_b[c, :, block(16, ib), :] + got_b[c, 0] + got_b[c, 1] + got_b[c, 2]
        swap_y[c].start()

    def probe_4(c):
        ia, ib = axes[c][0][0], axes[c][1][0]
        swap_y[c].wait_recv()
        out_probe[:, c, block(16, ib, ia * 64), :] = y_send_buf[c] + y_got[c]
        for k in (1, 0, 2):
            gather_b[c, k].start()

    def probe_5(c):
        for k in range(3):
            gather_b[c, k].wait_recv()
        for k in (1, 0, 2):
            gather_a[c, k].start()

    def probe_6(c):
        for k in range(3):
            gather_a[c, k].wait_recv()

    to_share[0].wait_recv()
    back_to_slice_1(0)
    back_to_probe([(0, 0)])
    factors(1)
    to_share[1].wait_recv()
    back_to_slice_1(1)
    reduce_start(1)
    back_to_probe([(1, 0)])
    probe_1(0)
    back_to_probe([(0, 1), (1, 1)])
    probe_1(1)
    probe_2(0)
    reduce_start(0)
    probe_2(1)
    probe_3(0)
    reduce_middle(1)
    probe_3(1)
    probe_4(0)
    reduce_middle(0)
    probe_4(1)
    probe_5(0)
    reduce_end(1)
    probe_5(1)
    reduce_end(0)
    probe_6(0)
    probe_6(1)

    for group in (scatter_a, scatter_b, swap_y, gather_b, gather_a):
        for copy in group.values():
            copy.wait_send()
    for group in (sends, crosses, relays, rs_pair, rs_over, rs_edge):
        for copy in group.values():
            copy.wait_send()
    for group in (to_pair, to_other, to_share):
        for copy in group:
            copy.wait_send()


def gradients(obj_re, obj_im, probe, measured, positions, table, orders):
    tiles = lax.axis_size("tile")
    shape = jax.ShapeDtypeStruct
    anywhere = pl.BlockSpec(memory_space=pl.ANY)
    vmem = pl.BlockSpec(memory_space=pltpu.VMEM)
    return pl.pallas_call(
        functools.partial(kernel, tiles),
        out_shape=(shape(obj_re.shape, F32), shape(obj_im.shape, F32), shape(probe.shape, F32)),
        in_specs=[anywhere, anywhere, anywhere, anywhere, pl.BlockSpec(memory_space=pltpu.SMEM), anywhere, anywhere],
        out_specs=(vmem, vmem, vmem),
        scratch_shapes=[
            pltpu.VMEM((2, TILE, TILE), F32),
            pltpu.VMEM((2, TILE, TILE), F32),
            pltpu.VMEM((2, 2, 2, PX, PX), F32),
            pltpu.VMEM((2, 2, PX, PX), F32),
            pltpu.VMEM((2, PX, PX), F32),
            pltpu.VMEM(table.shape, BF16),
            pltpu.VMEM(orders.shape, BF16),
            pltpu.VMEM((2, 2, 2, PX, PX), F32),
            pltpu.VMEM((2, 2, 2, PX, PX), F32),
            pltpu.VMEM((2, PX, PX), F32),
            pltpu.VMEM((2, HALF, PX), F32),
            pltpu.VMEM((2, HALF, PX), F32),
            pltpu.VMEM((2, HALF, PX), F32),
            pltpu.VMEM((2, PX, PX), F32),
            pltpu.VMEM((2, 2, 2, PX, PX), F32),
            pltpu.VMEM((2, 2, TILE, TILE), F32),
            pltpu.VMEM((2, 2, 2, ROWS, TILE), F32),
            pltpu.VMEM((2, 2, 2, ROWS, TILE), F32),
            pltpu.VMEM((2, 2, ROWS, TILE), F32),
            pltpu.VMEM((2, 2, ROWS, TILE), F32),
            pltpu.VMEM((2, 2, ROWS, TILE), F32),
            pltpu.VMEM((2, 2, ROWS, 128), F32),
            pltpu.VMEM((2, 2, ROWS, 128), F32),
            pltpu.SemaphoreType.DMA((4,)),
            pltpu.SemaphoreType.DMA((2, 2)),
            pltpu.SemaphoreType.DMA((3, 2, 2)),
            pltpu.SemaphoreType.DMA((3, 2, 2)),
            pltpu.SemaphoreType.DMA((3, 2)),
            pltpu.SemaphoreType.DMA((3, 2)),
            pltpu.SemaphoreType.DMA((3, 2)),
            pltpu.SemaphoreType.DMA((3, 2)),
            pltpu.SemaphoreType.DMA((2, 2)),
            pltpu.SemaphoreType.DMA((2, 2)),
            pltpu.VMEM((2, 2, PX, PX), F32),
            pltpu.VMEM((2, 3, 2, 64, PX), F32),
            pltpu.VMEM((2, 3, 2, 16, PX), F32),
            pltpu.VMEM((2, 2, 64, PX), F32),
            pltpu.VMEM((2, 2, 16, PX), F32),
            pltpu.VMEM((2, 2, 16, PX), F32),
            pltpu.SemaphoreType.DMA((2, 5, 3)),
            pltpu.SemaphoreType.DMA((2, 5, 3)),
        ],
        compiler_params=pltpu.CompilerParams(
            collective_id=0, has_side_effects=True, vmem_limit_bytes=56 * 1024 * 1024
        ),
        cost_estimate=pl.CostEstimate(flops=7 * 10**9, bytes_accessed=10**7, transcendentals=10**6),
    )(obj_re, obj_im, probe, measured, positions, table, orders)


def body(object_real, object_imag, probe, measured, positions):
    table, orders = constants()
    return gradients(object_real, object_imag, probe, measured, positions, jnp.asarray(table), jnp.asarray(orders))


def solution(mesh):
    return jax.shard_map(
        body,
        mesh=mesh,
        in_specs=(
            P("tile", None, "mode", None),
            P("tile", None, "mode", None),
            P(None, "mode", None, None),
            P("tile", None, None, None),
            P("tile", None, None),
        ),
        out_specs=(
            P("tile", None, "mode", None),
            P("tile", None, "mode", None),
            P(None, "mode", None, None),
        ),
        check_vma=False,
    )
```

```python
import functools
import math

import jax
import jax.numpy as jnp
import ml_dtypes
import numpy as np
from jax import lax
from jax.experimental import pallas as pl
from jax.experimental.pallas import tpu as pltpu
from jax.sharding import PartitionSpec as P

PX = 256
HALF = PX // 2
TILE = 384
MARGIN = 64
ROWS = 96
EDGE = TILE - PX
FLOOR = 0.1
FRESNEL = 40.0
MESH = pl.DeviceIdType.MESH
F32 = jnp.float32
BF16 = jnp.bfloat16

A_LEFT, A_RIGHT, F_LEFT, F_RIGHT, B_LEFT, B_RIGHT = range(6)


def real_form(c):
    return np.block([[c.real, -c.imag], [c.imag, c.real]])


@functools.cache
def constants():
    index = np.arange(PX)
    fourier = np.exp(-2j * np.pi * (np.outer(index, index) % PX) / PX) / math.sqrt(PX)
    freq = ((index + HALF) % PX - HALF) / PX
    chirp = np.exp(-1j * np.pi * FRESNEL * freq**2)
    through = fourier.conj() @ (chirp[:, None] * fourier)
    near, far = through[:HALF, :HALF], through[:HALF, HALF:]
    pairs = [None] * 6
    moved = [(near + far) / 2, (near - far) / 2]
    split = [fourier[0::2, :HALF], fourier[1::2, :HALF]]
    pairs[A_LEFT] = [real_form(c) for c in moved]
    pairs[A_RIGHT] = [real_form(c).T for c in moved]
    pairs[F_LEFT] = [real_form(c) for c in split]
    pairs[F_RIGHT] = [real_form(c).T for c in split]
    pairs[B_LEFT] = [real_form(c.T) for c in split]
    pairs[B_RIGHT] = [real_form(c.T).T for c in split]
    table = np.array(pairs).reshape(12, PX, PX)
    high = table.astype(ml_dtypes.bfloat16)
    low = (table - high.astype(np.float64)).astype(ml_dtypes.bfloat16)
    order = np.zeros((PX, PX))
    order[np.arange(HALF), np.arange(0, PX, 2)] = 1
    order[np.arange(HALF) + HALF, np.arange(1, PX, 2)] = 1
    orders = np.array([order, order.T]).astype(ml_dtypes.bfloat16)
    return np.stack([high, low], axis=1), orders


def two_parts(x):
    high = x.astype(BF16)
    return high, (x - high.astype(F32)).astype(BF16)


def product(a, b):
    return jnp.dot(a, b, preferred_element_type=F32)


def apply_left(table, kind, sign, z):
    high, low = two_parts(z)
    c_high, c_low = table[2 * kind + sign, 0], table[2 * kind + sign, 1]
    return product(
        jnp.concatenate([c_high, c_low, c_high], axis=1),
        jnp.concatenate([high, high, low], axis=0),
    )


def apply_right(table, kind, sign, z):
    high, low = two_parts(z)
    c_high, c_low = table[2 * kind + sign, 0], table[2 * kind + sign, 1]
    return product(
        jnp.concatenate([high, high, low], axis=1),
        jnp.concatenate([c_high, c_low, c_high], axis=0),
    )


def rows_first(x):
    return x[:HALF], x[HALF:]


def lanes_first(x):
    return x[:, :HALF], x[:, HALF:]


def one_side(table, kind, re, im, left):
    halves, axis, apply = (rows_first, 0, apply_left) if left else (lanes_first, 1, apply_right)
    (r0, r1), (i0, i1) = halves(re), halves(im)
    if kind[0] != B_LEFT:
        r0, r1, i0, i1 = r0 + r1, r0 - r1, i0 + i1, i0 - i1
    which = kind[0] if left else kind[1]
    plus = apply(table, which, 0, jnp.concatenate([r0, i0], axis=axis))
    minus = apply(table, which, 1, jnp.concatenate([r1, i1], axis=axis))
    (pr, pi), (mr, mi) = halves(plus), halves(minus)
    if kind[0] != F_LEFT:
        pr, mr, pi, mi = pr + mr, pr - mr, pi + mi, pi - mi
    return jnp.concatenate([pr, mr], axis=axis), jnp.concatenate([pi, mi], axis=axis)


def both_sides(table, kind, re, im):
    re, im = one_side(table, kind, re, im, True)
    return one_side(table, kind, re, im, False)


THROUGH = (A_LEFT, A_RIGHT)
FORTH = (F_LEFT, F_RIGHT)
BACK = (B_LEFT, B_RIGHT)


def times(ar, ai, br, bi):
    return ar * br - ai * bi, ar * bi + ai * br


def kernel(
    tiles,
    obj_re,
    obj_im,
    probe_in,
    measured_in,
    positions,
    table_in,
    orders_in,
    out_re,
    out_im,
    out_probe,
    tile0,
    tile1,
    crops,
    probe,
    measured,
    table,
    orders,
    wave1,
    far,
    ipart,
    isib,
    isum,
    icross,
    factor,
    crop_grad,
    tile_grad,
    rs_send,
    rs_got,
    rs_cross,
    rs_cross_got,
    own,
    edge_send,
    edge_got,
    local_sem,
    tile_local,
    g_send,
    g_recv,
    i_send,
    i_recv,
    r_send,
    r_recv,
    e_send,
    e_recv,
    partial,
    got_a,
    got_b,
    part_b,
    y_send_buf,
    y_got,
    p_send,
    p_recv,
    total,
    out_sem,
    probe_sem,
):
    t = lax.axis_index("tile")
    m = lax.axis_index("mode")
    core = lax.rem(m, 2)
    high = m // 2
    sibling = high * 2 + (1 - core)
    across = (1 - high) * 2 + core
    diagonal = (1 - high) * 2 + (1 - core)
    left = lax.rem(t + tiles - 1, tiles)
    right = lax.rem(t + 1, tiles)
    to_sibling, to_across = (t, sibling), (t, across)
    to_left, to_right = (left, m), (right, m)

    ring = 4
    tz, ty, tx = lax.rem(t, ring), lax.rem(t // ring, 2), t // (2 * ring)
    z_peers = [(t - tz + lax.rem(tz + d, ring), m) for d in range(1, ring)]
    x_peers = [(lax.rem(t + 2 * ring * d, tiles), m) for d in range(1, ring)]
    y_peer = (t + ring * (1 - 2 * ty), m)

    barrier = pltpu.get_barrier_semaphore()
    for device in (to_sibling, to_across, to_left, to_right, y_peer, *z_peers, *x_peers):
        pl.semaphore_signal(barrier, inc=1, device_id=device, device_id_type=MESH)

    loads = [
        pltpu.make_async_copy(probe_in, probe, local_sem.at[0]),
        pltpu.make_async_copy(measured_in.at[0], measured, local_sem.at[1]),
        pltpu.make_async_copy(table_in, table, local_sem.at[2]),
        pltpu.make_async_copy(orders_in, orders, local_sem.at[3]),
    ]
    for load in loads:
        load.start()

    whole = (tile0, tile1)
    objects = (obj_re, obj_im)

    def my_rows(who):
        return pl.ds(pl.multiple_of(who * ROWS, ROWS), ROWS)

    def remote(src, dst, send, recv, device):
        return pltpu.make_async_remote_copy(
            src_ref=src, dst_ref=dst, send_sem=send, recv_sem=recv, device_id=device, device_id_type=MESH
        )

    own_copies, sends, crosses, relays = {}, {}, {}, {}
    for s in range(2):
        for p in range(2):
            src = objects[p].at[0, s]
            dst = whole[s].at[p, my_rows(m)]
            own_copies[s, p] = pltpu.make_async_copy(src, dst, tile_local.at[s, p])
            crosses[s, p] = remote(src, dst, g_send.at[0, s, p], g_recv.at[0, s, p], to_across)
            sends[s, p] = remote(src, dst, g_send.at[1, s, p], g_recv.at[1, s, p], to_sibling)
            got = whole[s].at[p, my_rows(across)]
            relays[s, p] = remote(got, got, g_send.at[2, s, p], g_recv.at[2, s, p], to_sibling)

    pl.semaphore_wait(barrier, 11)
    for s in range(2):
        for p in range(2):
            crosses[s, p].start()
    for s in range(2):
        for p in range(2):
            own_copies[s, p].start()
            sends[s, p].start()

    crop_grad[...] = jnp.zeros_like(crop_grad)
    partial[...] = jnp.zeros_like(partial)
    for load in loads:
        load.wait()
    for f in range(2):
        m_high, m_low = two_parts(measured[f])
        mixed = product(orders[0], m_high) + product(orders[0], m_low)
        m_high, m_low = two_parts(mixed)
        measured[f] = product(m_high, orders[1]) + product(m_low, orders[1])

    def tile_ready(s):
        for p in range(2):
            crosses[s, p].wait_recv()
            relays[s, p].start()
        for p in range(2):
            own_copies[s, p].wait()
            sends[s, p].wait_recv()
        for p in range(2):
            relays[s, p].wait_recv()

    row = [positions[0, f, 0] for f in range(2)]
    col = [positions[0, f, 1] for f in range(2)]

    def take_crops(s):
        for f in range(2):
            up, back = lax.rem(TILE - row[f], TILE), lax.rem(TILE - col[f], TILE)
            for p in range(2):
                lines = pltpu.roll(whole[s][p], up, 0)[:PX]
                crops[f, s, p] = pltpu.roll(lines, back, 1)[:, :PX]

    tile_ready(0)
    take_crops(0)

    def pass_through(step, carry):
        f, mode = step // 2, lax.rem(step, 2)
        re, im = times(probe[0, mode], probe[1, mode], crops[f, 0, 0], crops[f, 0, 1])
        re, im = both_sides(table, THROUGH, re, im)
        wave1[f, mode, 0] = re
        wave1[f, mode, 1] = im
        return carry

    lax.fori_loop(0, 4, pass_through, 0)
    tile_ready(1)
    take_crops(1)

    def far_fields(f):
        ipart[f] = jnp.zeros_like(ipart[f])

        def step(mode, carry):
            re, im = times(wave1[f, mode, 0], wave1[f, mode, 1], crops[f, 1, 0], crops[f, 1, 1])
            re, im = both_sides(table, FORTH, re, im)
            far[f, mode, 0] = re
            far[f, mode, 1] = im
            ipart[f] += re * re + im * im
            return carry

        lax.fori_loop(0, 2, step, 0)

    def half_rows(who):
        return pl.ds(pl.multiple_of(who * HALF, HALF), HALF)

    to_pair = [
        remote(ipart.at[f, half_rows(1 - core)], isib.at[f], i_send.at[0, f], i_recv.at[0, f], to_sibling) for f in range(2)
    ]
    to_other = [remote(isum.at[f], icross.at[f], i_send.at[1, f], i_recv.at[1, f], to_across) for f in range(2)]
    to_share = [
        remote(
            factor.at[f, half_rows(core)],
            factor.at[f, half_rows(core)],
            i_send.at[2, f],
            i_recv.at[2, f],
            to_sibling,
        )
        for f in range(2)
    ]

    def pair_sum(f):
        to_pair[f].wait_recv()
        isum[f] = ipart[f, half_rows(core), :] + isib[f]
        to_other[f].start()

    def factors(f):
        to_other[f].wait_recv()
        whole_sum = isum[f] + icross[f]
        factor[f, half_rows(core), :] = 2.0 - 2.0 * measured[f, half_rows(core), :] / jnp.sqrt(whole_sum + FLOOR)
        to_share[f].start()

    far_fields(0)
    to_pair[0].start()
    far_fields(1)
    to_pair[1].start()
    pair_sum(0)
    pair_sum(1)
    factors(0)

    def over(steps, body):
        def step(k, carry):
            f, mode = steps[0]
            if len(steps) > 1:
                f = f + k * (steps[1][0] - f)
                mode = mode + k * (steps[1][1] - mode)
            body(f, mode)
            return carry

        lax.fori_loop(0, len(steps), step, 0)

    def slice_1_step(f, mode):
        weight = factor[f]
        re, im = weight * far[f, mode, 0], -(weight * far[f, mode, 1])
        re, im = both_sides(table, BACK, re, im)
        gr, gi = times(wave1[f, mode, 0], wave1[f, mode, 1], re, im)
        crop_grad[f, 1, 0] += gr
        crop_grad[f, 1, 1] -= gi
        re, im = times(crops[f, 1, 0], crops[f, 1, 1], re, im)
        far[f, mode, 0] = re
        far[f, mode, 1] = im

    def probe_step(f, mode):
        re, im = both_sides(table, THROUGH, far[f, mode, 0], far[f, mode, 1])
        gr, gi = times(probe[0, mode], probe[1, mode], re, im)
        crop_grad[f, 0, 0] += gr
        crop_grad[f, 0, 1] -= gi
        gr, gi = times(crops[f, 0, 0], crops[f, 0, 1], re, im)
        partial[mode, 0] += gr
        partial[mode, 1] -= gi

    def both_steps(f, mode):
        slice_1_step(f, mode)
        probe_step(f, mode)

    def place(s):
        for p in range(2):
            placed = None
            for f in range(2):
                wide = jnp.concatenate([crop_grad[f, s, p], jnp.zeros((PX, EDGE), F32)], axis=1)
                wide = pltpu.roll(wide, col[f], 1)
                wide = jnp.concatenate([wide, jnp.zeros((EDGE, TILE), F32)], axis=0)
                wide = pltpu.roll(wide, row[f], 0)
                placed = wide if placed is None else placed + wide
            tile_grad[s, p] = placed

    def piece(s, p, who):
        return tile_grad[s, p, my_rows(who), :]

    parts = (pl.ds(0, 128), pl.ds(TILE - 128, 128), pl.ds(128, TILE - 256))
    rs_pair, rs_over, rs_edge, outward = {}, {}, {}, {}
    for s in range(2):
        for k in range(2):
            rs_pair[s, k] = remote(rs_send.at[s, k], rs_got.at[s, k], r_send.at[k, s], r_recv.at[k, s], to_sibling)
        for k in range(3):
            rs_over[s, k] = remote(
                rs_cross.at[s, :, :, parts[k]],
                rs_cross_got.at[s, :, :, parts[k]],
                r_send.at[2 + k, s],
                r_recv.at[2 + k, s],
                to_across,
            )
        rs_edge[s, 0] = remote(edge_send.at[s, 0], edge_got.at[s, 0], e_send.at[0, s], e_recv.at[0, s], to_right)
        rs_edge[s, 1] = remote(edge_send.at[s, 1], edge_got.at[s, 1], e_send.at[1, s], e_recv.at[1, s], to_left)
        for p in range(2):
            outward[s, p] = pltpu.make_async_copy(own.at[s, p], (out_re, out_im)[p].at[0, s], out_sem.at[s, p])

    def reduce_1(s):
        place(s)
        for k, who in enumerate((diagonal, sibling)):
            for p in range(2):
                rs_send[s, k, p] = piece(s, p, who)
            rs_pair[s, k].start()

    def reduce_2(s):
        rs_pair[s, 0].wait_recv()
        for p in range(2):
            rs_cross[s, p] = piece(s, p, across) + rs_got[s, 0, p]
        for k in range(3):
            rs_over[s, k].start()
        rs_pair[s, 1].wait_recv()
        for p in range(2):
            own[s, p] = piece(s, p, m) + rs_got[s, 1, p]

    lane = lax.broadcasted_iota(jnp.int32, (ROWS, 128), 1)
    lower = lane < MARGIN

    def reduce_3(s):
        for k in range(2):
            rs_over[s, k].wait_recv()
            for p in range(2):
                own[s, p, :, parts[k]] += rs_cross_got[s, p, :, parts[k]]
        last = (own[s, 0, :, TILE - 128 :], own[s, 1, :, TILE - 128 :])
        first = (own[s, 0, :, :128], own[s, 1, :, :128])
        edge_send[s, 0] = jnp.where(lower, pltpu.roll(last[0], MARGIN, 1), last[1])
        edge_send[s, 1] = jnp.where(lower, first[0], pltpu.roll(first[1], MARGIN, 1))
        rs_edge[s, 0].start()
        rs_edge[s, 1].start()

    def reduce_4(s):
        rs_over[s, 2].wait_recv()
        for p in range(2):
            own[s, p, :, parts[2]] += rs_cross_got[s, p, :, parts[2]]
        rs_edge[s, 0].wait_recv()
        rs_edge[s, 1].wait_recv()
        before, after = edge_got[s, 0], edge_got[s, 1]
        at_first = jnp.logical_and(lower, t > 0)
        at_last = jnp.logical_and(jnp.logical_not(lower), t < tiles - 1)
        befores = (before, pltpu.roll(before, MARGIN, 1))
        afters = (pltpu.roll(after, MARGIN, 1), after)
        for p in range(2):
            own[s, p, :, parts[0]] += jnp.where(at_first, befores[p], 0.0)
            own[s, p, :, parts[1]] += jnp.where(at_last, afters[p], 0.0)
            outward[s, p].start()

    axes = (((tz, z_peers), (tx, x_peers)), ((tx, x_peers), (tz, z_peers)))

    def block(length, index, base=0):
        return pl.ds(pl.multiple_of(base + index * length, length), length)

    scatter_a, scatter_b, swap_y, gather_b, gather_a, probe_out = {}, {}, {}, {}, {}, {}
    chunks = range(2)
    for c in chunks:
        (ia, peers_a), (ib, peers_b) = axes[c]
        for k in range(ring - 1):
            ja, jb = lax.rem(ia + k + 1, ring), lax.rem(ib + k + 1, ring)
            sems = [(p_send.at[c, i, k], p_recv.at[c, i, k]) for i in range(4)]
            scatter_a[c, k] = remote(
                partial.at[c, :, block(64, ja)], got_a.at[c, k], *sems[0], peers_a[k]
            )
            scatter_b[c, k] = remote(part_b.at[c, :, block(16, jb)], got_b.at[c, k], *sems[1], peers_b[k])
            mine_b = total.at[:, c, block(16, ib, ia * 64)]
            gather_b[c, k] = remote(mine_b, mine_b, *sems[2], peers_b[k])
            mine_a = total.at[:, c, block(64, ia)]
            gather_a[c, k] = remote(mine_a, mine_a, *sems[3], peers_a[k])
        swap_y[c] = remote(y_send_buf.at[c], y_got.at[c], p_send.at[c, 4, 0], p_recv.at[c, 4, 0], y_peer)
        probe_out[c] = pltpu.make_async_copy(total.at[:, c], out_probe.at[:, c], probe_sem.at[c])

    def send_all(group, c):
        for k in (1, 0, 2):
            group[c, k].start()

    def take_all(group, c):
        for k in range(3):
            group[c, k].wait_recv()

    def probe_1(c):
        send_all(scatter_a, c)

    def probe_2(c):
        ia = axes[c][0][0]
        take_all(scatter_a, c)
        got = got_a[c, 0] + got_a[c, 1] + got_a[c, 2]
        part_b[c] = partial[c, :, block(64, ia), :] + got
        send_all(scatter_b, c)

    def probe_3(c):
        ib = axes[c][1][0]
        take_all(scatter_b, c)
        got = got_b[c, 0] + got_b[c, 1] + got_b[c, 2]
        y_send_buf[c] = part_b[c, :, block(16, ib), :] + got
        swap_y[c].start()

    def probe_4(c):
        ia, ib = axes[c][0][0], axes[c][1][0]
        swap_y[c].wait_recv()
        total[:, c, block(16, ib, ia * 64), :] = y_send_buf[c] + y_got[c]
        send_all(gather_b, c)

    def probe_5(c):
        take_all(gather_b, c)
        send_all(gather_a, c)

    def probe_6(c):
        take_all(gather_a, c)
        probe_out[c].start()

    def each(step):
        for c in range(2):
            step(c)

    to_share[0].wait_recv()
    over([(0, 0), (0, 1)], both_steps)
    factors(1)
    to_share[1].wait_recv()
    over([(1, 0)], both_steps)
    probe_1(0)
    over([(1, 1)], both_steps)
    probe_1(1)
    reduce_1(1)
    reduce_1(0)
    reduce_2(1)
    each(probe_2)
    each(probe_3)
    reduce_2(0)
    each(probe_4)
    reduce_3(1)
    each(probe_5)
    reduce_4(1)
    reduce_3(0)
    reduce_4(0)
    each(probe_6)

    for group in (probe_out, outward):
        for copy in group.values():
            copy.wait()
    for group in (scatter_a, scatter_b, swap_y, gather_b, gather_a):
        for copy in group.values():
            copy.wait_send()
    for group in (sends, crosses, relays, rs_pair, rs_over, rs_edge):
        for copy in group.values():
            copy.wait_send()
    for group in (to_pair, to_other, to_share):
        for copy in group:
            copy.wait_send()


def gradients(obj_re, obj_im, probe, measured, positions, table, orders):
    tiles = lax.axis_size("tile")
    shape = jax.ShapeDtypeStruct
    anywhere = pl.BlockSpec(memory_space=pl.ANY)
    return pl.pallas_call(
        functools.partial(kernel, tiles),
        out_shape=(shape(obj_re.shape, F32), shape(obj_im.shape, F32), shape(probe.shape, F32)),
        in_specs=[anywhere, anywhere, anywhere, anywhere, pl.BlockSpec(memory_space=pltpu.SMEM), anywhere, anywhere],
        out_specs=(anywhere, anywhere, anywhere),
        scratch_shapes=[
            pltpu.VMEM((2, TILE, TILE), F32),
            pltpu.VMEM((2, TILE, TILE), F32),
            pltpu.VMEM((2, 2, 2, PX, PX), F32),
            pltpu.VMEM((2, 2, PX, PX), F32),
            pltpu.VMEM((2, PX, PX), F32),
            pltpu.VMEM(table.shape, BF16),
            pltpu.VMEM(orders.shape, BF16),
            pltpu.VMEM((2, 2, 2, PX, PX), F32),
            pltpu.VMEM((2, 2, 2, PX, PX), F32),
            pltpu.VMEM((2, PX, PX), F32),
            pltpu.VMEM((2, HALF, PX), F32),
            pltpu.VMEM((2, HALF, PX), F32),
            pltpu.VMEM((2, HALF, PX), F32),
            pltpu.VMEM((2, PX, PX), F32),
            pltpu.VMEM((2, 2, 2, PX, PX), F32),
            pltpu.VMEM((2, 2, TILE, TILE), F32),
            pltpu.VMEM((2, 2, 2, ROWS, TILE), F32),
            pltpu.VMEM((2, 2, 2, ROWS, TILE), F32),
            pltpu.VMEM((2, 2, ROWS, TILE), F32),
            pltpu.VMEM((2, 2, ROWS, TILE), F32),
            pltpu.VMEM((2, 2, ROWS, TILE), F32),
            pltpu.VMEM((2, 2, ROWS, 128), F32),
            pltpu.VMEM((2, 2, ROWS, 128), F32),
            pltpu.SemaphoreType.DMA((4,)),
            pltpu.SemaphoreType.DMA((2, 2)),
            pltpu.SemaphoreType.DMA((3, 2, 2)),
            pltpu.SemaphoreType.DMA((3, 2, 2)),
            pltpu.SemaphoreType.DMA((3, 2)),
            pltpu.SemaphoreType.DMA((3, 2)),
            pltpu.SemaphoreType.DMA((5, 2)),
            pltpu.SemaphoreType.DMA((5, 2)),
            pltpu.SemaphoreType.DMA((2, 2)),
            pltpu.SemaphoreType.DMA((2, 2)),
            pltpu.VMEM((2, 2, PX, PX), F32),
            pltpu.VMEM((2, 3, 2, 64, PX), F32),
            pltpu.VMEM((2, 3, 2, 16, PX), F32),
            pltpu.VMEM((2, 2, 64, PX), F32),
            pltpu.VMEM((2, 2, 16, PX), F32),
            pltpu.VMEM((2, 2, 16, PX), F32),
            pltpu.SemaphoreType.DMA((2, 5, 3)),
            pltpu.SemaphoreType.DMA((2, 5, 3)),
            pltpu.VMEM((2, 2, PX, PX), F32),
            pltpu.SemaphoreType.DMA((2, 2)),
            pltpu.SemaphoreType.DMA((2,)),
        ],
        compiler_params=pltpu.CompilerParams(
            collective_id=0, has_side_effects=True, vmem_limit_bytes=56 * 1024 * 1024
        ),
        cost_estimate=pl.CostEstimate(flops=7 * 10**9, bytes_accessed=10**7, transcendentals=10**6),
    )(obj_re, obj_im, probe, measured, positions, table, orders)


def deliver_kernel(count, *refs):
    sources, targets, held = refs[:count], refs[count : 2 * count], refs[2 * count : 3 * count]
    in_sem, out_sem = refs[3 * count :]
    inward, outward = [], []
    for i in range(count):
        for k in range(2):
            at = (slice(None), k)
            inward.append(pltpu.make_async_copy(sources[i].at[at], held[i].at[at], in_sem.at[i, k]))
            outward.append(pltpu.make_async_copy(held[i].at[at], targets[i].at[at], out_sem.at[i, k]))
    for copy in inward:
        copy.start()
    for copy, onward in zip(inward, outward):
        copy.wait()
        onward.start()
    for copy in outward:
        copy.wait()


def delivered(arrays):
    anywhere = pl.BlockSpec(memory_space=pl.ANY)
    count = len(arrays)
    return pl.pallas_call(
        functools.partial(deliver_kernel, count),
        out_shape=tuple(jax.ShapeDtypeStruct(a.shape, a.dtype) for a in arrays),
        in_specs=[anywhere] * count,
        out_specs=(anywhere,) * count,
        scratch_shapes=[pltpu.VMEM(a.shape, a.dtype) for a in arrays]
        + [pltpu.SemaphoreType.DMA((count, 2)), pltpu.SemaphoreType.DMA((count, 2))],
        compiler_params=pltpu.CompilerParams(vmem_limit_bytes=56 * 1024 * 1024),
    )(*arrays)


def body(object_real, object_imag, probe, measured, positions):
    table, orders = constants()
    return delivered(
        gradients(object_real, object_imag, probe, measured, positions, jnp.asarray(table), jnp.asarray(orders))
    )


def solution(mesh):
    return jax.shard_map(
        body,
        mesh=mesh,
        in_specs=(
            P("tile", None, "mode", None),
            P("tile", None, "mode", None),
            P(None, "mode", None, None),
            P("tile", None, None, None),
            P("tile", None, None),
        ),
        out_specs=(
            P("tile", None, "mode", None),
            P("tile", None, "mode", None),
            P(None, "mode", None, None),
        ),
        check_vma=False,
    )
```

```python
import functools
import math

import jax
import jax.numpy as jnp
import ml_dtypes
import numpy as np
from jax import lax
from jax.experimental import pallas as pl
from jax.experimental.pallas import tpu as pltpu
from jax.sharding import PartitionSpec as P

PX = 256
HALF = PX // 2
TILE = 384
MARGIN = 64
ROWS = 96
EDGE = TILE - PX
FLOOR = 0.1
FRESNEL = 40.0
MESH = pl.DeviceIdType.MESH
F32 = jnp.float32
BF16 = jnp.bfloat16

A_LEFT, A_RIGHT, F_LEFT, F_RIGHT, B_LEFT, B_RIGHT = range(6)


def real_form(c):
    return np.block([[c.real, -c.imag], [c.imag, c.real]])


@functools.cache
def constants():
    index = np.arange(PX)
    fourier = np.exp(-2j * np.pi * (np.outer(index, index) % PX) / PX) / math.sqrt(PX)
    freq = ((index + HALF) % PX - HALF) / PX
    chirp = np.exp(-1j * np.pi * FRESNEL * freq**2)
    through = fourier.conj() @ (chirp[:, None] * fourier)
    near, far = through[:HALF, :HALF], through[:HALF, HALF:]
    pairs = [None] * 6
    moved = [(near + far) / 2, (near - far) / 2]
    split = [fourier[0::2, :HALF], fourier[1::2, :HALF]]
    pairs[A_LEFT] = [real_form(c) for c in moved]
    pairs[A_RIGHT] = [real_form(c).T for c in moved]
    pairs[F_LEFT] = [real_form(c) for c in split]
    pairs[F_RIGHT] = [real_form(c).T for c in split]
    pairs[B_LEFT] = [real_form(c.T) for c in split]
    pairs[B_RIGHT] = [real_form(c.T).T for c in split]
    table = np.array(pairs).reshape(12, PX, PX)
    high = table.astype(ml_dtypes.bfloat16)
    low = (table - high.astype(np.float64)).astype(ml_dtypes.bfloat16)
    order = np.zeros((PX, PX))
    order[np.arange(HALF), np.arange(0, PX, 2)] = 1
    order[np.arange(HALF) + HALF, np.arange(1, PX, 2)] = 1
    orders = np.array([order, order.T]).astype(ml_dtypes.bfloat16)
    return np.stack([high, low], axis=1), orders


def two_parts(x):
    high = x.astype(BF16)
    return high, (x - high.astype(F32)).astype(BF16)


def product(a, b):
    return jnp.dot(a, b, preferred_element_type=F32)


def apply_left(table, kind, sign, z):
    high, low = two_parts(z)
    c_high, c_low = table[2 * kind + sign, 0], table[2 * kind + sign, 1]
    return product(
        jnp.concatenate([c_high, c_low, c_high], axis=1),
        jnp.concatenate([high, high, low], axis=0),
    )


def apply_right(table, kind, sign, z):
    high, low = two_parts(z)
    c_high, c_low = table[2 * kind + sign, 0], table[2 * kind + sign, 1]
    return product(
        jnp.concatenate([high, high, low], axis=1),
        jnp.concatenate([c_high, c_low, c_high], axis=0),
    )


def rows_first(x):
    return x[:HALF], x[HALF:]


def lanes_first(x):
    return x[:, :HALF], x[:, HALF:]


def one_side(table, kind, re, im, left):
    halves, axis, apply = (rows_first, 0, apply_left) if left else (lanes_first, 1, apply_right)
    (r0, r1), (i0, i1) = halves(re), halves(im)
    if kind[0] != B_LEFT:
        r0, r1, i0, i1 = r0 + r1, r0 - r1, i0 + i1, i0 - i1
    which = kind[0] if left else kind[1]
    plus = apply(table, which, 0, jnp.concatenate([r0, i0], axis=axis))
    minus = apply(table, which, 1, jnp.concatenate([r1, i1], axis=axis))
    (pr, pi), (mr, mi) = halves(plus), halves(minus)
    if kind[0] != F_LEFT:
        pr, mr, pi, mi = pr + mr, pr - mr, pi + mi, pi - mi
    return jnp.concatenate([pr, mr], axis=axis), jnp.concatenate([pi, mi], axis=axis)


def both_sides(table, kind, re, im):
    re, im = one_side(table, kind, re, im, True)
    return one_side(table, kind, re, im, False)


THROUGH = (A_LEFT, A_RIGHT)
FORTH = (F_LEFT, F_RIGHT)
BACK = (B_LEFT, B_RIGHT)


def times(ar, ai, br, bi):
    return ar * br - ai * bi, ar * bi + ai * br


def kernel(
    tiles,
    obj_re,
    obj_im,
    probe_in,
    measured_in,
    positions,
    table_in,
    orders_in,
    out_re,
    out_im,
    out_probe,
    tile0,
    tile1,
    crops,
    probe,
    measured,
    table,
    orders,
    wave1,
    far,
    ipart,
    isib,
    isum,
    icross,
    factor,
    crop_grad,
    tile_grad,
    rs_send,
    rs_got,
    rs_cross,
    rs_cross_got,
    own,
    edge_send,
    edge_got,
    local_sem,
    tile_local,
    g_send,
    g_recv,
    i_send,
    i_recv,
    r_send,
    r_recv,
    e_send,
    e_recv,
    partial,
    got_a,
    got_b,
    part_b,
    y_send_buf,
    y_got,
    p_send,
    p_recv,
    total,
    out_sem,
    probe_sem,
):
    t = lax.axis_index("tile")
    m = lax.axis_index("mode")
    core = lax.rem(m, 2)
    high = m // 2
    sibling = high * 2 + (1 - core)
    across = (1 - high) * 2 + core
    diagonal = (1 - high) * 2 + (1 - core)
    left = lax.rem(t + tiles - 1, tiles)
    right = lax.rem(t + 1, tiles)
    to_sibling, to_across = (t, sibling), (t, across)
    to_left, to_right = (left, m), (right, m)

    ring = 4
    tz, ty, tx = lax.rem(t, ring), lax.rem(t // ring, 2), t // (2 * ring)
    z_peers = [(t - tz + lax.rem(tz + d, ring), m) for d in range(1, ring)]
    x_peers = [(lax.rem(t + 2 * ring * d, tiles), m) for d in range(1, ring)]
    y_peer = (t + ring * (1 - 2 * ty), m)

    barrier = pltpu.get_barrier_semaphore()
    for device in (to_sibling, to_across, to_left, to_right, y_peer, *z_peers, *x_peers):
        pl.semaphore_signal(barrier, inc=1, device_id=device, device_id_type=MESH)

    loads = [
        pltpu.make_async_copy(probe_in, probe, local_sem.at[0]),
        pltpu.make_async_copy(measured_in.at[0], measured, local_sem.at[1]),
        pltpu.make_async_copy(table_in, table, local_sem.at[2]),
        pltpu.make_async_copy(orders_in, orders, local_sem.at[3]),
    ]
    for load in loads:
        load.start()

    whole = (tile0, tile1)
    objects = (obj_re, obj_im)

    def my_rows(who):
        return pl.ds(pl.multiple_of(who * ROWS, ROWS), ROWS)

    def remote(src, dst, send, recv, device):
        return pltpu.make_async_remote_copy(
            src_ref=src, dst_ref=dst, send_sem=send, recv_sem=recv, device_id=device, device_id_type=MESH
        )

    own_copies, sends, crosses, relays = {}, {}, {}, {}
    for s in range(2):
        for p in range(2):
            src = objects[p].at[0, s]
            dst = whole[s].at[p, my_rows(m)]
            own_copies[s, p] = pltpu.make_async_copy(src, dst, tile_local.at[s, p])
            crosses[s, p] = remote(src, dst, g_send.at[0, s, p], g_recv.at[0, s, p], to_across)
            sends[s, p] = remote(src, dst, g_send.at[1, s, p], g_recv.at[1, s, p], to_sibling)
            got = whole[s].at[p, my_rows(across)]
            relays[s, p] = remote(got, got, g_send.at[2, s, p], g_recv.at[2, s, p], to_sibling)

    pl.semaphore_wait(barrier, 11)
    for s in range(2):
        for p in range(2):
            crosses[s, p].start()
    for s in range(2):
        for p in range(2):
            own_copies[s, p].start()
            sends[s, p].start()

    crop_grad[...] = jnp.zeros_like(crop_grad)
    partial[...] = jnp.zeros_like(partial)
    for load in loads:
        load.wait()
    for f in range(2):
        m_high, m_low = two_parts(measured[f])
        mixed = product(orders[0], m_high) + product(orders[0], m_low)
        m_high, m_low = two_parts(mixed)
        measured[f] = product(m_high, orders[1]) + product(m_low, orders[1])

    def tile_ready(s):
        for p in range(2):
            crosses[s, p].wait_recv()
            relays[s, p].start()
        for p in range(2):
            own_copies[s, p].wait()
            sends[s, p].wait_recv()
        for p in range(2):
            relays[s, p].wait_recv()

    row = [positions[0, f, 0] for f in range(2)]
    col = [positions[0, f, 1] for f in range(2)]

    def take_crops(s, frames=(0, 1)):
        for f in frames:
            up, back = lax.rem(TILE - row[f], TILE), lax.rem(TILE - col[f], TILE)
            for p in range(2):
                lines = pltpu.roll(whole[s][p], up, 0)[:PX]
                crops[f, s, p] = pltpu.roll(lines, back, 1)[:, :PX]

    tile_ready(0)
    take_crops(0)

    def pass_through(step, carry):
        f, mode = step // 2, lax.rem(step, 2)
        re, im = times(probe[0, mode], probe[1, mode], crops[f, 0, 0], crops[f, 0, 1])
        re, im = both_sides(table, THROUGH, re, im)
        wave1[f, mode, 0] = re
        wave1[f, mode, 1] = im
        return carry

    lax.fori_loop(0, 4, pass_through, 0, unroll=2)
    tile_ready(1)
    take_crops(1, (0,))

    def far_fields(f):
        ipart[f] = jnp.zeros_like(ipart[f])

        def step(mode, carry):
            re, im = times(wave1[f, mode, 0], wave1[f, mode, 1], crops[f, 1, 0], crops[f, 1, 1])
            re, im = both_sides(table, FORTH, re, im)
            far[f, mode, 0] = re
            far[f, mode, 1] = im
            ipart[f] += re * re + im * im
            return carry

        lax.fori_loop(0, 2, step, 0, unroll=True)

    def half_rows(who):
        return pl.ds(pl.multiple_of(who * HALF, HALF), HALF)

    to_pair = [
        remote(ipart.at[f, half_rows(1 - core)], isib.at[f], i_send.at[0, f], i_recv.at[0, f], to_sibling) for f in range(2)
    ]
    to_other = [remote(isum.at[f], icross.at[f], i_send.at[1, f], i_recv.at[1, f], to_across) for f in range(2)]
    to_share = [
        remote(
            factor.at[f, half_rows(core)],
            factor.at[f, half_rows(core)],
            i_send.at[2, f],
            i_recv.at[2, f],
            to_sibling,
        )
        for f in range(2)
    ]

    def pair_sum(f):
        to_pair[f].wait_recv()
        isum[f] = ipart[f, half_rows(core), :] + isib[f]
        to_other[f].start()

    def factors(f):
        to_other[f].wait_recv()
        whole_sum = isum[f] + icross[f]
        factor[f, half_rows(core), :] = 2.0 - 2.0 * measured[f, half_rows(core), :] / jnp.sqrt(whole_sum + FLOOR)
        to_share[f].start()

    far_fields(0)
    to_pair[0].start()
    take_crops(1, (1,))
    far_fields(1)
    to_pair[1].start()
    pair_sum(0)
    pair_sum(1)
    factors(0)

    def over(steps, body):
        def step(k, carry):
            f, mode = steps[0]
            if len(steps) > 1:
                f = f + k * (steps[1][0] - f)
                mode = mode + k * (steps[1][1] - mode)
            body(f, mode)
            return carry

        lax.fori_loop(0, len(steps), step, 0)

    def slice_1_step(f, mode):
        weight = factor[f]
        re, im = weight * far[f, mode, 0], -(weight * far[f, mode, 1])
        re, im = both_sides(table, BACK, re, im)
        gr, gi = times(wave1[f, mode, 0], wave1[f, mode, 1], re, im)
        crop_grad[f, 1, 0] += gr
        crop_grad[f, 1, 1] -= gi
        re, im = times(crops[f, 1, 0], crops[f, 1, 1], re, im)
        far[f, mode, 0] = re
        far[f, mode, 1] = im

    def probe_step(f, mode):
        re, im = both_sides(table, THROUGH, far[f, mode, 0], far[f, mode, 1])
        gr, gi = times(probe[0, mode], probe[1, mode], re, im)
        crop_grad[f, 0, 0] += gr
        crop_grad[f, 0, 1] -= gi
        gr, gi = times(crops[f, 0, 0], crops[f, 0, 1], re, im)
        partial[mode, 0] += gr
        partial[mode, 1] -= gi

    def both_steps(f, mode):
        slice_1_step(f, mode)
        probe_step(f, mode)

    low_lanes = lax.broadcasted_iota(jnp.int32, (TILE, 128), 1) < MARGIN

    def place(s, f):
        for p in range(2):
            wide = jnp.concatenate([crop_grad[f, s, p], jnp.zeros((PX, EDGE), F32)], axis=1)
            wide = pltpu.roll(wide, col[f], 1)
            wide = jnp.concatenate([wide, jnp.zeros((EDGE, TILE), F32)], axis=0)
            wide = pltpu.roll(wide, row[f], 0)
            first, middle, last = wide[:, :128], wide[:, 128:256], wide[:, 256:]
            ends, between = jnp.where(low_lanes, first, last), jnp.where(low_lanes, last, first)
            blocks = jnp.concatenate([ends, middle, between], axis=1)
            tile_grad[s, p] = blocks if f == 0 else tile_grad[s, p] + blocks

    def piece(s, p, who):
        return tile_grad[s, p, my_rows(who), :]

    parts = (pl.ds(0, 128), pl.ds(128, TILE - 128))
    rs_pair, rs_over, rs_edge, outward = {}, {}, {}, {}
    for s in range(2):
        for k in range(2):
            rs_pair[s, k] = remote(rs_send.at[s, k], rs_got.at[s, k], r_send.at[k, s], r_recv.at[k, s], to_sibling)
        for k in range(2):
            rs_over[s, k] = remote(
                rs_cross.at[s, :, :, parts[k]],
                rs_cross_got.at[s, :, :, parts[k]],
                r_send.at[2 + k, s],
                r_recv.at[2 + k, s],
                to_across,
            )
        rs_edge[s, 0] = remote(edge_send.at[s, 0], edge_got.at[s, 0], e_send.at[0, s], e_recv.at[0, s], to_right)
        rs_edge[s, 1] = remote(edge_send.at[s, 1], edge_got.at[s, 1], e_send.at[1, s], e_recv.at[1, s], to_left)
        for p in range(2):
            outward[s, p] = pltpu.make_async_copy(own.at[s, p], (out_re, out_im)[p].at[0, s], out_sem.at[s, p])

    def reduce_1(s):
        place(s, 1)
        for k, who in enumerate((diagonal, sibling)):
            for p in range(2):
                rs_send[s, k, p] = piece(s, p, who)
            rs_pair[s, k].start()

    def reduce_2(s):
        rs_pair[s, 0].wait_recv()
        for p in range(2):
            rs_cross[s, p] = piece(s, p, across) + rs_got[s, 0, p]
        rs_over[s, 0].start()
        rs_pair[s, 1].wait_recv()
        for p in range(2):
            own[s, p] = piece(s, p, m) + rs_got[s, 1, p]

    lane = lax.broadcasted_iota(jnp.int32, (ROWS, 128), 1)
    lower = lane < MARGIN

    def reduce_3(s):
        rs_over[s, 0].wait_recv()
        ends = [own[s, p, :, :128] + rs_cross_got[s, p, :, :128] for p in range(2)]
        for p in range(2):
            own[s, p, :, :128] = ends[p]
        edge_send[s, 0] = jnp.where(lower, pltpu.roll(ends[0], MARGIN, 1), ends[1])
        edge_send[s, 1] = jnp.where(lower, ends[0], pltpu.roll(ends[1], MARGIN, 1))
        rs_edge[s, 0].start()
        rs_edge[s, 1].start()

    def reduce_4(s):
        rs_edge[s, 0].wait_recv()
        rs_edge[s, 1].wait_recv()
        before, after = edge_got[s, 0], edge_got[s, 1]
        at_first = jnp.logical_and(lower, t > 0)
        at_last = jnp.logical_and(jnp.logical_not(lower), t < tiles - 1)
        befores = (before, pltpu.roll(before, MARGIN, 1))
        afters = (pltpu.roll(after, MARGIN, 1), after)
        rs_over[s, 1].wait_recv()
        for p in range(2):
            ends = own[s, p, :, :128] + jnp.where(at_first, befores[p], 0.0) + jnp.where(at_last, afters[p], 0.0)
            between = own[s, p, :, 256:] + rs_cross_got[s, p, :, 256:]
            own[s, p, :, 128:256] += rs_cross_got[s, p, :, 128:256]
            own[s, p, :, :128] = jnp.where(lower, ends, between)
            own[s, p, :, 256:] = jnp.where(lower, between, ends)
            outward[s, p].start()

    axes = (((tz, z_peers), (tx, x_peers)), ((tx, x_peers), (tz, z_peers)))

    def block(length, index, base=0):
        return pl.ds(pl.multiple_of(base + index * length, length), length)

    scatter_a, scatter_b, swap_y, gather_b, gather_a, probe_out = {}, {}, {}, {}, {}, {}
    chunks = [(c, h) for h in range(2) for c in range(2)]
    for c, h in chunks:
        (ia, peers_a), (ib, peers_b) = axes[c]
        for k in range(ring - 1):
            ja, jb = lax.rem(ia + k + 1, ring), lax.rem(ib + k + 1, ring)
            sems = [(p_send.at[c, h, i, k], p_recv.at[c, h, i, k]) for i in range(4)]
            scatter_a[c, h, k] = remote(
                partial.at[c, :, block(32, ja, h * HALF)], got_a.at[c, h, k], *sems[0], peers_a[k]
            )
            scatter_b[c, h, k] = remote(part_b.at[c, h, :, block(8, jb)], got_b.at[c, h, k], *sems[1], peers_b[k])
            mine_b = total.at[:, c, block(8, ib, h * HALF + ia * 32)]
            gather_b[c, h, k] = remote(mine_b, mine_b, *sems[2], peers_b[k])
            mine_a = total.at[:, c, block(32, ia, h * HALF)]
            gather_a[c, h, k] = remote(mine_a, mine_a, *sems[3], peers_a[k])
        swap_y[c, h] = remote(y_send_buf.at[c, h], y_got.at[c, h], p_send.at[c, h, 4, 0], p_recv.at[c, h, 4, 0], y_peer)
        some = pl.ds(h * HALF, HALF)
        probe_out[c, h] = pltpu.make_async_copy(total.at[:, c, some], out_probe.at[:, c, some], probe_sem.at[c, h])

    def send_all(group, c, h):
        for k in (1, 0, 2):
            group[c, h, k].start()

    def take_all(group, c, h):
        for k in range(3):
            group[c, h, k].wait_recv()

    def probe_1(c):
        for h in range(2):
            send_all(scatter_a, c, h)

    def probe_2(c, h):
        ia = axes[c][0][0]
        take_all(scatter_a, c, h)
        got = got_a[c, h, 0] + got_a[c, h, 1] + got_a[c, h, 2]
        part_b[c, h] = partial[c, :, block(32, ia, h * HALF), :] + got
        send_all(scatter_b, c, h)

    def probe_3(c, h):
        ib = axes[c][1][0]
        take_all(scatter_b, c, h)
        got = got_b[c, h, 0] + got_b[c, h, 1] + got_b[c, h, 2]
        y_send_buf[c, h] = part_b[c, h, :, block(8, ib), :] + got
        swap_y[c, h].start()

    def probe_4(c, h):
        ia, ib = axes[c][0][0], axes[c][1][0]
        swap_y[c, h].wait_recv()
        total[:, c, block(8, ib, h * HALF + ia * 32), :] = y_send_buf[c, h] + y_got[c, h]
        send_all(gather_b, c, h)

    def probe_5(c, h):
        take_all(gather_b, c, h)
        send_all(gather_a, c, h)

    def probe_6(c, h):
        take_all(gather_a, c, h)
        probe_out[c, h].start()

    def each(step, h):
        for c in range(2):
            step(c, h)

    to_share[0].wait_recv()
    over([(0, 0)], both_steps)
    factors(1)
    over([(0, 1)], both_steps)
    place(1, 0)
    place(0, 0)
    to_share[1].wait_recv()
    over([(1, 0)], both_steps)
    probe_1(0)
    over([(1, 1)], both_steps)
    probe_1(1)
    reduce_1(1)
    reduce_1(0)
    reduce_2(1)
    reduce_2(0)
    each(probe_2, 0)
    each(probe_2, 1)
    each(probe_3, 0)
    reduce_3(1)
    each(probe_3, 1)
    rs_over[1, 1].start()
    rs_over[0, 1].start()
    each(probe_4, 0)
    reduce_3(0)
    each(probe_4, 1)
    each(probe_5, 0)
    each(probe_5, 1)
    reduce_4(1)
    each(probe_6, 0)
    reduce_4(0)
    each(probe_6, 1)

    for group in (probe_out, outward):
        for copy in group.values():
            copy.wait()
    for group in (scatter_a, scatter_b, swap_y, gather_b, gather_a):
        for copy in group.values():
            copy.wait_send()
    for group in (sends, crosses, relays, rs_pair, rs_over, rs_edge):
        for copy in group.values():
            copy.wait_send()
    for group in (to_pair, to_other, to_share):
        for copy in group:
            copy.wait_send()


def gradients(obj_re, obj_im, probe, measured, positions, table, orders):
    tiles = lax.axis_size("tile")
    shape = jax.ShapeDtypeStruct
    anywhere = pl.BlockSpec(memory_space=pl.ANY)
    return pl.pallas_call(
        functools.partial(kernel, tiles),
        out_shape=(shape(obj_re.shape, F32), shape(obj_im.shape, F32), shape(probe.shape, F32)),
        in_specs=[anywhere, anywhere, anywhere, anywhere, pl.BlockSpec(memory_space=pltpu.SMEM), anywhere, anywhere],
        out_specs=(anywhere, anywhere, anywhere),
        scratch_shapes=[
            pltpu.VMEM((2, TILE, TILE), F32),
            pltpu.VMEM((2, TILE, TILE), F32),
            pltpu.VMEM((2, 2, 2, PX, PX), F32),
            pltpu.VMEM((2, 2, PX, PX), F32),
            pltpu.VMEM((2, PX, PX), F32),
            pltpu.VMEM(table.shape, BF16),
            pltpu.VMEM(orders.shape, BF16),
            pltpu.VMEM((2, 2, 2, PX, PX), F32),
            pltpu.VMEM((2, 2, 2, PX, PX), F32),
            pltpu.VMEM((2, PX, PX), F32),
            pltpu.VMEM((2, HALF, PX), F32),
            pltpu.VMEM((2, HALF, PX), F32),
            pltpu.VMEM((2, HALF, PX), F32),
            pltpu.VMEM((2, PX, PX), F32),
            pltpu.VMEM((2, 2, 2, PX, PX), F32),
            pltpu.VMEM((2, 2, TILE, TILE), F32),
            pltpu.VMEM((2, 2, 2, ROWS, TILE), F32),
            pltpu.VMEM((2, 2, 2, ROWS, TILE), F32),
            pltpu.VMEM((2, 2, ROWS, TILE), F32),
            pltpu.VMEM((2, 2, ROWS, TILE), F32),
            pltpu.VMEM((2, 2, ROWS, TILE), F32),
            pltpu.VMEM((2, 2, ROWS, 128), F32),
            pltpu.VMEM((2, 2, ROWS, 128), F32),
            pltpu.SemaphoreType.DMA((4,)),
            pltpu.SemaphoreType.DMA((2, 2)),
            pltpu.SemaphoreType.DMA((3, 2, 2)),
            pltpu.SemaphoreType.DMA((3, 2, 2)),
            pltpu.SemaphoreType.DMA((3, 2)),
            pltpu.SemaphoreType.DMA((3, 2)),
            pltpu.SemaphoreType.DMA((5, 2)),
            pltpu.SemaphoreType.DMA((5, 2)),
            pltpu.SemaphoreType.DMA((2, 2)),
            pltpu.SemaphoreType.DMA((2, 2)),
            pltpu.VMEM((2, 2, PX, PX), F32),
            pltpu.VMEM((2, 2, 3, 2, 32, PX), F32),
            pltpu.VMEM((2, 2, 3, 2, 8, PX), F32),
            pltpu.VMEM((2, 2, 2, 32, PX), F32),
            pltpu.VMEM((2, 2, 2, 8, PX), F32),
            pltpu.VMEM((2, 2, 2, 8, PX), F32),
            pltpu.SemaphoreType.DMA((2, 2, 5, 3)),
            pltpu.SemaphoreType.DMA((2, 2, 5, 3)),
            pltpu.VMEM((2, 2, PX, PX), F32),
            pltpu.SemaphoreType.DMA((2, 2)),
            pltpu.SemaphoreType.DMA((2, 2)),
        ],
        compiler_params=pltpu.CompilerParams(
            collective_id=0, has_side_effects=True, vmem_limit_bytes=56 * 1024 * 1024
        ),
        cost_estimate=pl.CostEstimate(flops=7 * 10**9, bytes_accessed=10**7, transcendentals=10**6),
    )(obj_re, obj_im, probe, measured, positions, table, orders)


def deliver_kernel(count, *refs):
    sources, targets, held = refs[:count], refs[count : 2 * count], refs[2 * count : 3 * count]
    in_sem, out_sem = refs[3 * count :]
    inward, outward = [], []
    for i in range(count):
        for k in range(2):
            at = (slice(None), k)
            inward.append(pltpu.make_async_copy(sources[i].at[at], held[i].at[at], in_sem.at[i, k]))
            outward.append(pltpu.make_async_copy(held[i].at[at], targets[i].at[at], out_sem.at[i, k]))
    for copy in inward:
        copy.start()
    for copy, onward in zip(inward, outward):
        copy.wait()
        onward.start()
    for copy in outward:
        copy.wait()


def delivered(arrays):
    anywhere = pl.BlockSpec(memory_space=pl.ANY)
    count = len(arrays)
    return pl.pallas_call(
        functools.partial(deliver_kernel, count),
        out_shape=tuple(jax.ShapeDtypeStruct(a.shape, a.dtype) for a in arrays),
        in_specs=[anywhere] * count,
        out_specs=(anywhere,) * count,
        scratch_shapes=[pltpu.VMEM(a.shape, a.dtype) for a in arrays]
        + [pltpu.SemaphoreType.DMA((count, 2)), pltpu.SemaphoreType.DMA((count, 2))],
        compiler_params=pltpu.CompilerParams(vmem_limit_bytes=56 * 1024 * 1024),
    )(*arrays)


def body(object_real, object_imag, probe, measured, positions):
    table, orders = constants()
    return delivered(
        gradients(object_real, object_imag, probe, measured, positions, jnp.asarray(table), jnp.asarray(orders))
    )


def solution(mesh):
    return jax.shard_map(
        body,
        mesh=mesh,
        in_specs=(
            P("tile", None, "mode", None),
            P("tile", None, "mode", None),
            P(None, "mode", None, None),
            P("tile", None, None, None),
            P("tile", None, None),
        ),
        out_specs=(
            P("tile", None, "mode", None),
            P("tile", None, "mode", None),
            P(None, "mode", None, None),
        ),
        check_vma=False,
    )
```

```python
import functools
import math

import jax
import jax.numpy as jnp
import ml_dtypes
import numpy as np
from jax import lax
from jax.experimental import pallas as pl
from jax.experimental.pallas import tpu as pltpu
from jax.sharding import PartitionSpec as P

PX = 256
HALF = PX // 2
TILE = 384
MARGIN = 64
ROWS = 96
EDGE = TILE - PX
FLOOR = 0.1
FRESNEL = 40.0
MESH = pl.DeviceIdType.MESH
F32 = jnp.float32
BF16 = jnp.bfloat16

A_LEFT, A_RIGHT, F_LEFT, F_RIGHT, B_LEFT, B_RIGHT = range(6)


def real_form(c):
    return np.block([[c.real, -c.imag], [c.imag, c.real]])


@functools.cache
def constants():
    index = np.arange(PX)
    fourier = np.exp(-2j * np.pi * (np.outer(index, index) % PX) / PX) / math.sqrt(PX)
    freq = ((index + HALF) % PX - HALF) / PX
    chirp = np.exp(-1j * np.pi * FRESNEL * freq**2)
    through = fourier.conj() @ (chirp[:, None] * fourier)
    near, far = through[:HALF, :HALF], through[:HALF, HALF:]
    pairs = [None] * 6
    moved = [(near + far) / 2, (near - far) / 2]
    split = [fourier[0::2, :HALF], fourier[1::2, :HALF]]
    pairs[A_LEFT] = [real_form(c) for c in moved]
    pairs[A_RIGHT] = [real_form(c).T for c in moved]
    pairs[F_LEFT] = [real_form(c) for c in split]
    pairs[F_RIGHT] = [real_form(c).T for c in split]
    pairs[B_LEFT] = [real_form(c.T) for c in split]
    pairs[B_RIGHT] = [real_form(c.T).T for c in split]
    table = np.array(pairs).reshape(12, PX, PX)
    high = table.astype(ml_dtypes.bfloat16)
    low = (table - high.astype(np.float64)).astype(ml_dtypes.bfloat16)
    order = np.zeros((PX, PX))
    order[np.arange(HALF), np.arange(0, PX, 2)] = 1
    order[np.arange(HALF) + HALF, np.arange(1, PX, 2)] = 1
    orders = np.array([order, order.T]).astype(ml_dtypes.bfloat16)
    return np.stack([high, low], axis=1), orders


def two_parts(x):
    high = x.astype(BF16)
    return high, (x - high.astype(F32)).astype(BF16)


def product(a, b):
    return jnp.dot(a, b, preferred_element_type=F32)


def apply_left(table, kind, sign, z):
    high, low = two_parts(z)
    c_high, c_low = table[2 * kind + sign, 0], table[2 * kind + sign, 1]
    return product(
        jnp.concatenate([c_high, c_low, c_high], axis=1),
        jnp.concatenate([high, high, low], axis=0),
    )


def apply_right(table, kind, sign, z):
    high, low = two_parts(z)
    c_high, c_low = table[2 * kind + sign, 0], table[2 * kind + sign, 1]
    return product(
        jnp.concatenate([high, high, low], axis=1),
        jnp.concatenate([c_high, c_low, c_high], axis=0),
    )


def rows_first(x):
    return x[:HALF], x[HALF:]


def lanes_first(x):
    return x[:, :HALF], x[:, HALF:]


def one_side(table, kind, re, im, left):
    halves, axis, apply = (rows_first, 0, apply_left) if left else (lanes_first, 1, apply_right)
    (r0, r1), (i0, i1) = halves(re), halves(im)
    if kind[0] != B_LEFT:
        r0, r1, i0, i1 = r0 + r1, r0 - r1, i0 + i1, i0 - i1
    which = kind[0] if left else kind[1]
    plus = apply(table, which, 0, jnp.concatenate([r0, i0], axis=axis))
    minus = apply(table, which, 1, jnp.concatenate([r1, i1], axis=axis))
    (pr, pi), (mr, mi) = halves(plus), halves(minus)
    if kind[0] != F_LEFT:
        pr, mr, pi, mi = pr + mr, pr - mr, pi + mi, pi - mi
    return jnp.concatenate([pr, mr], axis=axis), jnp.concatenate([pi, mi], axis=axis)


def both_sides(table, kind, re, im):
    re, im = one_side(table, kind, re, im, True)
    return one_side(table, kind, re, im, False)


THROUGH = (A_LEFT, A_RIGHT)
FORTH = (F_LEFT, F_RIGHT)
BACK = (B_LEFT, B_RIGHT)


def times(ar, ai, br, bi):
    return ar * br - ai * bi, ar * bi + ai * br


def kernel(
    tiles,
    obj_re,
    obj_im,
    probe_in,
    measured_in,
    positions,
    table_in,
    orders_in,
    out_re,
    out_im,
    out_probe,
    tile0,
    tile1,
    crops,
    probe,
    measured,
    table,
    orders,
    wave1,
    far,
    ipart,
    isib,
    isum,
    icross,
    factor,
    crop_grad,
    tile_grad,
    rs_got,
    rs_cross,
    rs_cross_got,
    own,
    edge_send,
    edge_got,
    local_sem,
    tile_local,
    g_send,
    g_recv,
    i_send,
    i_recv,
    r_send,
    r_recv,
    e_send,
    e_recv,
    partial,
    got_a,
    got_b,
    part_b,
    y_send_buf,
    y_got,
    p_send,
    p_recv,
    total,
    out_sem,
    probe_sem,
):
    t = lax.axis_index("tile")
    m = lax.axis_index("mode")
    core = lax.rem(m, 2)
    high = m // 2
    sibling = high * 2 + (1 - core)
    across = (1 - high) * 2 + core
    diagonal = (1 - high) * 2 + (1 - core)
    left = lax.rem(t + tiles - 1, tiles)
    right = lax.rem(t + 1, tiles)
    to_sibling, to_across = (t, sibling), (t, across)
    to_left, to_right = (left, m), (right, m)

    ring = 4
    tz, ty, tx = lax.rem(t, ring), lax.rem(t // ring, 2), t // (2 * ring)
    z_peers = [(t - tz + lax.rem(tz + d, ring), m) for d in range(1, ring)]
    x_peers = [(lax.rem(t + 2 * ring * d, tiles), m) for d in range(1, ring)]
    y_peer = (t + ring * (1 - 2 * ty), m)

    barrier = pltpu.get_barrier_semaphore()
    for device in (to_sibling, to_across, to_left, to_right, y_peer, *z_peers, *x_peers):
        pl.semaphore_signal(barrier, inc=1, device_id=device, device_id_type=MESH)

    loads = [
        pltpu.make_async_copy(probe_in, probe, local_sem.at[0]),
        pltpu.make_async_copy(measured_in.at[0], measured, local_sem.at[1]),
        pltpu.make_async_copy(table_in, table, local_sem.at[2]),
        pltpu.make_async_copy(orders_in, orders, local_sem.at[3]),
    ]
    for load in loads:
        load.start()

    whole = (tile0, tile1)
    objects = (obj_re, obj_im)

    def my_rows(who):
        return pl.ds(pl.multiple_of(who * ROWS, ROWS), ROWS)

    def remote(src, dst, send, recv, device):
        return pltpu.make_async_remote_copy(
            src_ref=src, dst_ref=dst, send_sem=send, recv_sem=recv, device_id=device, device_id_type=MESH
        )

    own_copies, sends, crosses, relays = {}, {}, {}, {}
    for s in range(2):
        for p in range(2):
            src = objects[p].at[0, s]
            dst = whole[s].at[p, my_rows(m)]
            own_copies[s, p] = pltpu.make_async_copy(src, dst, tile_local.at[s, p])
            crosses[s, p] = remote(src, dst, g_send.at[0, s, p], g_recv.at[0, s, p], to_across)
            sends[s, p] = remote(src, dst, g_send.at[1, s, p], g_recv.at[1, s, p], to_sibling)
            got = whole[s].at[p, my_rows(across)]
            relays[s, p] = remote(got, got, g_send.at[2, s, p], g_recv.at[2, s, p], to_sibling)

    pl.semaphore_wait(barrier, 11)
    for s in range(2):
        for p in range(2):
            crosses[s, p].start()
    for s in range(2):
        for p in range(2):
            own_copies[s, p].start()
            sends[s, p].start()

    crop_grad[...] = jnp.zeros_like(crop_grad)
    partial[...] = jnp.zeros_like(partial)
    for load in loads:
        load.wait()
    for f in range(2):
        m_high, m_low = two_parts(measured[f])
        mixed = product(orders[0], m_high) + product(orders[0], m_low)
        m_high, m_low = two_parts(mixed)
        measured[f] = product(m_high, orders[1]) + product(m_low, orders[1])

    def tile_ready(s):
        for p in range(2):
            crosses[s, p].wait_recv()
            relays[s, p].start()
        for p in range(2):
            own_copies[s, p].wait()
            sends[s, p].wait_recv()
        for p in range(2):
            relays[s, p].wait_recv()

    row = [positions[0, f, 0] for f in range(2)]
    col = [positions[0, f, 1] for f in range(2)]

    def take_crops(s, frames=(0, 1)):
        for f in frames:
            up, back = lax.rem(TILE - row[f], TILE), lax.rem(TILE - col[f], TILE)
            for p in range(2):
                lines = pltpu.roll(whole[s][p], up, 0)[:PX]
                crops[f, s, p] = pltpu.roll(lines, back, 1)[:, :PX]

    tile_ready(0)
    take_crops(0)

    def pass_through(step, carry):
        f, mode = step // 2, lax.rem(step, 2)
        re, im = times(probe[0, mode], probe[1, mode], crops[f, 0, 0], crops[f, 0, 1])
        re, im = both_sides(table, THROUGH, re, im)
        wave1[f, mode, 0] = re
        wave1[f, mode, 1] = im
        return carry

    lax.fori_loop(0, 4, pass_through, 0, unroll=2)
    tile_ready(1)
    take_crops(1, (0,))

    def far_fields(f):
        ipart[f] = jnp.zeros_like(ipart[f])

        def step(mode, carry):
            re, im = times(wave1[f, mode, 0], wave1[f, mode, 1], crops[f, 1, 0], crops[f, 1, 1])
            re, im = both_sides(table, FORTH, re, im)
            far[f, mode, 0] = re
            far[f, mode, 1] = im
            ipart[f] += re * re + im * im
            return carry

        lax.fori_loop(0, 2, step, 0, unroll=True)

    def half_rows(who):
        return pl.ds(pl.multiple_of(who * HALF, HALF), HALF)

    to_pair = [
        remote(ipart.at[f, half_rows(1 - core)], isib.at[f], i_send.at[0, f], i_recv.at[0, f], to_sibling) for f in range(2)
    ]
    to_other = [remote(isum.at[f], icross.at[f], i_send.at[1, f], i_recv.at[1, f], to_across) for f in range(2)]
    to_share = [
        remote(
            factor.at[f, half_rows(core)],
            factor.at[f, half_rows(core)],
            i_send.at[2, f],
            i_recv.at[2, f],
            to_sibling,
        )
        for f in range(2)
    ]

    def pair_sum(f):
        to_pair[f].wait_recv()
        isum[f] = ipart[f, half_rows(core), :] + isib[f]
        to_other[f].start()

    def factors(f):
        to_other[f].wait_recv()
        whole_sum = isum[f] + icross[f]
        factor[f, half_rows(core), :] = 2.0 - 2.0 * measured[f, half_rows(core), :] / jnp.sqrt(whole_sum + FLOOR)
        to_share[f].start()

    far_fields(0)
    to_pair[0].start()
    take_crops(1, (1,))
    far_fields(1)
    to_pair[1].start()
    pair_sum(0)
    pair_sum(1)
    factors(0)

    def over(steps, body):
        def step(k, carry):
            f, mode = steps[0]
            if len(steps) > 1:
                f = f + k * (steps[1][0] - f)
                mode = mode + k * (steps[1][1] - mode)
            body(f, mode)
            return carry

        lax.fori_loop(0, len(steps), step, 0)

    def slice_1_step(f, mode):
        weight = factor[f]
        re, im = weight * far[f, mode, 0], -(weight * far[f, mode, 1])
        re, im = both_sides(table, BACK, re, im)
        gr, gi = times(wave1[f, mode, 0], wave1[f, mode, 1], re, im)
        crop_grad[f, 1, 0] += gr
        crop_grad[f, 1, 1] -= gi
        re, im = times(crops[f, 1, 0], crops[f, 1, 1], re, im)
        far[f, mode, 0] = re
        far[f, mode, 1] = im

    def probe_step(f, mode):
        re, im = both_sides(table, THROUGH, far[f, mode, 0], far[f, mode, 1])
        gr, gi = times(probe[0, mode], probe[1, mode], re, im)
        crop_grad[f, 0, 0] += gr
        crop_grad[f, 0, 1] -= gi
        gr, gi = times(crops[f, 0, 0], crops[f, 0, 1], re, im)
        partial[mode, 0] += gr
        partial[mode, 1] -= gi

    def both_steps(f, mode):
        slice_1_step(f, mode)
        probe_step(f, mode)

    low_lanes = lax.broadcasted_iota(jnp.int32, (TILE, 128), 1) < MARGIN

    def place(s, f):
        for p in range(2):
            wide = jnp.concatenate([crop_grad[f, s, p], jnp.zeros((PX, EDGE), F32)], axis=1)
            wide = pltpu.roll(wide, col[f], 1)
            wide = jnp.concatenate([wide, jnp.zeros((EDGE, TILE), F32)], axis=0)
            wide = pltpu.roll(wide, row[f], 0)
            first, middle, last = wide[:, :128], wide[:, 128:256], wide[:, 256:]
            ends, between = jnp.where(low_lanes, first, last), jnp.where(low_lanes, last, first)
            blocks = jnp.concatenate([ends, middle, between], axis=1)
            tile_grad[s, p] = blocks if f == 0 else tile_grad[s, p] + blocks

    def piece(s, p, who):
        return tile_grad[s, p, my_rows(who), :]

    parts = (pl.ds(0, 128), pl.ds(128, TILE - 128))
    rs_pair, rs_over, rs_edge, outward = {}, {}, {}, {}
    for s in range(2):
        for k, who in enumerate((diagonal, sibling)):
            lines = tile_grad.at[s, :, my_rows(who)]
            rs_pair[s, k] = remote(lines, rs_got.at[s, k], r_send.at[k, s], r_recv.at[k, s], to_sibling)
        for k in range(2):
            rs_over[s, k] = remote(
                rs_cross.at[s, :, :, parts[k]],
                rs_cross_got.at[s, :, :, parts[k]],
                r_send.at[2 + k, s],
                r_recv.at[2 + k, s],
                to_across,
            )
        rs_edge[s, 0] = remote(edge_send.at[s, 0], edge_got.at[s, 0], e_send.at[0, s], e_recv.at[0, s], to_right)
        rs_edge[s, 1] = remote(edge_send.at[s, 1], edge_got.at[s, 1], e_send.at[1, s], e_recv.at[1, s], to_left)
        for p in range(2):
            outward[s, p] = pltpu.make_async_copy(own.at[s, p], (out_re, out_im)[p].at[0, s], out_sem.at[s, p])

    def reduce_1(s):
        place(s, 1)
        for k in range(2):
            rs_pair[s, k].start()

    def reduce_2(s):
        rs_pair[s, 0].wait_recv()
        for p in range(2):
            rs_cross[s, p] = piece(s, p, across) + rs_got[s, 0, p]
        rs_over[s, 0].start()

    def reduce_own(s):
        rs_pair[s, 1].wait_recv()
        for p in range(2):
            own[s, p] = piece(s, p, m) + rs_got[s, 1, p]

    lane = lax.broadcasted_iota(jnp.int32, (ROWS, 128), 1)
    lower = lane < MARGIN

    def reduce_3(s):
        rs_over[s, 0].wait_recv()
        ends = [own[s, p, :, :128] + rs_cross_got[s, p, :, :128] for p in range(2)]
        for p in range(2):
            own[s, p, :, :128] = ends[p]
        edge_send[s, 0] = jnp.where(lower, pltpu.roll(ends[0], MARGIN, 1), ends[1])
        edge_send[s, 1] = jnp.where(lower, ends[0], pltpu.roll(ends[1], MARGIN, 1))
        rs_edge[s, 0].start()
        rs_edge[s, 1].start()

    def reduce_4(s):
        rs_edge[s, 0].wait_recv()
        rs_edge[s, 1].wait_recv()
        before, after = edge_got[s, 0], edge_got[s, 1]
        at_first = jnp.logical_and(lower, t > 0)
        at_last = jnp.logical_and(jnp.logical_not(lower), t < tiles - 1)
        befores = (before, pltpu.roll(before, MARGIN, 1))
        afters = (pltpu.roll(after, MARGIN, 1), after)
        rs_over[s, 1].wait_recv()
        for p in range(2):
            ends = own[s, p, :, :128] + jnp.where(at_first, befores[p], 0.0) + jnp.where(at_last, afters[p], 0.0)
            between = own[s, p, :, 256:] + rs_cross_got[s, p, :, 256:]
            own[s, p, :, 128:256] += rs_cross_got[s, p, :, 128:256]
            own[s, p, :, :128] = jnp.where(lower, ends, between)
            own[s, p, :, 256:] = jnp.where(lower, between, ends)
            outward[s, p].start()

    axes = (((tz, z_peers), (tx, x_peers)), ((tx, x_peers), (tz, z_peers)))

    def block(length, index, base=0):
        return pl.ds(pl.multiple_of(base + index * length, length), length)

    scatter_a, scatter_b, swap_y, gather_b, gather_a, probe_out = {}, {}, {}, {}, {}, {}
    chunks = [(c, h) for h in range(2) for c in range(2)]
    for c, h in chunks:
        (ia, peers_a), (ib, peers_b) = axes[c]
        for k in range(ring - 1):
            ja, jb = lax.rem(ia + k + 1, ring), lax.rem(ib + k + 1, ring)
            sems = [(p_send.at[c, h, i, k], p_recv.at[c, h, i, k]) for i in range(4)]
            scatter_a[c, h, k] = remote(
                partial.at[c, :, block(32, ja, h * HALF)], got_a.at[c, h, k], *sems[0], peers_a[k]
            )
            scatter_b[c, h, k] = remote(part_b.at[c, h, :, block(8, jb)], got_b.at[c, h, k], *sems[1], peers_b[k])
            mine_b = total.at[:, c, block(8, ib, h * HALF + ia * 32)]
            gather_b[c, h, k] = remote(mine_b, mine_b, *sems[2], peers_b[k])
            mine_a = total.at[:, c, block(32, ia, h * HALF)]
            gather_a[c, h, k] = remote(mine_a, mine_a, *sems[3], peers_a[k])
        swap_y[c, h] = remote(y_send_buf.at[c, h], y_got.at[c, h], p_send.at[c, h, 4, 0], p_recv.at[c, h, 4, 0], y_peer)
        some = pl.ds(h * HALF, HALF)
        probe_out[c, h] = pltpu.make_async_copy(total.at[:, c, some], out_probe.at[:, c, some], probe_sem.at[c, h])

    def send_all(group, c, h):
        for k in (1, 0, 2):
            group[c, h, k].start()

    def take_all(group, c, h):
        for k in range(3):
            group[c, h, k].wait_recv()

    def probe_1(c):
        for h in range(2):
            send_all(scatter_a, c, h)

    def probe_2(c, h):
        ia = axes[c][0][0]
        take_all(scatter_a, c, h)
        got = got_a[c, h, 0] + got_a[c, h, 1] + got_a[c, h, 2]
        part_b[c, h] = partial[c, :, block(32, ia, h * HALF), :] + got
        send_all(scatter_b, c, h)

    def probe_3(c, h):
        ib = axes[c][1][0]
        take_all(scatter_b, c, h)
        got = got_b[c, h, 0] + got_b[c, h, 1] + got_b[c, h, 2]
        y_send_buf[c, h] = part_b[c, h, :, block(8, ib), :] + got
        swap_y[c, h].start()

    def probe_4(c, h):
        ia, ib = axes[c][0][0], axes[c][1][0]
        swap_y[c, h].wait_recv()
        total[:, c, block(8, ib, h * HALF + ia * 32), :] = y_send_buf[c, h] + y_got[c, h]
        send_all(gather_b, c, h)

    def probe_5(c, h):
        take_all(gather_b, c, h)
        send_all(gather_a, c, h)

    def probe_6(c, h):
        take_all(gather_a, c, h)
        probe_out[c, h].start()

    def each(step, h):
        for c in range(2):
            step(c, h)

    to_share[0].wait_recv()
    over([(0, 0)], both_steps)
    factors(1)
    over([(0, 1)], both_steps)
    place(1, 0)
    place(0, 0)
    to_share[1].wait_recv()
    over([(1, 0)], both_steps)
    probe_1(0)
    over([(1, 1)], both_steps)
    probe_1(1)
    reduce_1(1)
    reduce_1(0)
    reduce_2(1)
    reduce_2(0)
    each(probe_2, 0)
    each(probe_2, 1)
    reduce_own(1)
    each(probe_3, 0)
    reduce_own(0)
    reduce_3(1)
    each(probe_3, 1)
    rs_over[1, 1].start()
    rs_over[0, 1].start()
    each(probe_4, 0)
    reduce_3(0)
    each(probe_4, 1)
    each(probe_5, 0)
    each(probe_5, 1)
    reduce_4(1)
    each(probe_6, 0)
    reduce_4(0)
    each(probe_6, 1)

    for group in (probe_out, outward):
        for copy in group.values():
            copy.wait()
    for group in (scatter_a, scatter_b, swap_y, gather_b, gather_a):
        for copy in group.values():
            copy.wait_send()
    for group in (sends, crosses, relays, rs_pair, rs_over, rs_edge):
        for copy in group.values():
            copy.wait_send()
    for group in (to_pair, to_other, to_share):
        for copy in group:
            copy.wait_send()


def gradients(obj_re, obj_im, probe, measured, positions, table, orders):
    tiles = lax.axis_size("tile")
    shape = jax.ShapeDtypeStruct
    anywhere = pl.BlockSpec(memory_space=pl.ANY)
    return pl.pallas_call(
        functools.partial(kernel, tiles),
        out_shape=(shape(obj_re.shape, F32), shape(obj_im.shape, F32), shape(probe.shape, F32)),
        in_specs=[anywhere, anywhere, anywhere, anywhere, pl.BlockSpec(memory_space=pltpu.SMEM), anywhere, anywhere],
        out_specs=(anywhere, anywhere, anywhere),
        scratch_shapes=[
            pltpu.VMEM((2, TILE, TILE), F32),
            pltpu.VMEM((2, TILE, TILE), F32),
            pltpu.VMEM((2, 2, 2, PX, PX), F32),
            pltpu.VMEM((2, 2, PX, PX), F32),
            pltpu.VMEM((2, PX, PX), F32),
            pltpu.VMEM(table.shape, BF16),
            pltpu.VMEM(orders.shape, BF16),
            pltpu.VMEM((2, 2, 2, PX, PX), F32),
            pltpu.VMEM((2, 2, 2, PX, PX), F32),
            pltpu.VMEM((2, PX, PX), F32),
            pltpu.VMEM((2, HALF, PX), F32),
            pltpu.VMEM((2, HALF, PX), F32),
            pltpu.VMEM((2, HALF, PX), F32),
            pltpu.VMEM((2, PX, PX), F32),
            pltpu.VMEM((2, 2, 2, PX, PX), F32),
            pltpu.VMEM((2, 2, TILE, TILE), F32),
            pltpu.VMEM((2, 2, 2, ROWS, TILE), F32),
            pltpu.VMEM((2, 2, ROWS, TILE), F32),
            pltpu.VMEM((2, 2, ROWS, TILE), F32),
            pltpu.VMEM((2, 2, ROWS, TILE), F32),
            pltpu.VMEM((2, 2, ROWS, 128), F32),
            pltpu.VMEM((2, 2, ROWS, 128), F32),
            pltpu.SemaphoreType.DMA((4,)),
            pltpu.SemaphoreType.DMA((2, 2)),
            pltpu.SemaphoreType.DMA((3, 2, 2)),
            pltpu.SemaphoreType.DMA((3, 2, 2)),
            pltpu.SemaphoreType.DMA((3, 2)),
            pltpu.SemaphoreType.DMA((3, 2)),
            pltpu.SemaphoreType.DMA((5, 2)),
            pltpu.SemaphoreType.DMA((5, 2)),
            pltpu.SemaphoreType.DMA((2, 2)),
            pltpu.SemaphoreType.DMA((2, 2)),
            pltpu.VMEM((2, 2, PX, PX), F32),
            pltpu.VMEM((2, 2, 3, 2, 32, PX), F32),
            pltpu.VMEM((2, 2, 3, 2, 8, PX), F32),
            pltpu.VMEM((2, 2, 2, 32, PX), F32),
            pltpu.VMEM((2, 2, 2, 8, PX), F32),
            pltpu.VMEM((2, 2, 2, 8, PX), F32),
            pltpu.SemaphoreType.DMA((2, 2, 5, 3)),
            pltpu.SemaphoreType.DMA((2, 2, 5, 3)),
            pltpu.VMEM((2, 2, PX, PX), F32),
            pltpu.SemaphoreType.DMA((2, 2)),
            pltpu.SemaphoreType.DMA((2, 2)),
        ],
        compiler_params=pltpu.CompilerParams(
            collective_id=0, has_side_effects=True, vmem_limit_bytes=56 * 1024 * 1024
        ),
        cost_estimate=pl.CostEstimate(flops=7 * 10**9, bytes_accessed=10**7, transcendentals=10**6),
    )(obj_re, obj_im, probe, measured, positions, table, orders)


def deliver_kernel(count, *refs):
    sources, targets, held = refs[:count], refs[count : 2 * count], refs[2 * count : 3 * count]
    in_sem, out_sem = refs[3 * count :]
    inward, outward = [], []
    for i in range(count):
        for k in range(2):
            at = (slice(None), k)
            inward.append(pltpu.make_async_copy(sources[i].at[at], held[i].at[at], in_sem.at[i, k]))
            outward.append(pltpu.make_async_copy(held[i].at[at], targets[i].at[at], out_sem.at[i, k]))
    for copy in inward:
        copy.start()
    for copy, onward in zip(inward, outward):
        copy.wait()
        onward.start()
    for copy in outward:
        copy.wait()


def delivered(arrays):
    anywhere = pl.BlockSpec(memory_space=pl.ANY)
    count = len(arrays)
    return pl.pallas_call(
        functools.partial(deliver_kernel, count),
        out_shape=tuple(jax.ShapeDtypeStruct(a.shape, a.dtype) for a in arrays),
        in_specs=[anywhere] * count,
        out_specs=(anywhere,) * count,
        scratch_shapes=[pltpu.VMEM(a.shape, a.dtype) for a in arrays]
        + [pltpu.SemaphoreType.DMA((count, 2)), pltpu.SemaphoreType.DMA((count, 2))],
        compiler_params=pltpu.CompilerParams(vmem_limit_bytes=56 * 1024 * 1024),
    )(*arrays)


def body(object_real, object_imag, probe, measured, positions):
    table, orders = constants()
    return delivered(
        gradients(object_real, object_imag, probe, measured, positions, jnp.asarray(table), jnp.asarray(orders))
    )


def solution(mesh):
    return jax.shard_map(
        body,
        mesh=mesh,
        in_specs=(
            P("tile", None, "mode", None),
            P("tile", None, "mode", None),
            P(None, "mode", None, None),
            P("tile", None, None, None),
            P("tile", None, None),
        ),
        out_specs=(
            P("tile", None, "mode", None),
            P("tile", None, "mode", None),
            P(None, "mode", None, None),
        ),
        check_vma=False,
    )
```

```python
import functools
import math

import jax
import jax.numpy as jnp
import ml_dtypes
import numpy as np
from jax import lax
from jax.experimental import pallas as pl
from jax.experimental.pallas import tpu as pltpu
from jax.sharding import PartitionSpec as P

PX = 256
HALF = PX // 2
TILE = 384
MARGIN = 64
ROWS = 96
EDGE = TILE - PX
FLOOR = 0.1
FRESNEL = 40.0
MESH = pl.DeviceIdType.MESH
F32 = jnp.float32
BF16 = jnp.bfloat16

A_LEFT, A_RIGHT, F_LEFT, F_RIGHT, B_LEFT, B_RIGHT = range(6)


def real_form(c):
    return np.block([[c.real, -c.imag], [c.imag, c.real]])


@functools.cache
def constants():
    index = np.arange(PX)
    fourier = np.exp(-2j * np.pi * (np.outer(index, index) % PX) / PX) / math.sqrt(PX)
    freq = ((index + HALF) % PX - HALF) / PX
    chirp = np.exp(-1j * np.pi * FRESNEL * freq**2)
    through = fourier.conj() @ (chirp[:, None] * fourier)
    near, far = through[:HALF, :HALF], through[:HALF, HALF:]
    pairs = [None] * 6
    moved = [(near + far) / 2, (near - far) / 2]
    split = [fourier[0::2, :HALF], fourier[1::2, :HALF]]
    pairs[A_LEFT] = [real_form(c) for c in moved]
    pairs[A_RIGHT] = [real_form(c).T for c in moved]
    pairs[F_LEFT] = [real_form(c) for c in split]
    pairs[F_RIGHT] = [real_form(c).T for c in split]
    pairs[B_LEFT] = [real_form(c.T) for c in split]
    pairs[B_RIGHT] = [real_form(c.T).T for c in split]
    table = np.array(pairs).reshape(12, PX, PX)
    high = table.astype(ml_dtypes.bfloat16)
    low = (table - high.astype(np.float64)).astype(ml_dtypes.bfloat16)
    order = np.zeros((PX, PX))
    order[np.arange(HALF), np.arange(0, PX, 2)] = 1
    order[np.arange(HALF) + HALF, np.arange(1, PX, 2)] = 1
    orders = np.array([order, order.T]).astype(ml_dtypes.bfloat16)
    return np.stack([high, low], axis=1), orders


def two_parts(x):
    high = x.astype(BF16)
    return high, (x - high.astype(F32)).astype(BF16)


def product(a, b):
    return jnp.dot(a, b, preferred_element_type=F32)


def apply_left(table, kind, sign, z):
    high, low = two_parts(z)
    c_high, c_low = table[2 * kind + sign, 0], table[2 * kind + sign, 1]
    return product(
        jnp.concatenate([c_high, c_low, c_high], axis=1),
        jnp.concatenate([high, high, low], axis=0),
    )


def apply_right(table, kind, sign, z):
    high, low = two_parts(z)
    c_high, c_low = table[2 * kind + sign, 0], table[2 * kind + sign, 1]
    return product(
        jnp.concatenate([high, high, low], axis=1),
        jnp.concatenate([c_high, c_low, c_high], axis=0),
    )


def rows_first(x):
    return x[:HALF], x[HALF:]


def lanes_first(x):
    return x[:, :HALF], x[:, HALF:]


def one_side(table, kind, re, im, left):
    halves, axis, apply = (rows_first, 0, apply_left) if left else (lanes_first, 1, apply_right)
    (r0, r1), (i0, i1) = halves(re), halves(im)
    if kind[0] != B_LEFT:
        r0, r1, i0, i1 = r0 + r1, r0 - r1, i0 + i1, i0 - i1
    which = kind[0] if left else kind[1]
    plus = apply(table, which, 0, jnp.concatenate([r0, i0], axis=axis))
    minus = apply(table, which, 1, jnp.concatenate([r1, i1], axis=axis))
    (pr, pi), (mr, mi) = halves(plus), halves(minus)
    if kind[0] != F_LEFT:
        pr, mr, pi, mi = pr + mr, pr - mr, pi + mi, pi - mi
    return jnp.concatenate([pr, mr], axis=axis), jnp.concatenate([pi, mi], axis=axis)


def both_sides(table, kind, re, im):
    re, im = one_side(table, kind, re, im, True)
    return one_side(table, kind, re, im, False)


THROUGH = (A_LEFT, A_RIGHT)
FORTH = (F_LEFT, F_RIGHT)
BACK = (B_LEFT, B_RIGHT)


def times(ar, ai, br, bi):
    return ar * br - ai * bi, ar * bi + ai * br


def kernel(
    tiles,
    obj_re,
    obj_im,
    probe_in,
    measured_in,
    positions,
    table_in,
    orders_in,
    out_re,
    out_im,
    out_probe,
    tile0,
    tile1,
    crops,
    probe,
    measured,
    table,
    orders,
    wave1,
    far,
    ipart,
    isib,
    isum,
    icross,
    factor,
    crop_grad,
    tile_grad,
    rs_send,
    rs_got,
    rs_cross,
    rs_cross_got,
    own,
    edge_send,
    edge_got,
    local_sem,
    tile_local,
    g_send,
    g_recv,
    i_send,
    i_recv,
    r_send,
    r_recv,
    e_send,
    e_recv,
    partial,
    got_a,
    got_b,
    part_b,
    y_send_buf,
    y_got,
    p_send,
    p_recv,
    total,
    out_sem,
    probe_sem,
):
    t = lax.axis_index("tile")
    m = lax.axis_index("mode")
    core = lax.rem(m, 2)
    high = m // 2
    sibling = high * 2 + (1 - core)
    across = (1 - high) * 2 + core
    diagonal = (1 - high) * 2 + (1 - core)
    left = lax.rem(t + tiles - 1, tiles)
    right = lax.rem(t + 1, tiles)
    to_sibling, to_across = (t, sibling), (t, across)
    to_left, to_right = (left, m), (right, m)

    ring = 4
    tz, ty, tx = lax.rem(t, ring), lax.rem(t // ring, 2), t // (2 * ring)
    z_peers = [(t - tz + lax.rem(tz + d, ring), m) for d in range(1, ring)]
    x_peers = [(lax.rem(t + 2 * ring * d, tiles), m) for d in range(1, ring)]
    y_peer = (t + ring * (1 - 2 * ty), m)

    barrier = pltpu.get_barrier_semaphore()
    for device in (to_sibling, to_across, to_left, to_right, y_peer, *z_peers, *x_peers):
        pl.semaphore_signal(barrier, inc=1, device_id=device, device_id_type=MESH)

    loads = [
        pltpu.make_async_copy(probe_in, probe, local_sem.at[0]),
        pltpu.make_async_copy(measured_in.at[0], measured, local_sem.at[1]),
        pltpu.make_async_copy(table_in, table, local_sem.at[2]),
        pltpu.make_async_copy(orders_in, orders, local_sem.at[3]),
    ]
    for load in loads:
        load.start()

    whole = (tile0, tile1)
    objects = (obj_re, obj_im)

    def my_rows(who):
        return pl.ds(pl.multiple_of(who * ROWS, ROWS), ROWS)

    def remote(src, dst, send, recv, device):
        return pltpu.make_async_remote_copy(
            src_ref=src, dst_ref=dst, send_sem=send, recv_sem=recv, device_id=device, device_id_type=MESH
        )

    own_copies, sends, crosses, relays = {}, {}, {}, {}
    for s in range(2):
        for p in range(2):
            src = objects[p].at[0, s]
            dst = whole[s].at[p, my_rows(m)]
            own_copies[s, p] = pltpu.make_async_copy(src, dst, tile_local.at[s, p])
            crosses[s, p] = remote(src, dst, g_send.at[0, s, p], g_recv.at[0, s, p], to_across)
            sends[s, p] = remote(src, dst, g_send.at[1, s, p], g_recv.at[1, s, p], to_sibling)
            got = whole[s].at[p, my_rows(across)]
            relays[s, p] = remote(got, got, g_send.at[2, s, p], g_recv.at[2, s, p], to_sibling)

    pl.semaphore_wait(barrier, 11)
    for s in range(2):
        for p in range(2):
            crosses[s, p].start()
    for s in range(2):
        for p in range(2):
            own_copies[s, p].start()
            sends[s, p].start()

    crop_grad[...] = jnp.zeros_like(crop_grad)
    partial[...] = jnp.zeros_like(partial)
    for load in loads:
        load.wait()
    for f in range(2):
        m_high, m_low = two_parts(measured[f])
        mixed = product(orders[0], m_high) + product(orders[0], m_low)
        m_high, m_low = two_parts(mixed)
        measured[f] = product(m_high, orders[1]) + product(m_low, orders[1])

    def tile_ready(s):
        for p in range(2):
            crosses[s, p].wait_recv()
            relays[s, p].start()
        for p in range(2):
            own_copies[s, p].wait()
            sends[s, p].wait_recv()
        for p in range(2):
            relays[s, p].wait_recv()

    row = [positions[0, f, 0] for f in range(2)]
    col = [positions[0, f, 1] for f in range(2)]

    def take_crops(s, frames=(0, 1)):
        for f in frames:
            up, back = lax.rem(TILE - row[f], TILE), lax.rem(TILE - col[f], TILE)
            for p in range(2):
                lines = pltpu.roll(whole[s][p], up, 0)[:PX]
                crops[f, s, p] = pltpu.roll(lines, back, 1)[:, :PX]

    tile_ready(0)
    take_crops(0)

    def pass_through(step, carry):
        f, mode = step // 2, lax.rem(step, 2)
        re, im = times(probe[0, mode], probe[1, mode], crops[f, 0, 0], crops[f, 0, 1])
        re, im = both_sides(table, THROUGH, re, im)
        wave1[f, mode, 0] = re
        wave1[f, mode, 1] = im
        return carry

    lax.fori_loop(0, 4, pass_through, 0, unroll=2)
    tile_ready(1)
    take_crops(1, (0,))

    def far_fields(f):
        ipart[f] = jnp.zeros_like(ipart[f])

        def step(mode, carry):
            re, im = times(wave1[f, mode, 0], wave1[f, mode, 1], crops[f, 1, 0], crops[f, 1, 1])
            re, im = both_sides(table, FORTH, re, im)
            far[f, mode, 0] = re
            far[f, mode, 1] = im
            ipart[f] += re * re + im * im
            return carry

        lax.fori_loop(0, 2, step, 0, unroll=True)

    def half_rows(who):
        return pl.ds(pl.multiple_of(who * HALF, HALF), HALF)

    to_pair = [
        remote(ipart.at[f, half_rows(1 - core)], isib.at[f], i_send.at[0, f], i_recv.at[0, f], to_sibling) for f in range(2)
    ]
    to_other = [remote(isum.at[f], icross.at[f], i_send.at[1, f], i_recv.at[1, f], to_across) for f in range(2)]
    to_share = [
        remote(
            factor.at[f, half_rows(core)],
            factor.at[f, half_rows(core)],
            i_send.at[2, f],
            i_recv.at[2, f],
            to_sibling,
        )
        for f in range(2)
    ]

    def pair_sum(f):
        to_pair[f].wait_recv()
        isum[f] = ipart[f, half_rows(core), :] + isib[f]
        to_other[f].start()

    def factors(f):
        to_other[f].wait_recv()
        whole_sum = isum[f] + icross[f]
        factor[f, half_rows(core), :] = 2.0 - 2.0 * measured[f, half_rows(core), :] / jnp.sqrt(whole_sum + FLOOR)
        to_share[f].start()

    far_fields(0)
    to_pair[0].start()
    take_crops(1, (1,))
    far_fields(1)
    to_pair[1].start()
    pair_sum(0)
    pair_sum(1)
    factors(0)

    def over(steps, body):
        def step(k, carry):
            f, mode = steps[0]
            if len(steps) > 1:
                f = f + k * (steps[1][0] - f)
                mode = mode + k * (steps[1][1] - mode)
            body(f, mode)
            return carry

        lax.fori_loop(0, len(steps), step, 0)

    def slice_1_step(f, mode):
        weight = factor[f]
        re, im = weight * far[f, mode, 0], -(weight * far[f, mode, 1])
        re, im = both_sides(table, BACK, re, im)
        gr, gi = times(wave1[f, mode, 0], wave1[f, mode, 1], re, im)
        crop_grad[f, 1, 0] += gr
        crop_grad[f, 1, 1] -= gi
        re, im = times(crops[f, 1, 0], crops[f, 1, 1], re, im)
        far[f, mode, 0] = re
        far[f, mode, 1] = im

    def probe_step(f, mode):
        re, im = both_sides(table, THROUGH, far[f, mode, 0], far[f, mode, 1])
        gr, gi = times(probe[0, mode], probe[1, mode], re, im)
        crop_grad[f, 0, 0] += gr
        crop_grad[f, 0, 1] -= gi
        gr, gi = times(crops[f, 0, 0], crops[f, 0, 1], re, im)
        partial[mode, 0] += gr
        partial[mode, 1] -= gi

    def both_steps(f, mode):
        slice_1_step(f, mode)
        probe_step(f, mode)

    low_lanes = lax.broadcasted_iota(jnp.int32, (TILE, 128), 1) < MARGIN

    def place(s, f):
        for p in range(2):
            wide = jnp.concatenate([crop_grad[f, s, p], jnp.zeros((PX, EDGE), F32)], axis=1)
            wide = pltpu.roll(wide, col[f], 1)
            wide = jnp.concatenate([wide, jnp.zeros((EDGE, TILE), F32)], axis=0)
            wide = pltpu.roll(wide, row[f], 0)
            first, middle, last = wide[:, :128], wide[:, 128:256], wide[:, 256:]
            ends, between = jnp.where(low_lanes, first, last), jnp.where(low_lanes, last, first)
            blocks = jnp.concatenate([ends, middle, between], axis=1)
            tile_grad[s, p] = blocks if f == 0 else tile_grad[s, p] + blocks

    def piece(s, p, who):
        return tile_grad[s, p, my_rows(who), :]

    parts = (pl.ds(0, 128), pl.ds(128, TILE - 128))
    rs_pair, rs_over, rs_edge, outward = {}, {}, {}, {}
    for s in range(2):
        for k in range(2):
            rs_pair[s, k] = remote(rs_send.at[s, k], rs_got.at[s, k], r_send.at[k, s], r_recv.at[k, s], to_sibling)
        for k in range(2):
            rs_over[s, k] = remote(
                rs_cross.at[s, :, :, parts[k]],
                rs_cross_got.at[s, :, :, parts[k]],
                r_send.at[2 + k, s],
                r_recv.at[2 + k, s],
                to_across,
            )
        rs_edge[s, 0] = remote(edge_send.at[s, 0], edge_got.at[s, 0], e_send.at[0, s], e_recv.at[0, s], to_right)
        rs_edge[s, 1] = remote(edge_send.at[s, 1], edge_got.at[s, 1], e_send.at[1, s], e_recv.at[1, s], to_left)
        for p in range(2):
            outward[s, p] = pltpu.make_async_copy(own.at[s, p], (out_re, out_im)[p].at[0, s], out_sem.at[s, p])

    def reduce_1(s):
        place(s, 1)
        for k, who in enumerate((diagonal, sibling)):
            for p in range(2):
                rs_send[s, k, p] = piece(s, p, who)
            rs_pair[s, k].start()

    def reduce_2(s):
        rs_pair[s, 0].wait_recv()
        for p in range(2):
            rs_cross[s, p] = piece(s, p, across) + rs_got[s, 0, p]
        rs_over[s, 0].start()
        rs_pair[s, 1].wait_recv()
        for p in range(2):
            own[s, p] = piece(s, p, m) + rs_got[s, 1, p]

    lane = lax.broadcasted_iota(jnp.int32, (ROWS, 128), 1)
    lower = lane < MARGIN

    def reduce_3(s):
        rs_over[s, 0].wait_recv()
        ends = [own[s, p, :, :128] + rs_cross_got[s, p, :, :128] for p in range(2)]
        for p in range(2):
            own[s, p, :, :128] = ends[p]
        edge_send[s, 0] = jnp.where(lower, pltpu.roll(ends[0], MARGIN, 1), ends[1])
        edge_send[s, 1] = jnp.where(lower, ends[0], pltpu.roll(ends[1], MARGIN, 1))
        rs_edge[s, 0].start()
        rs_edge[s, 1].start()

    def reduce_4(s):
        rs_edge[s, 0].wait_recv()
        rs_edge[s, 1].wait_recv()
        before, after = edge_got[s, 0], edge_got[s, 1]
        at_first = jnp.logical_and(lower, t > 0)
        at_last = jnp.logical_and(jnp.logical_not(lower), t < tiles - 1)
        befores = (before, pltpu.roll(before, MARGIN, 1))
        afters = (pltpu.roll(after, MARGIN, 1), after)
        rs_over[s, 1].wait_recv()
        for p in range(2):
            ends = own[s, p, :, :128] + jnp.where(at_first, befores[p], 0.0) + jnp.where(at_last, afters[p], 0.0)
            between = own[s, p, :, 256:] + rs_cross_got[s, p, :, 256:]
            own[s, p, :, 128:256] += rs_cross_got[s, p, :, 128:256]
            own[s, p, :, :128] = jnp.where(lower, ends, between)
            own[s, p, :, 256:] = jnp.where(lower, between, ends)
            outward[s, p].start()

    axes = (((tz, z_peers), (tx, x_peers)), ((tx, x_peers), (tz, z_peers)))

    def block(length, index, base=0):
        return pl.ds(pl.multiple_of(base + index * length, length), length)

    scatter_a, scatter_b, swap_y, gather_b, gather_a, probe_out = {}, {}, {}, {}, {}, {}
    chunks = [(c, h) for h in range(2) for c in range(2)]
    for c, h in chunks:
        (ia, peers_a), (ib, peers_b) = axes[c]
        for k in range(ring - 1):
            ja, jb = lax.rem(ia + k + 1, ring), lax.rem(ib + k + 1, ring)
            sems = [(p_send.at[c, h, i, k], p_recv.at[c, h, i, k]) for i in range(4)]
            scatter_a[c, h, k] = remote(
                partial.at[c, :, block(32, ja, h * HALF)], got_a.at[c, h, k], *sems[0], peers_a[k]
            )
            scatter_b[c, h, k] = remote(part_b.at[c, h, :, block(8, jb)], got_b.at[c, h, k], *sems[1], peers_b[k])
            mine_b = total.at[:, c, block(8, ib, h * HALF + ia * 32)]
            gather_b[c, h, k] = remote(mine_b, mine_b, *sems[2], peers_b[k])
            mine_a = total.at[:, c, block(32, ia, h * HALF)]
            gather_a[c, h, k] = remote(mine_a, mine_a, *sems[3], peers_a[k])
        swap_y[c, h] = remote(y_send_buf.at[c, h], y_got.at[c, h], p_send.at[c, h, 4, 0], p_recv.at[c, h, 4, 0], y_peer)
        some = pl.ds(h * HALF, HALF)
        probe_out[c, h] = pltpu.make_async_copy(total.at[:, c, some], out_probe.at[:, c, some], probe_sem.at[c, h])

    def send_all(group, c, h):
        for k in (1, 0, 2):
            group[c, h, k].start()

    def take_all(group, c, h):
        for k in range(3):
            group[c, h, k].wait_recv()

    def probe_1(c):
        for h in range(2):
            send_all(scatter_a, c, h)

    def probe_2(c, h):
        ia = axes[c][0][0]
        take_all(scatter_a, c, h)
        got = got_a[c, h, 0] + got_a[c, h, 1] + got_a[c, h, 2]
        part_b[c, h] = partial[c, :, block(32, ia, h * HALF), :] + got
        send_all(scatter_b, c, h)

    def probe_3(c, h):
        ib = axes[c][1][0]
        take_all(scatter_b, c, h)
        got = got_b[c, h, 0] + got_b[c, h, 1] + got_b[c, h, 2]
        y_send_buf[c, h] = part_b[c, h, :, block(8, ib), :] + got
        swap_y[c, h].start()

    def probe_4(c, h):
        ia, ib = axes[c][0][0], axes[c][1][0]
        swap_y[c, h].wait_recv()
        total[:, c, block(8, ib, h * HALF + ia * 32), :] = y_send_buf[c, h] + y_got[c, h]
        send_all(gather_b, c, h)

    def probe_5(c, h):
        take_all(gather_b, c, h)
        send_all(gather_a, c, h)

    def probe_6(c, h):
        take_all(gather_a, c, h)
        probe_out[c, h].start()

    def each(step, h):
        for c in range(2):
            step(c, h)

    to_share[0].wait_recv()
    over([(0, 0)], both_steps)
    factors(1)
    over([(0, 1)], both_steps)
    place(1, 0)
    place(0, 0)
    to_share[1].wait_recv()
    over([(1, 0)], both_steps)
    probe_1(0)
    over([(1, 1)], both_steps)
    probe_1(1)
    reduce_1(1)
    reduce_1(0)
    reduce_2(1)
    reduce_2(0)
    each(probe_2, 0)
    each(probe_2, 1)
    each(probe_3, 0)
    reduce_3(1)
    each(probe_3, 1)
    rs_over[1, 1].start()
    rs_over[0, 1].start()
    each(probe_4, 0)
    reduce_3(0)
    each(probe_4, 1)
    each(probe_5, 0)
    each(probe_5, 1)
    reduce_4(1)
    each(probe_6, 0)
    reduce_4(0)
    each(probe_6, 1)

    for group in (probe_out, outward):
        for copy in group.values():
            copy.wait()
    for group in (scatter_a, scatter_b, swap_y, gather_b, gather_a):
        for copy in group.values():
            copy.wait_send()
    for group in (sends, crosses, relays, rs_pair, rs_over, rs_edge):
        for copy in group.values():
            copy.wait_send()
    for group in (to_pair, to_other, to_share):
        for copy in group:
            copy.wait_send()


def gradients(obj_re, obj_im, probe, measured, positions, table, orders):
    tiles = lax.axis_size("tile")
    shape = jax.ShapeDtypeStruct
    anywhere = pl.BlockSpec(memory_space=pl.ANY)
    return pl.pallas_call(
        functools.partial(kernel, tiles),
        out_shape=(shape(obj_re.shape, F32), shape(obj_im.shape, F32), shape(probe.shape, F32)),
        in_specs=[anywhere, anywhere, anywhere, anywhere, pl.BlockSpec(memory_space=pltpu.SMEM), anywhere, anywhere],
        out_specs=(anywhere, anywhere, anywhere),
        scratch_shapes=[
            pltpu.VMEM((2, TILE, TILE), F32),
            pltpu.VMEM((2, TILE, TILE), F32),
            pltpu.VMEM((2, 2, 2, PX, PX), F32),
            pltpu.VMEM((2, 2, PX, PX), F32),
            pltpu.VMEM((2, PX, PX), F32),
            pltpu.VMEM(table.shape, BF16),
            pltpu.VMEM(orders.shape, BF16),
            pltpu.VMEM((2, 2, 2, PX, PX), F32),
            pltpu.VMEM((2, 2, 2, PX, PX), F32),
            pltpu.VMEM((2, PX, PX), F32),
            pltpu.VMEM((2, HALF, PX), F32),
            pltpu.VMEM((2, HALF, PX), F32),
            pltpu.VMEM((2, HALF, PX), F32),
            pltpu.VMEM((2, PX, PX), F32),
            pltpu.VMEM((2, 2, 2, PX, PX), F32),
            pltpu.VMEM((2, 2, TILE, TILE), F32),
            pltpu.VMEM((2, 2, 2, ROWS, TILE), F32),
            pltpu.VMEM((2, 2, 2, ROWS, TILE), F32),
            pltpu.VMEM((2, 2, ROWS, TILE), F32),
            pltpu.VMEM((2, 2, ROWS, TILE), F32),
            pltpu.VMEM((2, 2, ROWS, TILE), F32),
            pltpu.VMEM((2, 2, ROWS, 128), F32),
            pltpu.VMEM((2, 2, ROWS, 128), F32),
            pltpu.SemaphoreType.DMA((4,)),
            pltpu.SemaphoreType.DMA((2, 2)),
            pltpu.SemaphoreType.DMA((3, 2, 2)),
            pltpu.SemaphoreType.DMA((3, 2, 2)),
            pltpu.SemaphoreType.DMA((3, 2)),
            pltpu.SemaphoreType.DMA((3, 2)),
            pltpu.SemaphoreType.DMA((5, 2)),
            pltpu.SemaphoreType.DMA((5, 2)),
            pltpu.SemaphoreType.DMA((2, 2)),
            pltpu.SemaphoreType.DMA((2, 2)),
            pltpu.VMEM((2, 2, PX, PX), F32),
            pltpu.VMEM((2, 2, 3, 2, 32, PX), F32),
            pltpu.VMEM((2, 2, 3, 2, 8, PX), F32),
            pltpu.VMEM((2, 2, 2, 32, PX), F32),
            pltpu.VMEM((2, 2, 2, 8, PX), F32),
            pltpu.VMEM((2, 2, 2, 8, PX), F32),
            pltpu.SemaphoreType.DMA((2, 2, 5, 3)),
            pltpu.SemaphoreType.DMA((2, 2, 5, 3)),
            pltpu.VMEM((2, 2, PX, PX), F32),
            pltpu.SemaphoreType.DMA((2, 2)),
            pltpu.SemaphoreType.DMA((2, 2)),
        ],
        compiler_params=pltpu.CompilerParams(
            collective_id=0, has_side_effects=True, vmem_limit_bytes=56 * 1024 * 1024
        ),
        cost_estimate=pl.CostEstimate(flops=7 * 10**9, bytes_accessed=10**7, transcendentals=10**6),
    )(obj_re, obj_im, probe, measured, positions, table, orders)


def deliver_kernel(count, *refs):
    sources, targets, held = refs[:count], refs[count : 2 * count], refs[2 * count : 3 * count]
    in_sem, out_sem = refs[3 * count :]
    inward, outward = [], []
    for i in range(count):
        rows = sources[i].shape[2] // 2
        for k in range(4):
            at = (slice(None), k // 2, pl.ds(k % 2 * rows, rows))
            inward.append(pltpu.make_async_copy(sources[i].at[at], held[i].at[at], in_sem.at[i, k]))
            outward.append(pltpu.make_async_copy(held[i].at[at], targets[i].at[at], out_sem.at[i, k]))
    for copy in inward:
        copy.start()
    for copy, onward in zip(inward, outward):
        copy.wait()
        onward.start()
    for copy in outward:
        copy.wait()


def delivered(arrays):
    anywhere = pl.BlockSpec(memory_space=pl.ANY)
    count = len(arrays)
    return pl.pallas_call(
        functools.partial(deliver_kernel, count),
        out_shape=tuple(jax.ShapeDtypeStruct(a.shape, a.dtype) for a in arrays),
        in_specs=[anywhere] * count,
        out_specs=(anywhere,) * count,
        scratch_shapes=[pltpu.VMEM(a.shape, a.dtype) for a in arrays]
        + [pltpu.SemaphoreType.DMA((count, 4)), pltpu.SemaphoreType.DMA((count, 4))],
        compiler_params=pltpu.CompilerParams(vmem_limit_bytes=56 * 1024 * 1024),
    )(*arrays)


def body(object_real, object_imag, probe, measured, positions):
    table, orders = constants()
    return delivered(
        gradients(object_real, object_imag, probe, measured, positions, jnp.asarray(table), jnp.asarray(orders))
    )


def solution(mesh):
    return jax.shard_map(
        body,
        mesh=mesh,
        in_specs=(
            P("tile", None, "mode", None),
            P("tile", None, "mode", None),
            P(None, "mode", None, None),
            P("tile", None, None, None),
            P("tile", None, None),
        ),
        out_specs=(
            P("tile", None, "mode", None),
            P("tile", None, "mode", None),
            P(None, "mode", None, None),
        ),
        check_vma=False,
    )
```

```python
import functools
import math

import jax
import jax.numpy as jnp
import ml_dtypes
import numpy as np
from jax import lax
from jax.experimental import pallas as pl
from jax.experimental.pallas import tpu as pltpu
from jax.sharding import PartitionSpec as P

PX = 256
HALF = PX // 2
TILE = 384
MARGIN = 64
ROWS = 96
EDGE = TILE - PX
FLOOR = 0.1
FRESNEL = 40.0
MESH = pl.DeviceIdType.MESH
F32 = jnp.float32
BF16 = jnp.bfloat16

A_LEFT, A_RIGHT, F_LEFT, F_RIGHT, B_LEFT, B_RIGHT = range(6)


def real_form(c):
    return np.block([[c.real, -c.imag], [c.imag, c.real]])


@functools.cache
def constants():
    index = np.arange(PX)
    fourier = np.exp(-2j * np.pi * (np.outer(index, index) % PX) / PX) / math.sqrt(PX)
    freq = ((index + HALF) % PX - HALF) / PX
    chirp = np.exp(-1j * np.pi * FRESNEL * freq**2)
    through = fourier.conj() @ (chirp[:, None] * fourier)
    near, far = through[:HALF, :HALF], through[:HALF, HALF:]
    pairs = [None] * 6
    moved = [(near + far) / 2, (near - far) / 2]
    split = [fourier[0::2, :HALF], fourier[1::2, :HALF]]
    pairs[A_LEFT] = [real_form(c) for c in moved]
    pairs[A_RIGHT] = [real_form(c).T for c in moved]
    pairs[F_LEFT] = [real_form(c) for c in split]
    pairs[F_RIGHT] = [real_form(c).T for c in split]
    pairs[B_LEFT] = [real_form(c.T) for c in split]
    pairs[B_RIGHT] = [real_form(c.T).T for c in split]
    table = np.array(pairs).reshape(12, PX, PX)
    high = table.astype(ml_dtypes.bfloat16)
    low = (table - high.astype(np.float64)).astype(ml_dtypes.bfloat16)
    order = np.zeros((PX, PX))
    order[np.arange(HALF), np.arange(0, PX, 2)] = 1
    order[np.arange(HALF) + HALF, np.arange(1, PX, 2)] = 1
    orders = np.array([order, order.T]).astype(ml_dtypes.bfloat16)
    return np.stack([high, low], axis=1), orders


def two_parts(x):
    high = x.astype(BF16)
    return high, (x - high.astype(F32)).astype(BF16)


def product(a, b):
    return jnp.dot(a, b, preferred_element_type=F32)


def apply_left(table, kind, sign, z):
    high, low = two_parts(z)
    c_high, c_low = table[2 * kind + sign, 0], table[2 * kind + sign, 1]
    return product(
        jnp.concatenate([c_high, c_low, c_high], axis=1),
        jnp.concatenate([high, high, low], axis=0),
    )


def apply_right(table, kind, sign, z):
    high, low = two_parts(z)
    c_high, c_low = table[2 * kind + sign, 0], table[2 * kind + sign, 1]
    return product(
        jnp.concatenate([high, high, low], axis=1),
        jnp.concatenate([c_high, c_low, c_high], axis=0),
    )


def rows_first(x):
    return x[:HALF], x[HALF:]


def lanes_first(x):
    return x[:, :HALF], x[:, HALF:]


def one_side(table, kind, re, im, left):
    halves, axis, apply = (rows_first, 0, apply_left) if left else (lanes_first, 1, apply_right)
    (r0, r1), (i0, i1) = halves(re), halves(im)
    if kind[0] != B_LEFT:
        r0, r1, i0, i1 = r0 + r1, r0 - r1, i0 + i1, i0 - i1
    which = kind[0] if left else kind[1]
    plus = apply(table, which, 0, jnp.concatenate([r0, i0], axis=axis))
    minus = apply(table, which, 1, jnp.concatenate([r1, i1], axis=axis))
    (pr, pi), (mr, mi) = halves(plus), halves(minus)
    if kind[0] != F_LEFT:
        pr, mr, pi, mi = pr + mr, pr - mr, pi + mi, pi - mi
    return jnp.concatenate([pr, mr], axis=axis), jnp.concatenate([pi, mi], axis=axis)


def both_sides(table, kind, re, im):
    re, im = one_side(table, kind, re, im, True)
    return one_side(table, kind, re, im, False)


THROUGH = (A_LEFT, A_RIGHT)
FORTH = (F_LEFT, F_RIGHT)
BACK = (B_LEFT, B_RIGHT)


def times(ar, ai, br, bi):
    return ar * br - ai * bi, ar * bi + ai * br


def kernel(
    tiles,
    obj_re,
    obj_im,
    probe_in,
    measured_in,
    positions,
    table_in,
    orders_in,
    out_re,
    out_im,
    out_probe,
    tile0,
    tile1,
    crops,
    probe,
    measured,
    table,
    orders,
    wave1,
    far,
    ipart,
    isib,
    isum,
    icross,
    factor,
    crop_grad,
    tile_grad,
    rs_send,
    rs_got,
    rs_cross,
    rs_cross_got,
    own,
    edge_send,
    edge_got,
    local_sem,
    tile_local,
    g_send,
    g_recv,
    i_send,
    i_recv,
    r_send,
    r_recv,
    e_send,
    e_recv,
    partial,
    got_a,
    got_b,
    part_b,
    y_send_buf,
    y_got,
    p_send,
    p_recv,
    total,
    out_sem,
    probe_sem,
):
    t = lax.axis_index("tile")
    m = lax.axis_index("mode")
    core = lax.rem(m, 2)
    high = m // 2
    sibling = high * 2 + (1 - core)
    across = (1 - high) * 2 + core
    diagonal = (1 - high) * 2 + (1 - core)
    left = lax.rem(t + tiles - 1, tiles)
    right = lax.rem(t + 1, tiles)
    to_sibling, to_across = (t, sibling), (t, across)
    to_left, to_right = (left, m), (right, m)

    ring = 4
    tz, ty, tx = lax.rem(t, ring), lax.rem(t // ring, 2), t // (2 * ring)
    z_peers = [(t - tz + lax.rem(tz + d, ring), m) for d in range(1, ring)]
    x_peers = [(lax.rem(t + 2 * ring * d, tiles), m) for d in range(1, ring)]
    y_peer = (t + ring * (1 - 2 * ty), m)

    barrier = pltpu.get_barrier_semaphore()
    for device in (to_sibling, to_across, to_left, to_right, y_peer, *z_peers, *x_peers):
        pl.semaphore_signal(barrier, inc=1, device_id=device, device_id_type=MESH)

    loads = [
        pltpu.make_async_copy(probe_in, probe, local_sem.at[0]),
        pltpu.make_async_copy(measured_in.at[0], measured, local_sem.at[1]),
        pltpu.make_async_copy(table_in, table, local_sem.at[2]),
        pltpu.make_async_copy(orders_in, orders, local_sem.at[3]),
    ]
    for load in loads:
        load.start()

    whole = (tile0, tile1)
    objects = (obj_re, obj_im)

    def my_rows(who):
        return pl.ds(pl.multiple_of(who * ROWS, ROWS), ROWS)

    def remote(src, dst, send, recv, device):
        return pltpu.make_async_remote_copy(
            src_ref=src, dst_ref=dst, send_sem=send, recv_sem=recv, device_id=device, device_id_type=MESH
        )

    own_copies, sends, crosses, relays = {}, {}, {}, {}
    for s in range(2):
        for p in range(2):
            src = objects[p].at[0, s]
            dst = whole[s].at[p, my_rows(m)]
            own_copies[s, p] = pltpu.make_async_copy(src, dst, tile_local.at[s, p])
            crosses[s, p] = remote(src, dst, g_send.at[0, s, p], g_recv.at[0, s, p], to_across)
            sends[s, p] = remote(src, dst, g_send.at[1, s, p], g_recv.at[1, s, p], to_sibling)
            got = whole[s].at[p, my_rows(across)]
            relays[s, p] = remote(got, got, g_send.at[2, s, p], g_recv.at[2, s, p], to_sibling)

    pl.semaphore_wait(barrier, 11)
    for s in range(2):
        for p in range(2):
            crosses[s, p].start()
    for s in range(2):
        for p in range(2):
            own_copies[s, p].start()
            sends[s, p].start()

    crop_grad[...] = jnp.zeros_like(crop_grad)
    partial[...] = jnp.zeros_like(partial)
    for load in loads:
        load.wait()
    for f in range(2):
        m_high, m_low = two_parts(measured[f])
        mixed = product(orders[0], m_high) + product(orders[0], m_low)
        m_high, m_low = two_parts(mixed)
        measured[f] = product(m_high, orders[1]) + product(m_low, orders[1])

    def tile_ready(s):
        for p in range(2):
            crosses[s, p].wait_recv()
            relays[s, p].start()
        for p in range(2):
            own_copies[s, p].wait()
            sends[s, p].wait_recv()
        for p in range(2):
            relays[s, p].wait_recv()

    row = [positions[0, f, 0] for f in range(2)]
    col = [positions[0, f, 1] for f in range(2)]

    def take_crops(s, frames=(0, 1)):
        for f in frames:
            up, back = lax.rem(TILE - row[f], TILE), lax.rem(TILE - col[f], TILE)
            for p in range(2):
                lines = pltpu.roll(whole[s][p], up, 0)[:PX]
                crops[f, s, p] = pltpu.roll(lines, back, 1)[:, :PX]

    tile_ready(0)
    take_crops(0)

    def pass_through(step, carry):
        f, mode = step // 2, lax.rem(step, 2)
        re, im = times(probe[0, mode], probe[1, mode], crops[f, 0, 0], crops[f, 0, 1])
        re, im = both_sides(table, THROUGH, re, im)
        wave1[f, mode, 0] = re
        wave1[f, mode, 1] = im
        return carry

    lax.fori_loop(0, 4, pass_through, 0, unroll=2)
    tile_ready(1)
    take_crops(1, (0,))

    def far_fields(f):
        ipart[f] = jnp.zeros_like(ipart[f])

        def step(mode, carry):
            re, im = times(wave1[f, mode, 0], wave1[f, mode, 1], crops[f, 1, 0], crops[f, 1, 1])
            re, im = both_sides(table, FORTH, re, im)
            far[f, mode, 0] = re
            far[f, mode, 1] = im
            ipart[f] += re * re + im * im
            return carry

        lax.fori_loop(0, 2, step, 0, unroll=True)

    def half_rows(who):
        return pl.ds(pl.multiple_of(who * HALF, HALF), HALF)

    to_pair = [
        remote(ipart.at[f, half_rows(1 - core)], isib.at[f], i_send.at[0, f], i_recv.at[0, f], to_sibling) for f in range(2)
    ]
    to_other = [remote(isum.at[f], icross.at[f], i_send.at[1, f], i_recv.at[1, f], to_across) for f in range(2)]
    to_share = [
        remote(
            factor.at[f, half_rows(core)],
            factor.at[f, half_rows(core)],
            i_send.at[2, f],
            i_recv.at[2, f],
            to_sibling,
        )
        for f in range(2)
    ]

    def pair_sum(f):
        to_pair[f].wait_recv()
        isum[f] = ipart[f, half_rows(core), :] + isib[f]
        to_other[f].start()

    def factors(f):
        to_other[f].wait_recv()
        whole_sum = isum[f] + icross[f]
        factor[f, half_rows(core), :] = 2.0 - 2.0 * measured[f, half_rows(core), :] / jnp.sqrt(whole_sum + FLOOR)
        to_share[f].start()

    far_fields(0)
    to_pair[0].start()
    take_crops(1, (1,))
    far_fields(1)
    to_pair[1].start()
    pair_sum(0)
    pair_sum(1)
    factors(0)

    def over(steps, body):
        def step(k, carry):
            f, mode = steps[0]
            if len(steps) > 1:
                f = f + k * (steps[1][0] - f)
                mode = mode + k * (steps[1][1] - mode)
            body(f, mode)
            return carry

        lax.fori_loop(0, len(steps), step, 0)

    def slice_1_step(f, mode):
        weight = factor[f]
        re, im = weight * far[f, mode, 0], -(weight * far[f, mode, 1])
        re, im = both_sides(table, BACK, re, im)
        gr, gi = times(wave1[f, mode, 0], wave1[f, mode, 1], re, im)
        crop_grad[f, 1, 0] += gr
        crop_grad[f, 1, 1] -= gi
        re, im = times(crops[f, 1, 0], crops[f, 1, 1], re, im)
        far[f, mode, 0] = re
        far[f, mode, 1] = im

    def probe_step(f, mode):
        re, im = both_sides(table, THROUGH, far[f, mode, 0], far[f, mode, 1])
        gr, gi = times(probe[0, mode], probe[1, mode], re, im)
        crop_grad[f, 0, 0] += gr
        crop_grad[f, 0, 1] -= gi
        gr, gi = times(crops[f, 0, 0], crops[f, 0, 1], re, im)
        partial[mode, 0] += gr
        partial[mode, 1] -= gi

    def both_steps(f, mode):
        slice_1_step(f, mode)
        probe_step(f, mode)

    low_lanes = lax.broadcasted_iota(jnp.int32, (TILE, 128), 1) < MARGIN

    def place(s, f):
        for p in range(2):
            wide = jnp.concatenate([crop_grad[f, s, p], jnp.zeros((PX, EDGE), F32)], axis=1)
            wide = pltpu.roll(wide, col[f], 1)
            wide = jnp.concatenate([wide, jnp.zeros((EDGE, TILE), F32)], axis=0)
            wide = pltpu.roll(wide, row[f], 0)
            first, middle, last = wide[:, :128], wide[:, 128:256], wide[:, 256:]
            ends, between = jnp.where(low_lanes, first, last), jnp.where(low_lanes, last, first)
            blocks = jnp.concatenate([ends, middle, between], axis=1)
            tile_grad[s, p] = blocks if f == 0 else tile_grad[s, p] + blocks

    def piece(s, p, who):
        return tile_grad[s, p, my_rows(who), :]

    parts = (pl.ds(0, 128), pl.ds(128, TILE - 128))
    rs_pair, rs_over, rs_edge, outward = {}, {}, {}, {}
    for s in range(2):
        for k in range(2):
            rs_pair[s, k] = remote(rs_send.at[s, k], rs_got.at[s, k], r_send.at[k, s], r_recv.at[k, s], to_sibling)
        for k in range(2):
            rs_over[s, k] = remote(
                rs_cross.at[s, :, :, parts[k]],
                rs_cross_got.at[s, :, :, parts[k]],
                r_send.at[2 + k, s],
                r_recv.at[2 + k, s],
                to_across,
            )
        rs_edge[s, 0] = remote(edge_send.at[s, 0], edge_got.at[s, 0], e_send.at[0, s], e_recv.at[0, s], to_right)
        rs_edge[s, 1] = remote(edge_send.at[s, 1], edge_got.at[s, 1], e_send.at[1, s], e_recv.at[1, s], to_left)
        for p in range(2):
            outward[s, p] = pltpu.make_async_copy(own.at[s, p], (out_re, out_im)[p].at[0, s], out_sem.at[s, p])

    def reduce_1(s):
        place(s, 1)
        for k, who in enumerate((diagonal, sibling)):
            for p in range(2):
                rs_send[s, k, p] = piece(s, p, who)
            rs_pair[s, k].start()

    def reduce_2(s):
        rs_pair[s, 0].wait_recv()
        for p in range(2):
            rs_cross[s, p] = piece(s, p, across) + rs_got[s, 0, p]
        rs_over[s, 0].start()
        rs_pair[s, 1].wait_recv()
        for p in range(2):
            own[s, p] = piece(s, p, m) + rs_got[s, 1, p]

    lane = lax.broadcasted_iota(jnp.int32, (ROWS, 128), 1)
    lower = lane < MARGIN

    def reduce_3(s):
        rs_over[s, 0].wait_recv()
        ends = [own[s, p, :, :128] + rs_cross_got[s, p, :, :128] for p in range(2)]
        for p in range(2):
            own[s, p, :, :128] = ends[p]
        edge_send[s, 0] = jnp.where(lower, pltpu.roll(ends[0], MARGIN, 1), ends[1])
        edge_send[s, 1] = jnp.where(lower, ends[0], pltpu.roll(ends[1], MARGIN, 1))
        rs_edge[s, 0].start()
        rs_edge[s, 1].start()

    def reduce_4(s):
        rs_edge[s, 0].wait_recv()
        rs_edge[s, 1].wait_recv()
        before, after = edge_got[s, 0], edge_got[s, 1]
        at_first = jnp.logical_and(lower, t > 0)
        at_last = jnp.logical_and(jnp.logical_not(lower), t < tiles - 1)
        befores = (before, pltpu.roll(before, MARGIN, 1))
        afters = (pltpu.roll(after, MARGIN, 1), after)
        rs_over[s, 1].wait_recv()
        for p in range(2):
            ends = own[s, p, :, :128] + jnp.where(at_first, befores[p], 0.0) + jnp.where(at_last, afters[p], 0.0)
            between = own[s, p, :, 256:] + rs_cross_got[s, p, :, 256:]
            own[s, p, :, 128:256] += rs_cross_got[s, p, :, 128:256]
            own[s, p, :, :128] = jnp.where(lower, ends, between)
            own[s, p, :, 256:] = jnp.where(lower, between, ends)
            outward[s, p].start()

    axes = (((tz, z_peers), (tx, x_peers)), ((tx, x_peers), (tz, z_peers)))

    def block(length, index, base=0):
        return pl.ds(pl.multiple_of(base + index * length, length), length)

    scatter_a, scatter_b, swap_y, gather_b, gather_a, probe_out = {}, {}, {}, {}, {}, {}
    chunks = [(c, h) for h in range(4) for c in range(2)]

    def quarter(h, length, index, base=0):
        return block(length, index, h // 2 * HALF + base), pl.ds(h % 2 * HALF, HALF)

    for c, h in chunks:
        (ia, peers_a), (ib, peers_b) = axes[c]
        for k in range(ring - 1):
            ja, jb = lax.rem(ia + k + 1, ring), lax.rem(ib + k + 1, ring)
            sems = [(p_send.at[c, h, i, k], p_recv.at[c, h, i, k]) for i in range(4)]
            scatter_a[c, h, k] = remote(
                partial.at[(c, slice(None), *quarter(h, 32, ja))], got_a.at[c, h, k], *sems[0], peers_a[k]
            )
            scatter_b[c, h, k] = remote(part_b.at[c, h, :, block(8, jb)], got_b.at[c, h, k], *sems[1], peers_b[k])
            mine_b = total.at[(slice(None), c, *quarter(h, 8, ib, ia * 32))]
            gather_b[c, h, k] = remote(mine_b, mine_b, *sems[2], peers_b[k])
            mine_a = total.at[(slice(None), c, *quarter(h, 32, ia))]
            gather_a[c, h, k] = remote(mine_a, mine_a, *sems[3], peers_a[k])
        swap_y[c, h] = remote(y_send_buf.at[c, h], y_got.at[c, h], p_send.at[c, h, 4, 0], p_recv.at[c, h, 4, 0], y_peer)
        some = (slice(None), c, pl.ds(h // 2 * HALF, HALF), pl.ds(h % 2 * HALF, HALF))
        probe_out[c, h] = pltpu.make_async_copy(total.at[some], out_probe.at[some], probe_sem.at[c, h])

    def send_all(group, c, h):
        for k in (1, 0, 2):
            group[c, h, k].start()

    def take_all(group, c, h):
        for k in range(3):
            group[c, h, k].wait_recv()

    def probe_1(c):
        for h in range(4):
            send_all(scatter_a, c, h)

    def probe_2(c, h):
        ia = axes[c][0][0]
        take_all(scatter_a, c, h)
        got = got_a[c, h, 0] + got_a[c, h, 1] + got_a[c, h, 2]
        part_b[c, h] = partial[(c, slice(None), *quarter(h, 32, ia))] + got
        send_all(scatter_b, c, h)

    def probe_3(c, h):
        ib = axes[c][1][0]
        take_all(scatter_b, c, h)
        got = got_b[c, h, 0] + got_b[c, h, 1] + got_b[c, h, 2]
        y_send_buf[c, h] = part_b[c, h, :, block(8, ib), :] + got
        swap_y[c, h].start()

    def probe_4(c, h):
        ia, ib = axes[c][0][0], axes[c][1][0]
        swap_y[c, h].wait_recv()
        total[(slice(None), c, *quarter(h, 8, ib, ia * 32))] = y_send_buf[c, h] + y_got[c, h]
        send_all(gather_b, c, h)

    def probe_5(c, h):
        take_all(gather_b, c, h)
        send_all(gather_a, c, h)

    def probe_6(c, h):
        take_all(gather_a, c, h)
        probe_out[c, h].start()

    def each(step, h):
        for c in range(2):
            step(c, h)

    to_share[0].wait_recv()
    over([(0, 0)], both_steps)
    factors(1)
    over([(0, 1)], both_steps)
    place(1, 0)
    place(0, 0)
    to_share[1].wait_recv()
    over([(1, 0)], both_steps)
    probe_1(0)
    over([(1, 1)], both_steps)
    probe_1(1)
    reduce_1(1)
    reduce_1(0)
    reduce_2(1)
    reduce_2(0)
    each(probe_2, 0)
    each(probe_2, 1)
    each(probe_3, 0)
    each(probe_2, 2)
    each(probe_3, 1)
    each(probe_2, 3)
    each(probe_3, 2)
    each(probe_4, 0)
    reduce_3(1)
    each(probe_3, 3)
    rs_over[1, 1].start()
    rs_over[0, 1].start()
    each(probe_4, 1)
    reduce_3(0)
    each(probe_5, 0)
    each(probe_4, 2)
    each(probe_5, 1)
    each(probe_4, 3)
    each(probe_5, 2)
    each(probe_5, 3)
    reduce_4(1)
    each(probe_6, 0)
    each(probe_6, 1)
    each(probe_6, 2)
    reduce_4(0)
    each(probe_6, 3)

    for group in (probe_out, outward):
        for copy in group.values():
            copy.wait()
    for group in (scatter_a, scatter_b, swap_y, gather_b, gather_a):
        for copy in group.values():
            copy.wait_send()
    for group in (sends, crosses, relays, rs_pair, rs_over, rs_edge):
        for copy in group.values():
            copy.wait_send()
    for group in (to_pair, to_other, to_share):
        for copy in group:
            copy.wait_send()


def gradients(obj_re, obj_im, probe, measured, positions, table, orders):
    tiles = lax.axis_size("tile")
    shape = jax.ShapeDtypeStruct
    anywhere = pl.BlockSpec(memory_space=pl.ANY)
    return pl.pallas_call(
        functools.partial(kernel, tiles),
        out_shape=(shape(obj_re.shape, F32), shape(obj_im.shape, F32), shape(probe.shape, F32)),
        in_specs=[anywhere, anywhere, anywhere, anywhere, pl.BlockSpec(memory_space=pltpu.SMEM), anywhere, anywhere],
        out_specs=(anywhere, anywhere, anywhere),
        scratch_shapes=[
            pltpu.VMEM((2, TILE, TILE), F32),
            pltpu.VMEM((2, TILE, TILE), F32),
            pltpu.VMEM((2, 2, 2, PX, PX), F32),
            pltpu.VMEM((2, 2, PX, PX), F32),
            pltpu.VMEM((2, PX, PX), F32),
            pltpu.VMEM(table.shape, BF16),
            pltpu.VMEM(orders.shape, BF16),
            pltpu.VMEM((2, 2, 2, PX, PX), F32),
            pltpu.VMEM((2, 2, 2, PX, PX), F32),
            pltpu.VMEM((2, PX, PX), F32),
            pltpu.VMEM((2, HALF, PX), F32),
            pltpu.VMEM((2, HALF, PX), F32),
            pltpu.VMEM((2, HALF, PX), F32),
            pltpu.VMEM((2, PX, PX), F32),
            pltpu.VMEM((2, 2, 2, PX, PX), F32),
            pltpu.VMEM((2, 2, TILE, TILE), F32),
            pltpu.VMEM((2, 2, 2, ROWS, TILE), F32),
            pltpu.VMEM((2, 2, 2, ROWS, TILE), F32),
            pltpu.VMEM((2, 2, ROWS, TILE), F32),
            pltpu.VMEM((2, 2, ROWS, TILE), F32),
            pltpu.VMEM((2, 2, ROWS, TILE), F32),
            pltpu.VMEM((2, 2, ROWS, 128), F32),
            pltpu.VMEM((2, 2, ROWS, 128), F32),
            pltpu.SemaphoreType.DMA((4,)),
            pltpu.SemaphoreType.DMA((2, 2)),
            pltpu.SemaphoreType.DMA((3, 2, 2)),
            pltpu.SemaphoreType.DMA((3, 2, 2)),
            pltpu.SemaphoreType.DMA((3, 2)),
            pltpu.SemaphoreType.DMA((3, 2)),
            pltpu.SemaphoreType.DMA((5, 2)),
            pltpu.SemaphoreType.DMA((5, 2)),
            pltpu.SemaphoreType.DMA((2, 2)),
            pltpu.SemaphoreType.DMA((2, 2)),
            pltpu.VMEM((2, 2, PX, PX), F32),
            pltpu.VMEM((2, 4, 3, 2, 32, HALF), F32),
            pltpu.VMEM((2, 4, 3, 2, 8, HALF), F32),
            pltpu.VMEM((2, 4, 2, 32, HALF), F32),
            pltpu.VMEM((2, 4, 2, 8, HALF), F32),
            pltpu.VMEM((2, 4, 2, 8, HALF), F32),
            pltpu.SemaphoreType.DMA((2, 4, 5, 3)),
            pltpu.SemaphoreType.DMA((2, 4, 5, 3)),
            pltpu.VMEM((2, 2, PX, PX), F32),
            pltpu.SemaphoreType.DMA((2, 2)),
            pltpu.SemaphoreType.DMA((2, 4)),
        ],
        compiler_params=pltpu.CompilerParams(
            collective_id=0, has_side_effects=True, vmem_limit_bytes=56 * 1024 * 1024
        ),
        cost_estimate=pl.CostEstimate(flops=7 * 10**9, bytes_accessed=10**7, transcendentals=10**6),
    )(obj_re, obj_im, probe, measured, positions, table, orders)


def deliver_kernel(count, *refs):
    sources, targets, held = refs[:count], refs[count : 2 * count], refs[2 * count : 3 * count]
    in_sem, out_sem = refs[3 * count :]
    inward, outward = [], []
    for i in range(count):
        for k in range(2):
            at = (slice(None), k)
            inward.append(pltpu.make_async_copy(sources[i].at[at], held[i].at[at], in_sem.at[i, k]))
            outward.append(pltpu.make_async_copy(held[i].at[at], targets[i].at[at], out_sem.at[i, k]))
    for copy in inward:
        copy.start()
    for copy, onward in zip(inward, outward):
        copy.wait()
        onward.start()
    for copy in outward:
        copy.wait()


def delivered(arrays):
    anywhere = pl.BlockSpec(memory_space=pl.ANY)
    count = len(arrays)
    return pl.pallas_call(
        functools.partial(deliver_kernel, count),
        out_shape=tuple(jax.ShapeDtypeStruct(a.shape, a.dtype) for a in arrays),
        in_specs=[anywhere] * count,
        out_specs=(anywhere,) * count,
        scratch_shapes=[pltpu.VMEM(a.shape, a.dtype) for a in arrays]
        + [pltpu.SemaphoreType.DMA((count, 2)), pltpu.SemaphoreType.DMA((count, 2))],
        compiler_params=pltpu.CompilerParams(vmem_limit_bytes=56 * 1024 * 1024),
    )(*arrays)


def body(object_real, object_imag, probe, measured, positions):
    table, orders = constants()
    return delivered(
        gradients(object_real, object_imag, probe, measured, positions, jnp.asarray(table), jnp.asarray(orders))
    )


def solution(mesh):
    return jax.shard_map(
        body,
        mesh=mesh,
        in_specs=(
            P("tile", None, "mode", None),
            P("tile", None, "mode", None),
            P(None, "mode", None, None),
            P("tile", None, None, None),
            P("tile", None, None),
        ),
        out_specs=(
            P("tile", None, "mode", None),
            P("tile", None, "mode", None),
            P(None, "mode", None, None),
        ),
        check_vma=False,
    )
```

```python
import functools
import math

import jax
import jax.numpy as jnp
import ml_dtypes
import numpy as np
from jax import lax
from jax.experimental import pallas as pl
from jax.experimental.pallas import tpu as pltpu
from jax.sharding import PartitionSpec as P

PX = 256
HALF = PX // 2
TILE = 384
MARGIN = 64
ROWS = 96
EDGE = TILE - PX
FLOOR = 0.1
FRESNEL = 40.0
MESH = pl.DeviceIdType.MESH
F32 = jnp.float32
BF16 = jnp.bfloat16

A_LEFT, A_RIGHT, F_LEFT, F_RIGHT, B_LEFT, B_RIGHT = range(6)


def real_form(c):
    return np.block([[c.real, -c.imag], [c.imag, c.real]])


@functools.cache
def constants():
    index = np.arange(PX)
    fourier = np.exp(-2j * np.pi * (np.outer(index, index) % PX) / PX) / math.sqrt(PX)
    freq = ((index + HALF) % PX - HALF) / PX
    chirp = np.exp(-1j * np.pi * FRESNEL * freq**2)
    through = fourier.conj() @ (chirp[:, None] * fourier)
    near, far = through[:HALF, :HALF], through[:HALF, HALF:]
    pairs = [None] * 6
    moved = [(near + far) / 2, (near - far) / 2]
    split = [fourier[0::2, :HALF], fourier[1::2, :HALF]]
    pairs[A_LEFT] = [real_form(c) for c in moved]
    pairs[A_RIGHT] = [real_form(c).T for c in moved]
    pairs[F_LEFT] = [real_form(c) for c in split]
    pairs[F_RIGHT] = [real_form(c).T for c in split]
    pairs[B_LEFT] = [real_form(c.T) for c in split]
    pairs[B_RIGHT] = [real_form(c.T).T for c in split]
    table = np.array(pairs).reshape(12, PX, PX)
    high = table.astype(ml_dtypes.bfloat16)
    low = (table - high.astype(np.float64)).astype(ml_dtypes.bfloat16)
    order = np.zeros((PX, PX))
    order[np.arange(HALF), np.arange(0, PX, 2)] = 1
    order[np.arange(HALF) + HALF, np.arange(1, PX, 2)] = 1
    orders = np.array([order, order.T]).astype(ml_dtypes.bfloat16)
    return np.stack([high, low], axis=1), orders


def two_parts(x):
    high = x.astype(BF16)
    return high, (x - high.astype(F32)).astype(BF16)


def product(a, b):
    return jnp.dot(a, b, preferred_element_type=F32)


def apply_left(table, kind, sign, z):
    high, low = two_parts(z)
    c_high, c_low = table[2 * kind + sign, 0], table[2 * kind + sign, 1]
    return product(
        jnp.concatenate([c_high, c_low, c_high], axis=1),
        jnp.concatenate([high, high, low], axis=0),
    )


def apply_right(table, kind, sign, z):
    high, low = two_parts(z)
    c_high, c_low = table[2 * kind + sign, 0], table[2 * kind + sign, 1]
    return product(
        jnp.concatenate([high, high, low], axis=1),
        jnp.concatenate([c_high, c_low, c_high], axis=0),
    )


def rows_first(x):
    return x[:HALF], x[HALF:]


def lanes_first(x):
    return x[:, :HALF], x[:, HALF:]


def one_side(table, kind, re, im, left):
    halves, axis, apply = (rows_first, 0, apply_left) if left else (lanes_first, 1, apply_right)
    (r0, r1), (i0, i1) = halves(re), halves(im)
    if kind[0] != B_LEFT:
        r0, r1, i0, i1 = r0 + r1, r0 - r1, i0 + i1, i0 - i1
    which = kind[0] if left else kind[1]
    plus = apply(table, which, 0, jnp.concatenate([r0, i0], axis=axis))
    minus = apply(table, which, 1, jnp.concatenate([r1, i1], axis=axis))
    (pr, pi), (mr, mi) = halves(plus), halves(minus)
    if kind[0] != F_LEFT:
        pr, mr, pi, mi = pr + mr, pr - mr, pi + mi, pi - mi
    return jnp.concatenate([pr, mr], axis=axis), jnp.concatenate([pi, mi], axis=axis)


def both_sides(table, kind, re, im):
    re, im = one_side(table, kind, re, im, True)
    return one_side(table, kind, re, im, False)


THROUGH = (A_LEFT, A_RIGHT)
FORTH = (F_LEFT, F_RIGHT)
BACK = (B_LEFT, B_RIGHT)


def times(ar, ai, br, bi):
    return ar * br - ai * bi, ar * bi + ai * br


def kernel(
    tiles,
    obj_re,
    obj_im,
    probe_in,
    measured_in,
    positions,
    table_in,
    orders_in,
    out_re,
    out_im,
    out_probe,
    tile0,
    tile1,
    crops,
    probe,
    measured,
    table,
    orders,
    wave1,
    far,
    ipart,
    isib,
    isum,
    icross,
    factor,
    crop_grad,
    tile_grad,
    rs_send,
    rs_got,
    rs_cross,
    rs_cross_got,
    own,
    edge_send,
    edge_got,
    local_sem,
    tile_local,
    g_send,
    g_recv,
    i_send,
    i_recv,
    r_send,
    r_recv,
    e_send,
    e_recv,
    partial,
    got_a,
    got_b,
    part_b,
    y_send_buf,
    y_got,
    p_send,
    p_recv,
    total,
    out_sem,
    probe_sem,
):
    t = lax.axis_index("tile")
    m = lax.axis_index("mode")
    core = lax.rem(m, 2)
    high = m // 2
    sibling = high * 2 + (1 - core)
    across = (1 - high) * 2 + core
    diagonal = (1 - high) * 2 + (1 - core)
    left = lax.rem(t + tiles - 1, tiles)
    right = lax.rem(t + 1, tiles)
    to_sibling, to_across = (t, sibling), (t, across)
    to_left, to_right = (left, m), (right, m)

    ring = 4
    tz, ty, tx = lax.rem(t, ring), lax.rem(t // ring, 2), t // (2 * ring)
    z_peers = [(t - tz + lax.rem(tz + d, ring), m) for d in range(1, ring)]
    x_peers = [(lax.rem(t + 2 * ring * d, tiles), m) for d in range(1, ring)]
    y_peer = (t + ring * (1 - 2 * ty), m)

    barrier = pltpu.get_barrier_semaphore()
    for device in (to_sibling, to_across, to_left, to_right, y_peer, *z_peers, *x_peers):
        pl.semaphore_signal(barrier, inc=1, device_id=device, device_id_type=MESH)

    loads = [
        pltpu.make_async_copy(probe_in, probe, local_sem.at[0]),
        pltpu.make_async_copy(measured_in.at[0], measured, local_sem.at[1]),
        pltpu.make_async_copy(table_in, table, local_sem.at[2]),
        pltpu.make_async_copy(orders_in, orders, local_sem.at[3]),
    ]
    for load in loads:
        load.start()

    whole = (tile0, tile1)
    objects = (obj_re, obj_im)

    def my_rows(who):
        return pl.ds(pl.multiple_of(who * ROWS, ROWS), ROWS)

    def remote(src, dst, send, recv, device):
        return pltpu.make_async_remote_copy(
            src_ref=src, dst_ref=dst, send_sem=send, recv_sem=recv, device_id=device, device_id_type=MESH
        )

    own_copies, sends, crosses, relays = {}, {}, {}, {}
    for s in range(2):
        for p in range(2):
            src = objects[p].at[0, s]
            dst = whole[s].at[p, my_rows(m)]
            own_copies[s, p] = pltpu.make_async_copy(src, dst, tile_local.at[s, p])
            crosses[s, p] = remote(src, dst, g_send.at[0, s, p], g_recv.at[0, s, p], to_across)
            sends[s, p] = remote(src, dst, g_send.at[1, s, p], g_recv.at[1, s, p], to_sibling)
            got = whole[s].at[p, my_rows(across)]
            relays[s, p] = remote(got, got, g_send.at[2, s, p], g_recv.at[2, s, p], to_sibling)

    pl.semaphore_wait(barrier, 11)
    for s in range(2):
        for p in range(2):
            crosses[s, p].start()
    for s in range(2):
        for p in range(2):
            own_copies[s, p].start()
            sends[s, p].start()

    crop_grad[...] = jnp.zeros_like(crop_grad)
    partial[...] = jnp.zeros_like(partial)
    for load in loads:
        load.wait()
    for f in range(2):
        m_high, m_low = two_parts(measured[f])
        mixed = product(orders[0], m_high) + product(orders[0], m_low)
        m_high, m_low = two_parts(mixed)
        measured[f] = product(m_high, orders[1]) + product(m_low, orders[1])

    def tile_ready(s):
        for p in range(2):
            crosses[s, p].wait_recv()
            relays[s, p].start()
        for p in range(2):
            own_copies[s, p].wait()
            sends[s, p].wait_recv()
        for p in range(2):
            relays[s, p].wait_recv()

    row = [positions[0, f, 0] for f in range(2)]
    col = [positions[0, f, 1] for f in range(2)]

    def take_crops(s, frames=(0, 1)):
        for f in frames:
            up, back = lax.rem(TILE - row[f], TILE), lax.rem(TILE - col[f], TILE)
            for p in range(2):
                lines = pltpu.roll(whole[s][p], up, 0)[:PX]
                crops[f, s, p] = pltpu.roll(lines, back, 1)[:, :PX]

    tile_ready(0)
    take_crops(0)

    def pass_through(step, carry):
        f, mode = step // 2, lax.rem(step, 2)
        re, im = times(probe[0, mode], probe[1, mode], crops[f, 0, 0], crops[f, 0, 1])
        re, im = both_sides(table, THROUGH, re, im)
        wave1[f, mode, 0] = re
        wave1[f, mode, 1] = im
        return carry

    lax.fori_loop(0, 4, pass_through, 0, unroll=2)
    tile_ready(1)
    take_crops(1, (0,))

    def far_fields(f):
        ipart[f] = jnp.zeros_like(ipart[f])

        def step(mode, carry):
            re, im = times(wave1[f, mode, 0], wave1[f, mode, 1], crops[f, 1, 0], crops[f, 1, 1])
            re, im = both_sides(table, FORTH, re, im)
            far[f, mode, 0] = re
            far[f, mode, 1] = im
            ipart[f] += re * re + im * im
            return carry

        lax.fori_loop(0, 2, step, 0, unroll=True)

    def half_rows(who):
        return pl.ds(pl.multiple_of(who * HALF, HALF), HALF)

    to_pair = [
        remote(ipart.at[f, half_rows(1 - core)], isib.at[f], i_send.at[0, f], i_recv.at[0, f], to_sibling) for f in range(2)
    ]
    to_other = [remote(isum.at[f], icross.at[f], i_send.at[1, f], i_recv.at[1, f], to_across) for f in range(2)]
    to_share = [
        remote(
            factor.at[f, half_rows(core)],
            factor.at[f, half_rows(core)],
            i_send.at[2, f],
            i_recv.at[2, f],
            to_sibling,
        )
        for f in range(2)
    ]

    def pair_sum(f):
        to_pair[f].wait_recv()
        isum[f] = ipart[f, half_rows(core), :] + isib[f]
        to_other[f].start()

    def factors(f):
        to_other[f].wait_recv()
        whole_sum = isum[f] + icross[f]
        factor[f, half_rows(core), :] = 2.0 - 2.0 * measured[f, half_rows(core), :] / jnp.sqrt(whole_sum + FLOOR)
        to_share[f].start()

    far_fields(0)
    to_pair[0].start()
    take_crops(1, (1,))
    far_fields(1)
    to_pair[1].start()
    pair_sum(0)
    pair_sum(1)
    factors(0)

    def over(steps, body):
        def step(k, carry):
            f, mode = steps[0]
            if len(steps) > 1:
                f = f + k * (steps[1][0] - f)
                mode = mode + k * (steps[1][1] - mode)
            body(f, mode)
            return carry

        lax.fori_loop(0, len(steps), step, 0)

    def slice_1_step(f, mode):
        weight = factor[f]
        re, im = weight * far[f, mode, 0], -(weight * far[f, mode, 1])
        re, im = both_sides(table, BACK, re, im)
        gr, gi = times(wave1[f, mode, 0], wave1[f, mode, 1], re, im)
        crop_grad[f, 1, 0] += gr
        crop_grad[f, 1, 1] -= gi
        re, im = times(crops[f, 1, 0], crops[f, 1, 1], re, im)
        far[f, mode, 0] = re
        far[f, mode, 1] = im

    def probe_step(f, mode):
        re, im = both_sides(table, THROUGH, far[f, mode, 0], far[f, mode, 1])
        gr, gi = times(probe[0, mode], probe[1, mode], re, im)
        crop_grad[f, 0, 0] += gr
        crop_grad[f, 0, 1] -= gi
        gr, gi = times(crops[f, 0, 0], crops[f, 0, 1], re, im)
        partial[mode, 0] += gr
        partial[mode, 1] -= gi

    def both_steps(f, mode):
        slice_1_step(f, mode)
        probe_step(f, mode)

    low_lanes = lax.broadcasted_iota(jnp.int32, (TILE, 128), 1) < MARGIN

    def place(s, f):
        for p in range(2):
            wide = jnp.concatenate([crop_grad[f, s, p], jnp.zeros((PX, EDGE), F32)], axis=1)
            wide = pltpu.roll(wide, col[f], 1)
            wide = jnp.concatenate([wide, jnp.zeros((EDGE, TILE), F32)], axis=0)
            wide = pltpu.roll(wide, row[f], 0)
            first, middle, last = wide[:, :128], wide[:, 128:256], wide[:, 256:]
            ends, between = jnp.where(low_lanes, first, last), jnp.where(low_lanes, last, first)
            blocks = jnp.concatenate([ends, middle, between], axis=1)
            tile_grad[s, p] = blocks if f == 0 else tile_grad[s, p] + blocks

    def piece(s, p, who):
        return tile_grad[s, p, my_rows(who), :]

    parts = (pl.ds(0, 128), pl.ds(128, TILE - 128))
    rs_pair, rs_over, rs_edge, outward = {}, {}, {}, {}
    for s in range(2):
        for k in range(2):
            rs_pair[s, k] = remote(rs_send.at[s, k], rs_got.at[s, k], r_send.at[k, s], r_recv.at[k, s], to_sibling)
        for k in range(2):
            rs_over[s, k] = remote(
                rs_cross.at[s, :, :, parts[k]],
                rs_cross_got.at[s, :, :, parts[k]],
                r_send.at[2 + k, s],
                r_recv.at[2 + k, s],
                to_across,
            )
        rs_edge[s, 0] = remote(edge_send.at[s, 0], edge_got.at[s, 0], e_send.at[0, s], e_recv.at[0, s], to_right)
        rs_edge[s, 1] = remote(edge_send.at[s, 1], edge_got.at[s, 1], e_send.at[1, s], e_recv.at[1, s], to_left)
        for p in range(2):
            outward[s, p] = pltpu.make_async_copy(own.at[s, p], (out_re, out_im)[p].at[0, s], out_sem.at[s, p])

    def reduce_1(s):
        place(s, 1)
        for k, who in enumerate((diagonal, sibling)):
            for p in range(2):
                rs_send[s, k, p] = piece(s, p, who)
            rs_pair[s, k].start()

    def reduce_2(s):
        rs_pair[s, 0].wait_recv()
        for p in range(2):
            rs_cross[s, p] = piece(s, p, across) + rs_got[s, 0, p]
        if s == 1:
            rs_over[s, 0].start()
        rs_pair[s, 1].wait_recv()
        for p in range(2):
            own[s, p] = piece(s, p, m) + rs_got[s, 1, p]

    lane = lax.broadcasted_iota(jnp.int32, (ROWS, 128), 1)
    lower = lane < MARGIN

    def reduce_3(s):
        rs_over[s, 0].wait_recv()
        ends = [own[s, p, :, :128] + rs_cross_got[s, p, :, :128] for p in range(2)]
        for p in range(2):
            own[s, p, :, :128] = ends[p]
        edge_send[s, 0] = jnp.where(lower, pltpu.roll(ends[0], MARGIN, 1), ends[1])
        edge_send[s, 1] = jnp.where(lower, ends[0], pltpu.roll(ends[1], MARGIN, 1))
        rs_edge[s, 0].start()
        rs_edge[s, 1].start()

    def reduce_4(s):
        rs_edge[s, 0].wait_recv()
        rs_edge[s, 1].wait_recv()
        before, after = edge_got[s, 0], edge_got[s, 1]
        at_first = jnp.logical_and(lower, t > 0)
        at_last = jnp.logical_and(jnp.logical_not(lower), t < tiles - 1)
        befores = (before, pltpu.roll(before, MARGIN, 1))
        afters = (pltpu.roll(after, MARGIN, 1), after)
        rs_over[s, 1].wait_recv()
        for p in range(2):
            ends = own[s, p, :, :128] + jnp.where(at_first, befores[p], 0.0) + jnp.where(at_last, afters[p], 0.0)
            between = own[s, p, :, 256:] + rs_cross_got[s, p, :, 256:]
            own[s, p, :, 128:256] += rs_cross_got[s, p, :, 128:256]
            own[s, p, :, :128] = jnp.where(lower, ends, between)
            own[s, p, :, 256:] = jnp.where(lower, between, ends)
            outward[s, p].start()

    axes = (((tz, z_peers), (tx, x_peers)), ((tx, x_peers), (tz, z_peers)))

    def block(length, index, base=0):
        return pl.ds(pl.multiple_of(base + index * length, length), length)

    scatter_a, scatter_b, swap_y, gather_b, gather_a, probe_out = {}, {}, {}, {}, {}, {}
    chunks = [(c, h) for h in range(2) for c in range(2)]
    for c, h in chunks:
        (ia, peers_a), (ib, peers_b) = axes[c]
        for k in range(ring - 1):
            ja, jb = lax.rem(ia + k + 1, ring), lax.rem(ib + k + 1, ring)
            sems = [(p_send.at[c, h, i, k], p_recv.at[c, h, i, k]) for i in range(4)]
            scatter_a[c, h, k] = remote(
                partial.at[c, :, block(32, ja, h * HALF)], got_a.at[c, h, k], *sems[0], peers_a[k]
            )
            scatter_b[c, h, k] = remote(part_b.at[c, h, :, block(8, jb)], got_b.at[c, h, k], *sems[1], peers_b[k])
            mine_b = total.at[:, c, block(8, ib, h * HALF + ia * 32)]
            gather_b[c, h, k] = remote(mine_b, mine_b, *sems[2], peers_b[k])
            mine_a = total.at[:, c, block(32, ia, h * HALF)]
            gather_a[c, h, k] = remote(mine_a, mine_a, *sems[3], peers_a[k])
        swap_y[c, h] = remote(y_send_buf.at[c, h], y_got.at[c, h], p_send.at[c, h, 4, 0], p_recv.at[c, h, 4, 0], y_peer)
        some = pl.ds(h * HALF, HALF)
        probe_out[c, h] = pltpu.make_async_copy(total.at[:, c, some], out_probe.at[:, c, some], probe_sem.at[c, h])

    def send_all(group, c, h):
        for k in (1, 0, 2):
            group[c, h, k].start()

    def take_all(group, c, h):
        for k in range(3):
            group[c, h, k].wait_recv()

    def probe_1(c):
        for h in range(2):
            send_all(scatter_a, c, h)

    def probe_2(c, h):
        ia = axes[c][0][0]
        take_all(scatter_a, c, h)
        got = got_a[c, h, 0] + got_a[c, h, 1] + got_a[c, h, 2]
        part_b[c, h] = partial[c, :, block(32, ia, h * HALF), :] + got
        send_all(scatter_b, c, h)

    def probe_3(c, h):
        ib = axes[c][1][0]
        take_all(scatter_b, c, h)
        got = got_b[c, h, 0] + got_b[c, h, 1] + got_b[c, h, 2]
        y_send_buf[c, h] = part_b[c, h, :, block(8, ib), :] + got
        swap_y[c, h].start()

    def probe_4(c, h):
        ia, ib = axes[c][0][0], axes[c][1][0]
        swap_y[c, h].wait_recv()
        total[:, c, block(8, ib, h * HALF + ia * 32), :] = y_send_buf[c, h] + y_got[c, h]
        send_all(gather_b, c, h)

    def probe_5(c, h):
        take_all(gather_b, c, h)
        send_all(gather_a, c, h)

    def probe_6(c, h):
        take_all(gather_a, c, h)
        probe_out[c, h].start()

    def each(step, h):
        for c in range(2):
            step(c, h)

    to_share[0].wait_recv()
    over([(0, 0)], both_steps)
    factors(1)
    over([(0, 1)], both_steps)
    place(1, 0)
    place(0, 0)
    to_share[1].wait_recv()
    over([(1, 0)], both_steps)
    probe_1(0)
    over([(1, 1)], both_steps)
    probe_1(1)
    reduce_1(1)
    reduce_1(0)
    reduce_2(1)
    reduce_2(0)
    each(probe_2, 0)
    each(probe_2, 1)
    each(probe_3, 0)
    rs_over[0, 0].start()
    reduce_3(1)
    each(probe_3, 1)
    rs_over[1, 1].start()
    rs_over[0, 1].start()
    each(probe_4, 0)
    reduce_3(0)
    each(probe_4, 1)
    each(probe_5, 0)
    each(probe_5, 1)
    reduce_4(1)
    each(probe_6, 0)
    reduce_4(0)
    each(probe_6, 1)

    for group in (probe_out, outward):
        for copy in group.values():
            copy.wait()
    for group in (scatter_a, scatter_b, swap_y, gather_b, gather_a):
        for copy in group.values():
            copy.wait_send()
    for group in (sends, crosses, relays, rs_pair, rs_over, rs_edge):
        for copy in group.values():
            copy.wait_send()
    for group in (to_pair, to_other, to_share):
        for copy in group:
            copy.wait_send()


def gradients(obj_re, obj_im, probe, measured, positions, table, orders):
    tiles = lax.axis_size("tile")
    shape = jax.ShapeDtypeStruct
    anywhere = pl.BlockSpec(memory_space=pl.ANY)
    return pl.pallas_call(
        functools.partial(kernel, tiles),
        out_shape=(shape(obj_re.shape, F32), shape(obj_im.shape, F32), shape(probe.shape, F32)),
        in_specs=[anywhere, anywhere, anywhere, anywhere, pl.BlockSpec(memory_space=pltpu.SMEM), anywhere, anywhere],
        out_specs=(anywhere, anywhere, anywhere),
        scratch_shapes=[
            pltpu.VMEM((2, TILE, TILE), F32),
            pltpu.VMEM((2, TILE, TILE), F32),
            pltpu.VMEM((2, 2, 2, PX, PX), F32),
            pltpu.VMEM((2, 2, PX, PX), F32),
            pltpu.VMEM((2, PX, PX), F32),
            pltpu.VMEM(table.shape, BF16),
            pltpu.VMEM(orders.shape, BF16),
            pltpu.VMEM((2, 2, 2, PX, PX), F32),
            pltpu.VMEM((2, 2, 2, PX, PX), F32),
            pltpu.VMEM((2, PX, PX), F32),
            pltpu.VMEM((2, HALF, PX), F32),
            pltpu.VMEM((2, HALF, PX), F32),
            pltpu.VMEM((2, HALF, PX), F32),
            pltpu.VMEM((2, PX, PX), F32),
            pltpu.VMEM((2, 2, 2, PX, PX), F32),
            pltpu.VMEM((2, 2, TILE, TILE), F32),
            pltpu.VMEM((2, 2, 2, ROWS, TILE), F32),
            pltpu.VMEM((2, 2, 2, ROWS, TILE), F32),
            pltpu.VMEM((2, 2, ROWS, TILE), F32),
            pltpu.VMEM((2, 2, ROWS, TILE), F32),
            pltpu.VMEM((2, 2, ROWS, TILE), F32),
            pltpu.VMEM((2, 2, ROWS, 128), F32),
            pltpu.VMEM((2, 2, ROWS, 128), F32),
            pltpu.SemaphoreType.DMA((4,)),
            pltpu.SemaphoreType.DMA((2, 2)),
            pltpu.SemaphoreType.DMA((3, 2, 2)),
            pltpu.SemaphoreType.DMA((3, 2, 2)),
            pltpu.SemaphoreType.DMA((3, 2)),
            pltpu.SemaphoreType.DMA((3, 2)),
            pltpu.SemaphoreType.DMA((5, 2)),
            pltpu.SemaphoreType.DMA((5, 2)),
            pltpu.SemaphoreType.DMA((2, 2)),
            pltpu.SemaphoreType.DMA((2, 2)),
            pltpu.VMEM((2, 2, PX, PX), F32),
            pltpu.VMEM((2, 2, 3, 2, 32, PX), F32),
            pltpu.VMEM((2, 2, 3, 2, 8, PX), F32),
            pltpu.VMEM((2, 2, 2, 32, PX), F32),
            pltpu.VMEM((2, 2, 2, 8, PX), F32),
            pltpu.VMEM((2, 2, 2, 8, PX), F32),
            pltpu.SemaphoreType.DMA((2, 2, 5, 3)),
            pltpu.SemaphoreType.DMA((2, 2, 5, 3)),
            pltpu.VMEM((2, 2, PX, PX), F32),
            pltpu.SemaphoreType.DMA((2, 2)),
            pltpu.SemaphoreType.DMA((2, 2)),
        ],
        compiler_params=pltpu.CompilerParams(
            collective_id=0, has_side_effects=True, vmem_limit_bytes=56 * 1024 * 1024
        ),
        cost_estimate=pl.CostEstimate(flops=7 * 10**9, bytes_accessed=10**7, transcendentals=10**6),
    )(obj_re, obj_im, probe, measured, positions, table, orders)


def deliver_kernel(count, *refs):
    sources, targets, held = refs[:count], refs[count : 2 * count], refs[2 * count : 3 * count]
    in_sem, out_sem = refs[3 * count :]
    inward, outward = [], []
    for i in range(count):
        for k in range(2):
            at = (slice(None), k)
            inward.append(pltpu.make_async_copy(sources[i].at[at], held[i].at[at], in_sem.at[i, k]))
            outward.append(pltpu.make_async_copy(held[i].at[at], targets[i].at[at], out_sem.at[i, k]))
    for copy in inward:
        copy.start()
    for copy, onward in zip(inward, outward):
        copy.wait()
        onward.start()
    for copy in outward:
        copy.wait()


def delivered(arrays):
    anywhere = pl.BlockSpec(memory_space=pl.ANY)
    count = len(arrays)
    return pl.pallas_call(
        functools.partial(deliver_kernel, count),
        out_shape=tuple(jax.ShapeDtypeStruct(a.shape, a.dtype) for a in arrays),
        in_specs=[anywhere] * count,
        out_specs=(anywhere,) * count,
        scratch_shapes=[pltpu.VMEM(a.shape, a.dtype) for a in arrays]
        + [pltpu.SemaphoreType.DMA((count, 2)), pltpu.SemaphoreType.DMA((count, 2))],
        compiler_params=pltpu.CompilerParams(vmem_limit_bytes=56 * 1024 * 1024),
    )(*arrays)


def body(object_real, object_imag, probe, measured, positions):
    table, orders = constants()
    return delivered(
        gradients(object_real, object_imag, probe, measured, positions, jnp.asarray(table), jnp.asarray(orders))
    )


def solution(mesh):
    return jax.shard_map(
        body,
        mesh=mesh,
        in_specs=(
            P("tile", None, "mode", None),
            P("tile", None, "mode", None),
            P(None, "mode", None, None),
            P("tile", None, None, None),
            P("tile", None, None),
        ),
        out_specs=(
            P("tile", None, "mode", None),
            P("tile", None, "mode", None),
            P(None, "mode", None, None),
        ),
        check_vma=False,
    )
```

```python
import functools
import math

import jax
import jax.numpy as jnp
import ml_dtypes
import numpy as np
from jax import lax
from jax.experimental import pallas as pl
from jax.experimental.pallas import tpu as pltpu
from jax.sharding import PartitionSpec as P

PX = 256
HALF = PX // 2
TILE = 384
MARGIN = 64
ROWS = 96
EDGE = TILE - PX
FLOOR = 0.1
FRESNEL = 40.0
MESH = pl.DeviceIdType.MESH
F32 = jnp.float32
BF16 = jnp.bfloat16

A_LEFT, A_RIGHT, F_LEFT, F_RIGHT, B_LEFT, B_RIGHT = range(6)


def real_form(c):
    return np.block([[c.real, -c.imag], [c.imag, c.real]])


@functools.cache
def constants():
    index = np.arange(PX)
    fourier = np.exp(-2j * np.pi * (np.outer(index, index) % PX) / PX) / math.sqrt(PX)
    freq = ((index + HALF) % PX - HALF) / PX
    chirp = np.exp(-1j * np.pi * FRESNEL * freq**2)
    through = fourier.conj() @ (chirp[:, None] * fourier)
    near, far = through[:HALF, :HALF], through[:HALF, HALF:]
    pairs = [None] * 6
    moved = [(near + far) / 2, (near - far) / 2]
    split = [fourier[0::2, :HALF], fourier[1::2, :HALF]]
    pairs[A_LEFT] = [real_form(c) for c in moved]
    pairs[A_RIGHT] = [real_form(c).T for c in moved]
    pairs[F_LEFT] = [real_form(c) for c in split]
    pairs[F_RIGHT] = [real_form(c).T for c in split]
    pairs[B_LEFT] = [real_form(c.T) for c in split]
    pairs[B_RIGHT] = [real_form(c.T).T for c in split]
    table = np.array(pairs).reshape(12, PX, PX)
    high = table.astype(ml_dtypes.bfloat16)
    low = (table - high.astype(np.float64)).astype(ml_dtypes.bfloat16)
    order = np.zeros((PX, PX))
    order[np.arange(HALF), np.arange(0, PX, 2)] = 1
    order[np.arange(HALF) + HALF, np.arange(1, PX, 2)] = 1
    orders = np.array([order, order.T]).astype(ml_dtypes.bfloat16)
    return np.stack([high, low], axis=1), orders


def two_parts(x):
    high = x.astype(BF16)
    return high, (x - high.astype(F32)).astype(BF16)


def product(a, b):
    return jnp.dot(a, b, preferred_element_type=F32)


def apply_left(table, kind, sign, z):
    high, low = two_parts(z)
    c_high, c_low = table[2 * kind + sign, 0], table[2 * kind + sign, 1]
    return product(
        jnp.concatenate([c_high, c_low, c_high], axis=1),
        jnp.concatenate([high, high, low], axis=0),
    )


def apply_right(table, kind, sign, z):
    high, low = two_parts(z)
    c_high, c_low = table[2 * kind + sign, 0], table[2 * kind + sign, 1]
    return product(
        jnp.concatenate([high, high, low], axis=1),
        jnp.concatenate([c_high, c_low, c_high], axis=0),
    )


def rows_first(x):
    return x[:HALF], x[HALF:]


def lanes_first(x):
    return x[:, :HALF], x[:, HALF:]


def one_side(table, kind, re, im, left):
    halves, axis, apply = (rows_first, 0, apply_left) if left else (lanes_first, 1, apply_right)
    (r0, r1), (i0, i1) = halves(re), halves(im)
    if kind[0] != B_LEFT:
        r0, r1, i0, i1 = r0 + r1, r0 - r1, i0 + i1, i0 - i1
    which = kind[0] if left else kind[1]
    plus = apply(table, which, 0, jnp.concatenate([r0, i0], axis=axis))
    minus = apply(table, which, 1, jnp.concatenate([r1, i1], axis=axis))
    (pr, pi), (mr, mi) = halves(plus), halves(minus)
    if kind[0] != F_LEFT:
        pr, mr, pi, mi = pr + mr, pr - mr, pi + mi, pi - mi
    return jnp.concatenate([pr, mr], axis=axis), jnp.concatenate([pi, mi], axis=axis)


def both_sides(table, kind, re, im):
    re, im = one_side(table, kind, re, im, True)
    return one_side(table, kind, re, im, False)


THROUGH = (A_LEFT, A_RIGHT)
FORTH = (F_LEFT, F_RIGHT)
BACK = (B_LEFT, B_RIGHT)


def times(ar, ai, br, bi):
    return ar * br - ai * bi, ar * bi + ai * br


def kernel(
    tiles,
    obj_re,
    obj_im,
    probe_in,
    measured_in,
    positions,
    table_in,
    orders_in,
    out_re,
    out_im,
    out_probe,
    tile0,
    tile1,
    crops,
    probe,
    measured,
    table,
    orders,
    wave1,
    far,
    ipart,
    isib,
    isum,
    icross,
    factor,
    crop_grad,
    tile_grad,
    rs_send,
    rs_got,
    rs_cross,
    rs_cross_got,
    own,
    edge_send,
    edge_got,
    local_sem,
    tile_local,
    g_send,
    g_recv,
    i_send,
    i_recv,
    r_send,
    r_recv,
    e_send,
    e_recv,
    partial,
    got_a,
    got_b,
    part_b,
    y_send_buf,
    y_got,
    p_send,
    p_recv,
    total,
    out_sem,
    probe_sem,
):
    t = lax.axis_index("tile")
    m = lax.axis_index("mode")
    core = lax.rem(m, 2)
    high = m // 2
    sibling = high * 2 + (1 - core)
    across = (1 - high) * 2 + core
    diagonal = (1 - high) * 2 + (1 - core)
    left = lax.rem(t + tiles - 1, tiles)
    right = lax.rem(t + 1, tiles)
    to_sibling, to_across = (t, sibling), (t, across)
    to_left, to_right = (left, m), (right, m)

    ring = 4
    tz, ty, tx = lax.rem(t, ring), lax.rem(t // ring, 2), t // (2 * ring)
    z_peers = [(t - tz + lax.rem(tz + d, ring), m) for d in range(1, ring)]
    x_peers = [(lax.rem(t + 2 * ring * d, tiles), m) for d in range(1, ring)]
    y_peer = (t + ring * (1 - 2 * ty), m)

    barrier = pltpu.get_barrier_semaphore()
    for device in (to_sibling, to_across, to_left, to_right, y_peer, *z_peers, *x_peers):
        pl.semaphore_signal(barrier, inc=1, device_id=device, device_id_type=MESH)

    loads = [
        pltpu.make_async_copy(probe_in, probe, local_sem.at[0]),
        pltpu.make_async_copy(measured_in.at[0], measured, local_sem.at[1]),
        pltpu.make_async_copy(table_in, table, local_sem.at[2]),
        pltpu.make_async_copy(orders_in, orders, local_sem.at[3]),
    ]
    for load in loads:
        load.start()

    whole = (tile0, tile1)
    objects = (obj_re, obj_im)

    def my_rows(who):
        return pl.ds(pl.multiple_of(who * ROWS, ROWS), ROWS)

    def remote(src, dst, send, recv, device):
        return pltpu.make_async_remote_copy(
            src_ref=src, dst_ref=dst, send_sem=send, recv_sem=recv, device_id=device, device_id_type=MESH
        )

    own_copies, sends, crosses, relays = {}, {}, {}, {}
    for s in range(2):
        for p in range(2):
            src = objects[p].at[0, s]
            dst = whole[s].at[p, my_rows(m)]
            own_copies[s, p] = pltpu.make_async_copy(src, dst, tile_local.at[s, p])
            crosses[s, p] = remote(src, dst, g_send.at[0, s, p], g_recv.at[0, s, p], to_across)
            sends[s, p] = remote(src, dst, g_send.at[1, s, p], g_recv.at[1, s, p], to_sibling)
            got = whole[s].at[p, my_rows(across)]
            relays[s, p] = remote(got, got, g_send.at[2, s, p], g_recv.at[2, s, p], to_sibling)

    pl.semaphore_wait(barrier, 11)
    for s in range(2):
        for p in range(2):
            crosses[s, p].start()
    for s in range(2):
        for p in range(2):
            own_copies[s, p].start()
            sends[s, p].start()

    crop_grad[...] = jnp.zeros_like(crop_grad)
    partial[...] = jnp.zeros_like(partial)
    for load in loads:
        load.wait()
    for f in range(2):
        m_high, m_low = two_parts(measured[f])
        mixed = product(orders[0], m_high) + product(orders[0], m_low)
        m_high, m_low = two_parts(mixed)
        measured[f] = product(m_high, orders[1]) + product(m_low, orders[1])

    def tile_ready(s):
        for p in range(2):
            crosses[s, p].wait_recv()
            relays[s, p].start()
        for p in range(2):
            own_copies[s, p].wait()
            sends[s, p].wait_recv()
        for p in range(2):
            relays[s, p].wait_recv()

    row = [positions[0, f, 0] for f in range(2)]
    col = [positions[0, f, 1] for f in range(2)]

    def take_crops(s, frames=(0, 1)):
        for f in frames:
            up, back = lax.rem(TILE - row[f], TILE), lax.rem(TILE - col[f], TILE)
            for p in range(2):
                lines = pltpu.roll(whole[s][p], up, 0)[:PX]
                crops[f, s, p] = pltpu.roll(lines, back, 1)[:, :PX]

    tile_ready(0)
    take_crops(0)

    def pass_through(step, carry):
        f, mode = step // 2, lax.rem(step, 2)
        re, im = times(probe[0, mode], probe[1, mode], crops[f, 0, 0], crops[f, 0, 1])
        re, im = both_sides(table, THROUGH, re, im)
        wave1[f, mode, 0] = re
        wave1[f, mode, 1] = im
        return carry

    lax.fori_loop(0, 4, pass_through, 0, unroll=2)
    tile_ready(1)
    take_crops(1, (0,))

    def far_fields(f):
        ipart[f] = jnp.zeros_like(ipart[f])

        def step(mode, carry):
            re, im = times(wave1[f, mode, 0], wave1[f, mode, 1], crops[f, 1, 0], crops[f, 1, 1])
            re, im = both_sides(table, FORTH, re, im)
            far[f, mode, 0] = re
            far[f, mode, 1] = im
            ipart[f] += re * re + im * im
            return carry

        lax.fori_loop(0, 2, step, 0, unroll=True)

    def half_rows(who):
        return pl.ds(pl.multiple_of(who * HALF, HALF), HALF)

    to_pair = [
        remote(ipart.at[f, half_rows(1 - core)], isib.at[f], i_send.at[0, f], i_recv.at[0, f], to_sibling) for f in range(2)
    ]
    to_other = [remote(isum.at[f], icross.at[f], i_send.at[1, f], i_recv.at[1, f], to_across) for f in range(2)]
    to_share = [
        remote(
            factor.at[f, half_rows(core)],
            factor.at[f, half_rows(core)],
            i_send.at[2, f],
            i_recv.at[2, f],
            to_sibling,
        )
        for f in range(2)
    ]

    def pair_sum(f):
        to_pair[f].wait_recv()
        isum[f] = ipart[f, half_rows(core), :] + isib[f]
        to_other[f].start()

    def factors(f):
        to_other[f].wait_recv()
        whole_sum = isum[f] + icross[f]
        factor[f, half_rows(core), :] = 2.0 - 2.0 * measured[f, half_rows(core), :] / jnp.sqrt(whole_sum + FLOOR)
        to_share[f].start()

    far_fields(0)
    to_pair[0].start()
    take_crops(1, (1,))
    far_fields(1)
    to_pair[1].start()
    pair_sum(0)
    pair_sum(1)
    factors(0)

    def over(steps, body):
        def step(k, carry):
            f, mode = steps[0]
            if len(steps) > 1:
                f = f + k * (steps[1][0] - f)
                mode = mode + k * (steps[1][1] - mode)
            body(f, mode)
            return carry

        lax.fori_loop(0, len(steps), step, 0)

    def slice_1_step(f, mode):
        weight = factor[f]
        re, im = weight * far[f, mode, 0], -(weight * far[f, mode, 1])
        re, im = both_sides(table, BACK, re, im)
        gr, gi = times(wave1[f, mode, 0], wave1[f, mode, 1], re, im)
        crop_grad[f, 1, 0] += gr
        crop_grad[f, 1, 1] -= gi
        re, im = times(crops[f, 1, 0], crops[f, 1, 1], re, im)
        far[f, mode, 0] = re
        far[f, mode, 1] = im

    def probe_step(f, mode):
        re, im = both_sides(table, THROUGH, far[f, mode, 0], far[f, mode, 1])
        gr, gi = times(probe[0, mode], probe[1, mode], re, im)
        crop_grad[f, 0, 0] += gr
        crop_grad[f, 0, 1] -= gi
        gr, gi = times(crops[f, 0, 0], crops[f, 0, 1], re, im)
        partial[mode, 0] += gr
        partial[mode, 1] -= gi

    def both_steps(f, mode):
        slice_1_step(f, mode)
        probe_step(f, mode)

    low_lanes = lax.broadcasted_iota(jnp.int32, (TILE, 128), 1) < MARGIN

    def place(s, f):
        for p in range(2):
            wide = jnp.concatenate([crop_grad[f, s, p], jnp.zeros((PX, EDGE), F32)], axis=1)
            wide = pltpu.roll(wide, col[f], 1)
            wide = jnp.concatenate([wide, jnp.zeros((EDGE, TILE), F32)], axis=0)
            wide = pltpu.roll(wide, row[f], 0)
            first, middle, last = wide[:, :128], wide[:, 128:256], wide[:, 256:]
            ends, between = jnp.where(low_lanes, first, last), jnp.where(low_lanes, last, first)
            blocks = jnp.concatenate([ends, middle, between], axis=1)
            tile_grad[s, p] = blocks if f == 0 else tile_grad[s, p] + blocks

    def piece(s, p, who):
        return tile_grad[s, p, my_rows(who), :]

    parts = (pl.ds(0, 128), pl.ds(128, TILE - 128))
    rs_pair, rs_over, rs_edge, outward = {}, {}, {}, {}
    for s in range(2):
        for k in range(2):
            rs_pair[s, k] = remote(rs_send.at[s, k], rs_got.at[s, k], r_send.at[k, s], r_recv.at[k, s], to_sibling)
        for k in range(2):
            rs_over[s, k] = remote(
                rs_cross.at[s, :, :, parts[k]],
                rs_cross_got.at[s, :, :, parts[k]],
                r_send.at[2 + k, s],
                r_recv.at[2 + k, s],
                to_across,
            )
        rs_edge[s, 0] = remote(edge_send.at[s, 0], edge_got.at[s, 0], e_send.at[0, s], e_recv.at[0, s], to_right)
        rs_edge[s, 1] = remote(edge_send.at[s, 1], edge_got.at[s, 1], e_send.at[1, s], e_recv.at[1, s], to_left)
        for p in range(2):
            outward[s, p] = pltpu.make_async_copy(own.at[s, p], (out_re, out_im)[p].at[0, s], out_sem.at[s, p])

    def reduce_1(s):
        place(s, 1)
        for k, who in enumerate((diagonal, sibling)):
            for p in range(2):
                rs_send[s, k, p] = piece(s, p, who)
            rs_pair[s, k].start()

    def reduce_2(s):
        rs_pair[s, 0].wait_recv()
        for p in range(2):
            rs_cross[s, p] = piece(s, p, across) + rs_got[s, 0, p]
        rs_over[s, 0].start()
        rs_pair[s, 1].wait_recv()
        for p in range(2):
            own[s, p] = piece(s, p, m) + rs_got[s, 1, p]

    lane = lax.broadcasted_iota(jnp.int32, (ROWS, 128), 1)
    lower = lane < MARGIN

    def reduce_3(s):
        rs_over[s, 0].wait_recv()
        ends = [own[s, p, :, :128] + rs_cross_got[s, p, :, :128] for p in range(2)]
        for p in range(2):
            own[s, p, :, :128] = ends[p]
        edge_send[s, 0] = jnp.where(lower, pltpu.roll(ends[0], MARGIN, 1), ends[1])
        edge_send[s, 1] = jnp.where(lower, ends[0], pltpu.roll(ends[1], MARGIN, 1))
        rs_edge[s, 0].start()
        rs_edge[s, 1].start()

    def reduce_4(s):
        rs_edge[s, 0].wait_recv()
        rs_edge[s, 1].wait_recv()
        before, after = edge_got[s, 0], edge_got[s, 1]
        at_first = jnp.logical_and(lower, t > 0)
        at_last = jnp.logical_and(jnp.logical_not(lower), t < tiles - 1)
        befores = (before, pltpu.roll(before, MARGIN, 1))
        afters = (pltpu.roll(after, MARGIN, 1), after)
        rs_over[s, 1].wait_recv()
        for p in range(2):
            ends = own[s, p, :, :128] + jnp.where(at_first, befores[p], 0.0) + jnp.where(at_last, afters[p], 0.0)
            between = own[s, p, :, 256:] + rs_cross_got[s, p, :, 256:]
            own[s, p, :, 128:256] += rs_cross_got[s, p, :, 128:256]
            own[s, p, :, :128] = jnp.where(lower, ends, between)
            own[s, p, :, 256:] = jnp.where(lower, between, ends)
            outward[s, p].start()

    axes = (((tz, z_peers), (tx, x_peers)), ((tx, x_peers), (tz, z_peers)))

    def block(length, index, base=0):
        return pl.ds(pl.multiple_of(base + index * length, length), length)

    scatter_a, scatter_b, swap_y, gather_b, gather_a, probe_out = {}, {}, {}, {}, {}, {}
    chunks = [(c, h) for h in range(2) for c in range(2)]
    for c, h in chunks:
        (ia, peers_a), (ib, peers_b) = axes[c]
        for k in range(ring - 1):
            ja, jb = lax.rem(ia + k + 1, ring), lax.rem(ib + k + 1, ring)
            sems = [(p_send.at[c, h, i, k], p_recv.at[c, h, i, k]) for i in range(4)]
            scatter_a[c, h, k] = remote(
                partial.at[c, :, block(32, ja, h * HALF)], got_a.at[c, h, k], *sems[0], peers_a[k]
            )
            scatter_b[c, h, k] = remote(part_b.at[c, h, :, block(8, jb)], got_b.at[c, h, k], *sems[1], peers_b[k])
            mine_b = total.at[:, c, block(8, ib, h * HALF + ia * 32)]
            gather_b[c, h, k] = remote(mine_b, mine_b, *sems[2], peers_b[k])
            mine_a = total.at[:, c, block(32, ia, h * HALF)]
            gather_a[c, h, k] = remote(mine_a, mine_a, *sems[3], peers_a[k])
        swap_y[c, h] = remote(y_send_buf.at[c, h], y_got.at[c, h], p_send.at[c, h, 4, 0], p_recv.at[c, h, 4, 0], y_peer)
        some = pl.ds(h * HALF, HALF)
        probe_out[c, h] = pltpu.make_async_copy(total.at[:, c, some], out_probe.at[:, c, some], probe_sem.at[c, h])

    def send_all(group, c, h):
        for k in (1, 0, 2):
            group[c, h, k].start()

    def take_all(group, c, h):
        for k in range(3):
            group[c, h, k].wait_recv()

    def probe_1(c):
        for h in range(2):
            send_all(scatter_a, c, h)

    def probe_2(c, h):
        ia = axes[c][0][0]
        take_all(scatter_a, c, h)
        got = got_a[c, h, 0] + got_a[c, h, 1] + got_a[c, h, 2]
        part_b[c, h] = partial[c, :, block(32, ia, h * HALF), :] + got
        send_all(scatter_b, c, h)

    def probe_3(c, h):
        ib = axes[c][1][0]
        take_all(scatter_b, c, h)
        got = got_b[c, h, 0] + got_b[c, h, 1] + got_b[c, h, 2]
        y_send_buf[c, h] = part_b[c, h, :, block(8, ib), :] + got
        swap_y[c, h].start()

    def probe_4(c, h):
        ia, ib = axes[c][0][0], axes[c][1][0]
        swap_y[c, h].wait_recv()
        total[:, c, block(8, ib, h * HALF + ia * 32), :] = y_send_buf[c, h] + y_got[c, h]
        send_all(gather_b, c, h)

    def probe_5(c, h):
        take_all(gather_b, c, h)
        send_all(gather_a, c, h)

    def probe_6(c, h):
        take_all(gather_a, c, h)
        probe_out[c, h].start()

    def each(step, h):
        for c in range(2):
            step(c, h)

    to_share[0].wait_recv()
    over([(0, 0)], both_steps)
    factors(1)
    over([(0, 1)], both_steps)
    place(1, 0)
    place(0, 0)
    to_share[1].wait_recv()
    over([(1, 0)], both_steps)
    probe_1(0)
    over([(1, 1)], both_steps)
    probe_1(1)
    reduce_1(1)
    reduce_1(0)
    reduce_2(1)
    reduce_2(0)
    each(probe_2, 0)
    each(probe_2, 1)
    each(probe_3, 0)
    reduce_3(1)
    each(probe_3, 1)
    reduce_3(0)
    rs_over[1, 1].start()
    rs_over[0, 1].start()
    each(probe_4, 0)
    each(probe_4, 1)
    each(probe_5, 0)
    each(probe_5, 1)
    reduce_4(1)
    each(probe_6, 0)
    reduce_4(0)
    each(probe_6, 1)

    for group in (probe_out, outward):
        for copy in group.values():
            copy.wait()
    for group in (scatter_a, scatter_b, swap_y, gather_b, gather_a):
        for copy in group.values():
            copy.wait_send()
    for group in (sends, crosses, relays, rs_pair, rs_over, rs_edge):
        for copy in group.values():
            copy.wait_send()
    for group in (to_pair, to_other, to_share):
        for copy in group:
            copy.wait_send()


def gradients(obj_re, obj_im, probe, measured, positions, table, orders):
    tiles = lax.axis_size("tile")
    shape = jax.ShapeDtypeStruct
    anywhere = pl.BlockSpec(memory_space=pl.ANY)
    return pl.pallas_call(
        functools.partial(kernel, tiles),
        out_shape=(shape(obj_re.shape, F32), shape(obj_im.shape, F32), shape(probe.shape, F32)),
        in_specs=[anywhere, anywhere, anywhere, anywhere, pl.BlockSpec(memory_space=pltpu.SMEM), anywhere, anywhere],
        out_specs=(anywhere, anywhere, anywhere),
        scratch_shapes=[
            pltpu.VMEM((2, TILE, TILE), F32),
            pltpu.VMEM((2, TILE, TILE), F32),
            pltpu.VMEM((2, 2, 2, PX, PX), F32),
            pltpu.VMEM((2, 2, PX, PX), F32),
            pltpu.VMEM((2, PX, PX), F32),
            pltpu.VMEM(table.shape, BF16),
            pltpu.VMEM(orders.shape, BF16),
            pltpu.VMEM((2, 2, 2, PX, PX), F32),
            pltpu.VMEM((2, 2, 2, PX, PX), F32),
            pltpu.VMEM((2, PX, PX), F32),
            pltpu.VMEM((2, HALF, PX), F32),
            pltpu.VMEM((2, HALF, PX), F32),
            pltpu.VMEM((2, HALF, PX), F32),
            pltpu.VMEM((2, PX, PX), F32),
            pltpu.VMEM((2, 2, 2, PX, PX), F32),
            pltpu.VMEM((2, 2, TILE, TILE), F32),
            pltpu.VMEM((2, 2, 2, ROWS, TILE), F32),
            pltpu.VMEM((2, 2, 2, ROWS, TILE), F32),
            pltpu.VMEM((2, 2, ROWS, TILE), F32),
            pltpu.VMEM((2, 2, ROWS, TILE), F32),
            pltpu.VMEM((2, 2, ROWS, TILE), F32),
            pltpu.VMEM((2, 2, ROWS, 128), F32),
            pltpu.VMEM((2, 2, ROWS, 128), F32),
            pltpu.SemaphoreType.DMA((4,)),
            pltpu.SemaphoreType.DMA((2, 2)),
            pltpu.SemaphoreType.DMA((3, 2, 2)),
            pltpu.SemaphoreType.DMA((3, 2, 2)),
            pltpu.SemaphoreType.DMA((3, 2)),
            pltpu.SemaphoreType.DMA((3, 2)),
            pltpu.SemaphoreType.DMA((5, 2)),
            pltpu.SemaphoreType.DMA((5, 2)),
            pltpu.SemaphoreType.DMA((2, 2)),
            pltpu.SemaphoreType.DMA((2, 2)),
            pltpu.VMEM((2, 2, PX, PX), F32),
            pltpu.VMEM((2, 2, 3, 2, 32, PX), F32),
            pltpu.VMEM((2, 2, 3, 2, 8, PX), F32),
            pltpu.VMEM((2, 2, 2, 32, PX), F32),
            pltpu.VMEM((2, 2, 2, 8, PX), F32),
            pltpu.VMEM((2, 2, 2, 8, PX), F32),
            pltpu.SemaphoreType.DMA((2, 2, 5, 3)),
            pltpu.SemaphoreType.DMA((2, 2, 5, 3)),
            pltpu.VMEM((2, 2, PX, PX), F32),
            pltpu.SemaphoreType.DMA((2, 2)),
            pltpu.SemaphoreType.DMA((2, 2)),
        ],
        compiler_params=pltpu.CompilerParams(
            collective_id=0, has_side_effects=True, vmem_limit_bytes=56 * 1024 * 1024
        ),
        cost_estimate=pl.CostEstimate(flops=7 * 10**9, bytes_accessed=10**7, transcendentals=10**6),
    )(obj_re, obj_im, probe, measured, positions, table, orders)


def deliver_kernel(count, *refs):
    sources, targets, held = refs[:count], refs[count : 2 * count], refs[2 * count : 3 * count]
    in_sem, out_sem = refs[3 * count :]
    inward, outward = [], []
    for i in range(count):
        for k in range(2):
            at = (slice(None), k)
            inward.append(pltpu.make_async_copy(sources[i].at[at], held[i].at[at], in_sem.at[i, k]))
            outward.append(pltpu.make_async_copy(held[i].at[at], targets[i].at[at], out_sem.at[i, k]))
    for copy in inward:
        copy.start()
    for copy, onward in zip(inward, outward):
        copy.wait()
        onward.start()
    for copy in outward:
        copy.wait()


def delivered(arrays):
    anywhere = pl.BlockSpec(memory_space=pl.ANY)
    count = len(arrays)
    return pl.pallas_call(
        functools.partial(deliver_kernel, count),
        out_shape=tuple(jax.ShapeDtypeStruct(a.shape, a.dtype) for a in arrays),
        in_specs=[anywhere] * count,
        out_specs=(anywhere,) * count,
        scratch_shapes=[pltpu.VMEM(a.shape, a.dtype) for a in arrays]
        + [pltpu.SemaphoreType.DMA((count, 2)), pltpu.SemaphoreType.DMA((count, 2))],
        compiler_params=pltpu.CompilerParams(vmem_limit_bytes=56 * 1024 * 1024),
    )(*arrays)


def body(object_real, object_imag, probe, measured, positions):
    table, orders = constants()
    return delivered(
        gradients(object_real, object_imag, probe, measured, positions, jnp.asarray(table), jnp.asarray(orders))
    )


def solution(mesh):
    return jax.shard_map(
        body,
        mesh=mesh,
        in_specs=(
            P("tile", None, "mode", None),
            P("tile", None, "mode", None),
            P(None, "mode", None, None),
            P("tile", None, None, None),
            P("tile", None, None),
        ),
        out_specs=(
            P("tile", None, "mode", None),
            P("tile", None, "mode", None),
            P(None, "mode", None, None),
        ),
        check_vma=False,
    )
```
